32 devices in a mesh: section: 2 (over x), dp: 8 (over z, core), tensor: 2 (over y).
Axes of the slice: x: 2, y: 2, z: 4, core: 2. Of those that a mesh axis runs over, the one named last changes fastest.
Arguments:
- block_input: bfloat16 [8, 2, 512, 1536], P('dp', None, 'tensor'), may hold values from -6 to 6
- plan: int32 [8, 2], P('dp'), may hold values from 0 to 1, each once within a row
- lengths: int32 [8, 2], P('dp'), may hold values from 128 to 512, as said below
- norm_gain: float32 [2, 1536], P('section'), may hold values from 0.1 to 1.9
- gate_proj: bfloat16 [2, 1536, 3072], P('section', 'dp', 'tensor'), may hold values from -0.15625 to 0.15625
- value_proj: bfloat16 [2, 1536, 3072], P('section', 'dp', 'tensor'), may hold values from -0.15625 to 0.15625
- shared_proj: bfloat16 [2, 1536, 256], P('section', 'dp', 'tensor'), may hold values from -0.15625 to 0.15625
- step_proj: bfloat16 [2, 1536, 48], P('section', 'dp', 'tensor'), may hold values from -0.15625 to 0.15625
- conv_value: float32 [2, 5, 3072], P('section', None, 'tensor'), may hold values from -3 to 3
- conv_shared: float32 [2, 5, 256], P('section', None, 'tensor'), may hold values from -3 to 3
- head_params: float32 [2, 3, 48], P('section', None, 'tensor'), may hold values from -7 to 3, as said below
- gate_gain: float32 [2, 3072], P('section', 'tensor'), may hold values from 0.1 to 1.9
- out_proj: bfloat16 [2, 1536, 3072], P('section', 'dp', 'tensor'), may hold values from -0.109375 to 0.109375
- cotangent: bfloat16 [8, 2, 512, 1536], P('dp', None, 'tensor'), may hold values from -6 to 6
Outputs:
- relay_ends: float32 [2, 8, 2, 512, 1536], P('section', 'dp', None, 'tensor')
- grad_norm_gain: float32 [2, 1536], P('section')
- grad_gate_proj: float32 [2, 1536, 3072], P('section', 'dp', 'tensor')
- grad_value_proj: float32 [2, 1536, 3072], P('section', 'dp', 'tensor')
- grad_shared_proj: float32 [2, 1536, 256], P('section', 'dp', 'tensor')
- grad_step_proj: float32 [2, 1536, 48], P('section', 'dp', 'tensor')
- grad_conv_value: float32 [2, 5, 3072], P('section', None, 'tensor')
- grad_conv_shared: float32 [2, 5, 256], P('section', None, 'tensor')
- grad_head_params: float32 [2, 3, 48], P('section', None, 'tensor')
- grad_gate_gain: float32 [2, 3072], P('section', 'tensor')
- grad_out_proj: float32 [2, 1536, 3072], P('section', 'dp', 'tensor')
The draws below stay inside these ranges and needn't reach their ends.
Inputs may be any that keep to these rules, and one draw needn't show every extreme that they name: lengths[d, k] valid tokens stand at the start of micro-batch plan[d, k]; in every row one entry equals 512. `plan`: each row names every micro-batch once. `head_params`: row 0: step biases; row 1: logarithms of the decay rates; row 2: skip weights.
All inputs are finite; a program needn't handle non-finite values.
Results may differ from the reference program's by a relative error of at most 0.015.
Values may be sent and summed in bfloat16 or wider, within the bound.
No kernel may reach another device: no remote copies, remote signals or barrier semaphores. Data moves between devices by JAX's collectives and lax.ppermute only.
A program may use at most 320 MiB of HBM per device.

```python
import math
import jax
import jax.numpy as jnp
from jax import lax

D = 1536
DI = 3072
P_SIZE = 64
N = 128
H = 48
CONV = 4
Q = 256
LEN = 512
MB = 2
N_SECTION = 2
N_DP = 8


def draw_lengths(key, part):
    key = jax.random.fold_in(key, 7)
    first_key, second_key = jax.random.split(key)
    others = jax.random.randint(first_key, (N_DP, MB), LEN // 4, LEN + 1)
    chosen = jax.random.randint(second_key, (N_DP, 1), 0, MB)
    slots = lax.broadcasted_iota(jnp.int32, (N_DP, MB), 1)
    return jnp.where(slots == chosen, LEN, others).astype(jnp.int32)


def draw_head_params(key, part):
    key = jax.random.fold_in(key, 11)
    step_key, decay_key, skip_key = jax.random.split(key, 3)
    step_init = jnp.exp(jax.random.uniform(step_key, (2, H), jnp.float32, math.log(0.001), math.log(0.1)))
    step_bias = step_init + jnp.log(-jnp.expm1(-step_init))
    decay_log = jnp.log(jax.random.uniform(decay_key, (2, H), jnp.float32, 1.0, 16.0))
    skip_weight = jax.random.uniform(skip_key, (2, H), jnp.float32, 0.5, 1.5)
    return jnp.stack([step_bias, decay_log, skip_weight], axis=1).astype(jnp.float32)


def steps_of(stream_key, extent, cuts, low, largest):
    level, own = 1.0, jax.random.fold_in(stream_key, 6)
    for position, shards_of in cuts:
        heights = jnp.exp(jax.random.uniform(jax.random.fold_in(own, position), (shards_of,), jnp.float32, low / len(cuts), largest / len(cuts)))
        level = level * jnp.repeat(heights, extent[position] // shards_of).reshape([-1 if axis == position else 1 for axis in range(len(extent))])
    return level


def normal_values(own_key, shape, deviation, most, cuts=(), held_as=jnp.bfloat16):
    values = jax.random.normal(own_key, shape, jnp.float32) * deviation
    if len(cuts) > 0:
        values = steps_of(own_key, shape, cuts, -0.22, 0.18) * values
    return jnp.clip(values, min=-most, max=most).astype(held_as)


def setup_inputs(seed: int = 0) -> dict:
    streams_of = jax.random.split(jax.random.key(seed), 15)
    return {
        "block_input": normal_values(streams_of[0], (N_DP, MB, LEN, D), 1.0, 6.0, ((0, 8), (2, 2))),
        "plan": jax.vmap(lambda own: jax.random.permutation(own, MB))(jax.random.split(streams_of[1], N_DP)).reshape((N_DP, MB)).astype(jnp.int32),
        "lengths": draw_lengths(jax.random.fold_in(streams_of[14], 71), 0),
        "norm_gain": jnp.clip(1.0 + 0.18 * jax.random.normal(streams_of[3], (N_SECTION, D), jnp.float32), 0.1, 1.9),
        "gate_proj": normal_values(streams_of[4], (N_SECTION, D, DI), D ** -0.5, 0.15625, ((0, 2), (1, 8), (2, 2))),
        "value_proj": normal_values(streams_of[5], (N_SECTION, D, DI), D ** -0.5, 0.15625, ((0, 2), (1, 8), (2, 2))),
        "shared_proj": normal_values(streams_of[6], (N_SECTION, D, 2 * N), D ** -0.5, 0.15625, ((0, 2), (1, 8), (2, 2))),
        "step_proj": normal_values(streams_of[7], (N_SECTION, D, H), D ** -0.5, 0.15625, ((0, 2), (1, 8), (2, 2))),
        "conv_value": normal_values(streams_of[8], (N_SECTION, CONV + 1, DI), 0.5, 3.0, ((0, 2), (2, 2)), jnp.float32),
        "conv_shared": normal_values(streams_of[9], (N_SECTION, CONV + 1, 2 * N), 0.5, 3.0, ((0, 2), (2, 2)), jnp.float32),
        "head_params": draw_head_params(jax.random.fold_in(streams_of[14], 71), 0),
        "gate_gain": jnp.clip(1.0 + 0.18 * jax.random.normal(streams_of[11], (N_SECTION, DI), jnp.float32), 0.1, 1.9),
        "out_proj": normal_values(streams_of[12], (N_SECTION, D, DI), DI ** -0.5, 0.109375, ((0, 2), (1, 8), (2, 2))),
        "cotangent": normal_values(streams_of[13], (N_DP, MB, LEN, D), 1.0, 6.0, ((0, 8), (2, 2))),
    }


eps = 1e-05
highest = lax.Precision.HIGHEST

@jax.custom_vjp
def low(v):
    return lax.optimization_barrier(v.astype(jnp.bfloat16)).astype(jnp.float32)

@jax.custom_vjp
def low_back(v):
    return v

def low_keep(v):
    return (low(v), None)

def low_pass(kept, grad):
    return (grad,)

def back_keep(v):
    return (v, None)

def back_low(kept, grad):
    return (low(grad),)
low.defvjp(low_keep, low_pass)
low_back.defvjp(back_keep, back_low)

def rms_norm(residual, gain_vector):
    return residual * lax.rsqrt(lax.optimization_barrier(jnp.mean(residual * residual, axis=1, keepdims=True)) + eps) * gain_vector

def conv_silu(values, kernel):
    length = values.shape[0]
    padded = jnp.concatenate([jnp.zeros((CONV - 1, values.shape[1]), jnp.float32), values], axis=0)
    summed = kernel[CONV] + kernel[0] * padded[0:length]
    for offset in range(1, CONV):
        summed = summed + kernel[offset] * padded[offset:offset + length]
    return jax.nn.silu(summed)

def scan_state(carried, inputs):
    factor, update = inputs
    return (factor[:, None, None] * carried + update, carried)

def state_space(inputs_x, step_size, decay_rate, keys_b, reads_c):
    length, head_count, head_width = inputs_x.shape
    blocks = length // Q
    scaled = (step_size * decay_rate[None, :]).reshape(blocks, Q, head_count)
    running = jnp.cumsum(scaled, axis=1).transpose(0, 2, 1)
    weighted = (inputs_x * step_size[:, :, None]).reshape(blocks, Q, head_count, head_width)
    block_b = keys_b.reshape(blocks, Q, N)
    block_c = reads_c.reshape(blocks, Q, N)
    scores = jnp.einsum('bin,bjn->bij', block_c, block_b, precision=highest)
    rowpos = lax.broadcasted_iota(jnp.int32, (Q, Q), 0)
    colpos = lax.broadcasted_iota(jnp.int32, (Q, Q), 1)
    spread = running[:, :, :, None] - running[:, :, None, :]
    decays = jnp.exp(jnp.where(rowpos >= colpos, spread, -1e+30))
    mixing = decays * scores[:, None, :, :]
    within_block = jnp.einsum('bhij,bjhp->bihp', mixing, weighted, precision=highest)
    tail_decay = jnp.exp(running[:, :, -1:] - running).transpose(0, 2, 1)
    tailed = weighted * tail_decay[:, :, :, None]
    states = jnp.einsum('bjn,bjhp->bhpn', block_b, tailed, precision=highest)
    factors = jnp.exp(running[:, :, -1])
    start_state = jnp.zeros((head_count, head_width, N), jnp.float32)
    unused, entering = lax.scan(scan_state, start_state, (factors, states))
    across_block = jnp.einsum('bin,bhpn->bihp', block_c, entering, precision=highest)
    across_block = across_block * jnp.exp(running).transpose(0, 2, 1)[:, :, :, None]
    return (within_block + across_block).reshape(length, head_count, head_width)

def mixer_core(pre_z, pre_x, pre_dt, shared_bc, kernel_x, head_values):
    length = pre_x.shape[0]
    head_count = pre_dt.shape[1]
    mixed_x = conv_silu(pre_x, kernel_x)
    step_size = jax.nn.softplus(pre_dt + head_values[0])
    decay_rate = -jnp.exp(head_values[1])
    heads_x = mixed_x.reshape(length, head_count, P_SIZE)
    result = state_space(heads_x, step_size, decay_rate, shared_bc[:, :N], shared_bc[:, N:])
    result = result + head_values[2][None, :, None] * heads_x
    gated = result.reshape(length, head_count * P_SIZE) * jax.nn.silu(pre_z)
    return (gated, lax.optimization_barrier(jnp.sum(gated * gated, axis=1)))

def gate_finish(gated, square_sum, gain_vector):
    return gated * lax.rsqrt(square_sum[:, None] / DI + eps) * gain_vector

def layer(residual, params):
    gain_norm, gate_w, value_w, shared_w, step_w, kernel_value, kernel_shared, head_values, gain_gate, out_w = params
    normed = low(rms_norm(residual, gain_norm))
    pre_z = low_back(jnp.dot(normed, gate_w, precision=highest))
    pre_x = low_back(jnp.dot(normed, value_w, precision=highest))
    pre_bc = low_back(jnp.dot(normed, shared_w, precision=highest))
    pre_dt = low_back(jnp.dot(normed, step_w, precision=highest))
    shared_bc = conv_silu(pre_bc, kernel_shared)
    gated, square_sum = mixer_core(pre_z, pre_x, pre_dt, shared_bc, kernel_value, head_values)
    outgoing = low(gate_finish(gated, square_sum, gain_gate))
    projected = low_back(jnp.dot(outgoing, out_w.T, precision=highest))
    return residual + projected

def reference(block_input, plan, lengths, norm_gain, gate_proj, value_proj, shared_proj, step_proj, conv_value, conv_shared, head_params, gate_gain, out_proj, cotangent):
    params = tuple((member.astype(jnp.float32) for member in (norm_gain, gate_proj, value_proj, shared_proj, step_proj, conv_value, conv_shared, head_params, gate_gain, out_proj)))
    seq_count = N_DP * MB
    inputs = block_input.astype(jnp.float32).reshape(seq_count, LEN, D)
    owners = plan[:, :, None] == lax.broadcasted_iota(jnp.int32, (N_DP, MB, MB), 2)
    by_batch = lax.optimization_barrier(jnp.sum(jnp.where(owners, lengths[:, :, None], 0), axis=1)).reshape(seq_count).astype(jnp.int32)
    positions = lax.broadcasted_iota(jnp.int32, (seq_count, LEN), 1)
    keeping = (positions < by_batch[:, None]).astype(jnp.float32)
    grads_in = cotangent.astype(jnp.float32).reshape(seq_count, LEN, D) * keeping[:, :, None]

    def model(weights, residual):
        first = layer(residual, tuple((member[0] for member in weights)))
        return layer(first, tuple((member[1] for member in weights)))

    def per_sequence(totals, sequence_pair):
        residual, incoming = sequence_pair
        output, pullback = jax.vjp(model, params, residual)
        param_grads, input_grad = pullback(incoming)
        return (jax.tree.map(jnp.add, totals, param_grads), (input_grad, output))
    initial = jax.tree.map(jnp.zeros_like, params)
    totals, (input_grads, outputs) = lax.scan(per_sequence, initial, (inputs, grads_in))
    relay_ends = jnp.stack([input_grads, outputs]).reshape(2, N_DP, MB, LEN, D)
    return (relay_ends, totals[0], totals[1], totals[2], totals[3], totals[4], totals[5], totals[6], totals[7], totals[8], totals[9])
```

```python
import jax
import jax.numpy as jnp
from jax import lax
from jax.experimental import pallas as pl
from jax.experimental.pallas import tpu as pltpu
from jax.sharding import PartitionSpec as P

DI = 3072
P_SIZE = 64
N = 128
T = 128
LANES = 128
HP = 16
eps = 1e-05
bf16 = jnp.bfloat16
f32 = jnp.float32


def dot_nn(a, b):
    return lax.dot_general(a, b, (((1,), (0,)), ((), ())), preferred_element_type=f32)


def dot_nt(a, b):
    return lax.dot_general(a, b, (((1,), (1,)), ((), ())), preferred_element_type=f32)


def dot_tn(a, b):
    return lax.dot_general(a, b, (((0,), (0,)), ((), ())), preferred_element_type=f32)


def sigmoid(v):
    return 0.5 + 0.5 * jnp.tanh(0.5 * v)


def shifted(cat):
    return (
        pltpu.roll(cat, 3, 0)[8:],
        pltpu.roll(cat, 2, 0)[8:],
        pltpu.roll(cat, 1, 0)[8:],
        cat[8:],
    )


def conv(parts, taps):
    total = taps[4:5]
    for j in range(4):
        total = total + taps[j : j + 1] * parts[j]
    return total


def conv_back(ds, after, taps):
    cat = jnp.concatenate([ds, after], axis=0)
    rows = cat.shape[0]
    total = taps[3:4] * ds
    for j in range(3):
        total = total + taps[j : j + 1] * pltpu.roll(cat, rows - (3 - j), 0)[: ds.shape[0]]
    return total


def lane_ids(shape):
    return lax.broadcasted_iota(jnp.int32, shape, len(shape) - 1)


def running_sum(v, lane):
    step = 1
    while step < LANES:
        v = v + jnp.where(lane >= step, pltpu.roll(v, step, 1), 0.0)
        step *= 2
    return v


def running_sum_back(v, lane):
    step = 1
    while step < LANES:
        v = v + jnp.where(lane < LANES - step, pltpu.roll(v, LANES - step, 1), 0.0)
        step *= 2
    return v


def step_rows(pre_dt, heads):
    logits = jnp.transpose(pre_dt)[:HP] + heads[:, 0:1]
    small = jnp.exp(-jnp.abs(logits))
    log_part = jnp.where(small < 1e-3, small * (1.0 - small * (0.5 - small / 3.0)), jnp.log(1.0 + small))
    steps = jnp.maximum(logits, 0.0) + log_part
    run = running_sum(steps * heads[:, 1:2], lane_ids((HP, T)))
    return logits, steps, run


def columns(rows):
    have = rows.shape[0]
    return jnp.transpose(jnp.concatenate([rows, jnp.zeros((LANES - have, T), f32)], axis=0))


def fwd_kernel(order, pz, px, halo, taps_x, taps_bc, heads, skip, gain, og_ref, y_ref, s_ref, sq_ref, state):
    k = pl.program_id(1)
    width = pz.shape[1]
    pairs = width // LANES
    bc_at, dt_at = width, width + 2 * N

    @pl.when(k == 0)
    def _():
        state[...] = jnp.zeros_like(state)

    keep = jnp.where(k > 0, 1.0, 0.0)
    lane = lane_ids((T, LANES))
    low = lane < P_SIZE
    row = lax.broadcasted_iota(jnp.int32, (T, T), 0)
    seen = row >= lane
    logits, steps, run = step_rows(px[:, dt_at : dt_at + LANES], heads[...])
    tail = jnp.exp(run[:, T - 1 : T] - run) * steps
    cols = columns(jnp.concatenate([run, tail], axis=0))
    bc_cat = jnp.concatenate([halo[:, bc_at : bc_at + 2 * N] * keep, px[:, bc_at : bc_at + 2 * N]], axis=0)
    s_bc = conv(shifted(bc_cat), taps_bc[...])
    bc = s_bc * sigmoid(s_bc)
    keys = bc[:, :N]
    keys_t = jnp.transpose(keys).astype(bf16)
    reads = bc[:, N:].astype(bf16)
    scores = jnp.where(seen, dot_nt(reads, keys.astype(bf16)), 0.0)
    squares = jnp.zeros((T, LANES), f32)
    for p in range(pairs):
        at = slice(p * LANES, (p + 1) * LANES)
        x_cat = jnp.concatenate([halo[:, at] * keep, px[:, at]], axis=0)
        s_x = conv(shifted(x_cat), taps_x[:, at])
        xs = s_x * sigmoid(s_x)
        xr = xs.astype(bf16)
        mixes = []
        wide = []
        for h in (2 * p, 2 * p + 1):
            ci = jnp.broadcast_to(cols[:, h : h + 1], (T, T))
            decay = jnp.exp(jnp.minimum(ci - run[h : h + 1], 0.0))
            mixes.append((decay * steps[h : h + 1] * scores).astype(bf16))
            wide.append(ci)
        c_pair = jnp.where(low, wide[0], wide[1])
        w_pair = jnp.where(low, cols[:, HP + 2 * p : HP + 2 * p + 1], cols[:, HP + 2 * p + 1 : HP + 2 * p + 2])
        e_pair = jnp.exp(c_pair)
        zero = jnp.zeros_like(xr)
        y = dot_nn(
            jnp.concatenate(mixes, axis=1),
            jnp.concatenate([jnp.where(low, xr, zero), jnp.where(low, zero, xr)], axis=0),
        )
        entering = state[:, at]
        entering_r = entering.astype(bf16)
        s_ref[0, :, at] = entering_r
        y = y + e_pair * dot_nn(reads, entering_r)
        state[:, at] = e_pair[T - 1 : T] * entering + dot_nn(keys_t, (xs * w_pair).astype(bf16))
        y_ref[:, at] = y
        z = pz[:, at]
        g = (y + skip[:, at] * xs) * (z * sigmoid(z))
        squares = squares + g * g
        og_ref[:, at] = (g * gain[:, at]).astype(bf16)
    sq_ref[0] = jnp.broadcast_to(jnp.sum(jnp.transpose(squares), axis=0, keepdims=True), (8, T))


def bwd_kernel(
    order, pz, px, halo, y_ref, s_ref, d_ref, stats, taps_x, taps_bc, heads, skip, gain, sums,
    dz_ref, dx_ref, acc_x, acc_bc, acc_dt, back, after_x, after_bc, d_scores,
):
    s_id, k = pl.program_id(0), pl.program_id(1)
    width = pz.shape[1]
    pairs = width // LANES
    bc_at, dt_at = width, width + 2 * N

    @pl.when(k == 0)
    def _():
        back[...] = jnp.zeros_like(back)
        after_x[...] = jnp.zeros_like(after_x)
        after_bc[...] = jnp.zeros_like(after_bc)

    @pl.when((k == 0) & (s_id == 0))
    def _():
        acc_x[...] = jnp.zeros_like(acc_x)
        acc_bc[...] = jnp.zeros_like(acc_bc)
        acc_dt[...] = jnp.zeros_like(acc_dt)

    keep = jnp.where(k < 3, 1.0, 0.0)
    lane = lane_ids((T, LANES))
    low = lane < P_SIZE
    row = lax.broadcasted_iota(jnp.int32, (T, T), 0)
    seen_t = lane >= row
    last = row == T - 1
    head_cols = heads[...]
    logits, steps, run = step_rows(px[:, dt_at : dt_at + LANES], head_cols)
    tail = jnp.exp(run[:, T - 1 : T] - run) * steps
    cols = columns(jnp.concatenate([run, steps, tail], axis=0))
    bc_cat = jnp.concatenate([halo[:, bc_at : bc_at + 2 * N] * keep, px[:, bc_at : bc_at + 2 * N]], axis=0)
    bc_parts = shifted(bc_cat)
    s_bc = conv(bc_parts, taps_bc[...])
    sig_bc = sigmoid(s_bc)
    bc = s_bc * sig_bc
    keys, reads = bc[:, :N].astype(bf16), bc[:, N:].astype(bf16)
    reads_t = jnp.transpose(bc[:, N:]).astype(bf16)
    scores_t = jnp.where(seen_t, dot_nt(keys, reads), 0.0)
    d_scores[...] = jnp.zeros_like(d_scores)
    d_reads = jnp.zeros((T, N), f32)
    d_keys = jnp.zeros((T, N), f32)
    head_sums = jnp.zeros((T, LANES), f32)
    row_scale = stats[:, 0:1]
    row_stat = stats[:, 1:2]
    for p in range(pairs):
        at = slice(p * LANES, (p + 1) * LANES)
        x_cat = jnp.concatenate([halo[:, at] * keep, px[:, at]], axis=0)
        x_parts = shifted(x_cat)
        s_x = conv(x_parts, taps_x[:, at])
        sig_x = sigmoid(s_x)
        xs = s_x * sig_x
        xr = xs.astype(bf16)
        z = pz[:, at]
        sig_z = sigmoid(z)
        silu_z = z * sig_z
        y = y_ref[:, at]
        y_all = y + skip[:, at] * xs
        g = y_all * silu_z
        dr = d_ref[:, at] * row_scale
        dg = gain[:, at] * dr - g * row_stat
        acc_x[5:6, at] += jnp.sum(dr * g, axis=0, keepdims=True)
        dz_ref[:, at] = (dg * y_all * (sig_z + silu_z * (1.0 - sig_z))).astype(bf16)
        dy = dg * silu_z
        dyr = dy.astype(bf16)
        acc_x[6:7, at] += jnp.sum(dy * xs, axis=0, keepdims=True)
        zero = jnp.zeros_like(xr)
        mixes_t = []
        wide = []
        total = d_scores[...]
        for i, h in enumerate((2 * p, 2 * p + 1)):
            cj = jnp.broadcast_to(cols[:, h : h + 1], (T, T))
            decay = jnp.exp(jnp.minimum(run[h : h + 1] - cj, 0.0)) * cols[:, HP + h : HP + h + 1]
            mixes_t.append((decay * scores_t).astype(bf16))
            x_one = jnp.where(low, xr, zero) if i == 0 else jnp.where(low, zero, xr)
            total = total + decay * dot_nt(x_one, dyr)
            wide.append(cj)
        d_scores[...] = total
        c_pair = jnp.where(low, wide[0], wide[1])
        at_w = 2 * HP + 2 * p
        w_pair = jnp.where(low, cols[:, at_w : at_w + 1], cols[:, at_w + 1 : at_w + 2])
        e_pair = jnp.exp(c_pair)
        dx_in = dot_nn(
            jnp.concatenate(mixes_t, axis=1),
            jnp.concatenate([jnp.where(low, dyr, zero), jnp.where(low, zero, dyr)], axis=0),
        )
        returning = back[:, at]
        returning_r = returning.astype(bf16)
        entering_r = s_ref[0, :, at]
        dx_out = w_pair * dot_nn(keys, returning_r)
        dye = (dy * e_pair).astype(bf16)
        d_reads = d_reads + dot_nt(dye, entering_r)
        d_keys = d_keys + dot_nt((xs * w_pair).astype(bf16), returning_r)
        e_last = e_pair[T - 1 : T]
        back[:, at] = e_last * returning + dot_nn(reads_t, dye)
        across = e_last * jnp.sum(returning * entering_r.astype(f32), axis=0, keepdims=True)
        xf, dyf = xr.astype(f32), dyr.astype(f32)
        one = dyf * y - xf * dx_in + jnp.where(last, across, 0.0)
        for i, part in enumerate((one, xf * dx_in, xf * dx_out)):
            high = part.astype(bf16)
            rest = (part - high.astype(f32)).astype(bf16)
            place = sums[(3 * p + i) * LANES : (3 * p + i + 1) * LANES]
            head_sums = head_sums + dot_nn(
                jnp.concatenate([high, rest], axis=1), jnp.concatenate([place, place], axis=0)
            )
        dxs = dx_in + dx_out + skip[:, at] * dy
        ds = dxs * (sig_x + xs * (1.0 - sig_x))
        for j in range(4):
            acc_x[j : j + 1, at] += jnp.sum(ds * x_parts[j], axis=0, keepdims=True)
        acc_x[4:5, at] += jnp.sum(ds, axis=0, keepdims=True)
        dx_ref[:, at] = conv_back(ds, after_x[:, at], taps_x[:, at]).astype(bf16)
        after_x[:, at] = ds[:8]
    rows = jnp.transpose(head_sums)
    one, two, three = rows[:HP], rows[HP : 2 * HP], rows[2 * HP : 3 * HP]
    lane_h = lane_ids((HP, T))
    d_decay = running_sum_back(one, lane_h) + running_sum(three, lane_h) - three
    sig_dt = sigmoid(logits)
    exact = jnp.exp(jnp.minimum(logits, 0.0)) / (1.0 + jnp.exp(-jnp.abs(logits)))
    ratio = jnp.where(logits < -15.0, 1.0, exact / jnp.maximum(steps, 1e-30))
    d_pre = (two + three) * ratio + head_cols[:, 1:2] * d_decay * sig_dt
    acc_dt[0:HP] += steps * d_decay
    acc_dt[HP : 2 * HP] += d_pre
    dx_ref[:, dt_at : dt_at + LANES] = columns(d_pre).astype(bf16)
    ds_t = jnp.where(seen_t, d_scores[...], 0.0)
    d_keys = d_keys + dot_nn(ds_t.astype(bf16), reads)
    d_reads = d_reads + dot_nn(jnp.transpose(ds_t).astype(bf16), keys)
    ds_bc = jnp.concatenate([d_keys, d_reads], axis=1) * (sig_bc + bc * (1.0 - sig_bc))
    for j in range(4):
        acc_bc[j : j + 1] += jnp.sum(ds_bc * bc_parts[j], axis=0, keepdims=True)
    acc_bc[4:5] += jnp.sum(ds_bc, axis=0, keepdims=True)
    dx_ref[:, bc_at : bc_at + 2 * N] = conv_back(ds_bc, after_bc[...], taps_bc[...]).astype(bf16)
    after_bc[...] = ds_bc[:8]


def whole_spec(array):
    return pl.BlockSpec(array.shape, lambda s, k, order: (0,) * array.ndim)


def scan_forward(order, pz, px, layer):
    rows, width = pz.shape
    steps = rows // T
    here = lambda s, k, order: (order[s * 4 + k], 0)
    before = lambda s, k, order: (order[s * 4 + jnp.maximum(k - 1, 0)] * (T // 8) + (T // 8 - 1), 0)
    small = (layer["taps_x"], layer["taps_bc"], layer["heads"], layer["skip"], layer["gain"])
    return pl.pallas_call(
        fwd_kernel,
        grid_spec=pltpu.PrefetchScalarGridSpec(
            num_scalar_prefetch=1,
            grid=(steps // 4, 4),
            in_specs=[
                pl.BlockSpec((T, width), here),
                pl.BlockSpec((T, px.shape[1]), here),
                pl.BlockSpec((8, px.shape[1]), before),
            ]
            + [whole_spec(m) for m in small],
            out_specs=[
                pl.BlockSpec((T, width), here),
                pl.BlockSpec((T, width), here),
                pl.BlockSpec((1, N, width), lambda s, k, order: (s * 4 + k, 0, 0)),
                pl.BlockSpec((1, 8, T), lambda s, k, order: (order[s * 4 + k], 0, 0)),
            ],
            scratch_shapes=[pltpu.VMEM((N, width), f32)],
        ),
        out_shape=[
            jax.ShapeDtypeStruct((rows, width), bf16),
            jax.ShapeDtypeStruct((rows, width), f32),
            jax.ShapeDtypeStruct((steps, N, width), bf16),
            jax.ShapeDtypeStruct((steps, 8, T), f32),
        ],
        compiler_params=pltpu.CompilerParams(vmem_limit_bytes=40 * 2**20),
        cost_estimate=pl.CostEstimate(flops=4 * 10**9, bytes_accessed=14 * 2**20, transcendentals=5 * 10**6),
        name="scan_forward",
    )(order, pz, px, px, *small)


def scan_backward(order, pz, px, y, states, d_out, stats, layer, sums):
    rows, width = pz.shape
    steps = rows // T
    here = lambda s, k, order: (order[s * 4 + 3 - k], 0)
    before = lambda s, k, order: (order[s * 4 + jnp.maximum(2 - k, 0)] * (T // 8) + (T // 8 - 1), 0)
    small = (layer["taps_x"], layer["taps_bc"], layer["heads"], layer["skip"], layer["gain"], sums)
    fixed = lambda s, k, order: (0, 0)
    return pl.pallas_call(
        bwd_kernel,
        grid_spec=pltpu.PrefetchScalarGridSpec(
            num_scalar_prefetch=1,
            grid=(steps // 4, 4),
            in_specs=[
                pl.BlockSpec((T, width), here),
                pl.BlockSpec((T, px.shape[1]), here),
                pl.BlockSpec((8, px.shape[1]), before),
                pl.BlockSpec((T, width), here),
                pl.BlockSpec((1, N, width), lambda s, k, order: (s * 4 + 3 - k, 0, 0)),
                pl.BlockSpec((T, width), here),
                pl.BlockSpec((T, stats.shape[1]), here),
            ]
            + [whole_spec(m) for m in small],
            out_specs=[
                pl.BlockSpec((T, width), here),
                pl.BlockSpec((T, px.shape[1]), here),
                pl.BlockSpec((8, width), fixed),
                pl.BlockSpec((8, 2 * N), fixed),
                pl.BlockSpec((2 * HP, T), fixed),
            ],
            scratch_shapes=[
                pltpu.VMEM((N, width), f32),
                pltpu.VMEM((8, width), f32),
                pltpu.VMEM((8, 2 * N), f32),
                pltpu.VMEM((T, T), f32),
            ],
        ),
        out_shape=[
            jax.ShapeDtypeStruct((rows, width), bf16),
            jax.ShapeDtypeStruct((rows, px.shape[1]), bf16),
            jax.ShapeDtypeStruct((8, width), f32),
            jax.ShapeDtypeStruct((8, 2 * N), f32),
            jax.ShapeDtypeStruct((2 * HP, T), f32),
        ],
        compiler_params=pltpu.CompilerParams(vmem_limit_bytes=40 * 2**20),
        cost_estimate=pl.CostEstimate(flops=8 * 10**9, bytes_accessed=24 * 2**20, transcendentals=10**7),
        name="scan_backward",
    )(order, pz, px, px, y, states, d_out, stats, *small)


def swap(value, axis):
    return lax.ppermute(value, axis, [(0, 1), (1, 0)])


AXES = (("section", "tensor"), ("tensor", "section"))


def spread(own, first, second):
    two = jnp.concatenate([own, swap(own, first)], axis=0)
    return jnp.concatenate([two, swap(two, second)], axis=0)


def spread_all(owns):
    return jnp.concatenate([spread(own, *axes) for own, axes in zip(owns, AXES)], axis=0)


def collect(parts, first, second):
    half = parts.shape[0] // 2
    two = parts[:half].astype(f32) + swap(parts[half:], second).astype(f32)
    quarter = half // 2
    return two[:quarter] + swap(two[quarter:].astype(parts.dtype), first).astype(f32)


def local(
    block_input,
    plan,
    lengths,
    norm_gain,
    gate_proj,
    value_proj,
    shared_proj,
    step_proj,
    conv_value,
    conv_shared,
    head_params,
    gate_gain,
    out_proj,
    cotangent,
):
    x = lax.axis_index("section")
    yy = lax.axis_index("tensor")
    streams = block_input.shape[1]
    model_width = block_input.shape[3]
    width = gate_proj.shape[2] // 2
    head_count = step_proj.shape[2] // 2
    rows_here = gate_proj.shape[1]

    def both(value):
        other = swap(value, "section")
        return jnp.where(x == 0, value, other), jnp.where(x == 0, other, value)

    def quarters(value):
        size = value.shape[-1] // 2
        axis = value.ndim - 1
        kept = lax.dynamic_slice_in_dim(value, x * size, size, axis)
        other = swap(lax.dynamic_slice_in_dim(value, (1 - x) * size, size, axis), "section")
        return jnp.where(x == 0, kept, other), jnp.where(x == 0, other, kept)

    shared_other = swap(shared_proj[0], "tensor")
    shared_full = jnp.where(
        yy == 0,
        jnp.concatenate([shared_proj[0], shared_other], axis=1),
        jnp.concatenate([shared_other, shared_proj[0]], axis=1),
    )
    step_padded = jnp.pad(
        step_proj[0].reshape(rows_here, 2, head_count), ((0, 0), (0, 0), (0, LANES - head_count))
    ).reshape(rows_here, 2 * LANES)
    value_two = quarters(value_proj[0])
    shared_two = both(shared_full)
    step_two = quarters(step_padded)
    gate_two = quarters(gate_proj[0])
    out_two = quarters(out_proj[0])
    weights = []
    for l in range(2):
        packed = jnp.concatenate([value_two[l], shared_two[l], step_two[l]], axis=1)
        weights.append(
            (
                lax.all_gather(packed, "dp", axis=0, tiled=True),
                lax.all_gather(gate_two[l], "dp", axis=0, tiled=True),
                lax.all_gather(out_two[l], "dp", axis=0, tiled=True),
            )
        )

    taps_x_two = quarters(jnp.pad(conv_value[0], ((0, 3), (0, 0))))
    shared_taps_other = swap(conv_shared[0], "tensor")
    taps_bc_full = jnp.where(
        yy == 0,
        jnp.concatenate([conv_shared[0], shared_taps_other], axis=1),
        jnp.concatenate([shared_taps_other, conv_shared[0]], axis=1),
    )
    taps_bc_two = both(jnp.pad(taps_bc_full, ((0, 3), (0, 0))))
    heads_two = quarters(head_params[0])
    gain_two = quarters(gate_gain)
    norm_two = both(norm_gain)
    layers = []
    for l in range(2):
        head_rows = heads_two[l]
        columns_of = jnp.stack([head_rows[0], -jnp.exp(head_rows[1])], axis=1)
        layers.append(
            dict(
                taps_x=taps_x_two[l],
                taps_bc=taps_bc_two[l],
                heads=jnp.pad(columns_of, ((0, HP - head_count), (0, LANES - 2))),
                skip=jnp.repeat(head_rows[2], P_SIZE)[None],
                gain=gain_two[l],
                norm=norm_two[l],
                decay=columns_of[:, 1],
            )
        )
    feature = lax.broadcasted_iota(jnp.int32, (3 * width, LANES), 0)
    target = lax.broadcasted_iota(jnp.int32, (3 * width, LANES), 1)
    pair, part, within = feature // (3 * LANES), (feature // LANES) % 3, feature % LANES
    sums = (target == part * HP + 2 * pair + within // P_SIZE).astype(bf16)

    chunk = jnp.arange(4, dtype=jnp.int32)
    x_bit, y_bit = (chunk & 1) ^ x, (chunk >> 1) ^ yy
    order = jnp.concatenate([2 * y_bit + x_bit, 4 + 2 * x_bit + y_bit]).astype(jnp.int32)

    def own_rows(value):
        half = value.shape[1] // 2
        return lax.dynamic_slice_in_dim(value, x * half, half, 1)

    first_rows = (2 * yy + x) * T
    positions = first_rows + lax.broadcasted_iota(jnp.int32, (T, 1), 0)
    valid = jnp.sum(jnp.where(plan[0][:, None] == jnp.arange(streams)[None, :], lengths[0][:, None], 0), axis=0)
    keep = (positions[None] < valid[:, None, None]).astype(f32)
    u = own_rows(block_input[0]).astype(f32)
    top = own_rows(cotangent[0]).astype(f32) * keep

    saved = []
    for l in range(2):
        w_in, w_gate, w_out = weights[l]
        layer = layers[l]
        rho = lax.rsqrt(jnp.mean(u * u, axis=2, keepdims=True) + eps)
        a_own = (u * rho * layer["norm"][None]).astype(bf16)
        a = spread_all([a_own[s] for s in range(streams)])
        px = dot_nn(a, w_in)
        pz = dot_nn(a, w_gate)
        og, y, states, squares = scan_forward(order, pz, px, layer)
        o_part = dot_nt(og, w_out).astype(bf16)
        sq = squares[:, 0, :].reshape(streams, 4 * T)
        size = 4 * T
        o = jnp.stack([collect(o_part[s * size : (s + 1) * size], *AXES[s]) for s in range(streams)])
        total = jnp.stack([collect(sq[s], *AXES[s]) for s in range(streams)])[:, :, None]
        r = lax.rsqrt(total / DI + eps)
        o = o * r
        saved.append((u, rho, a, pz, px, og, y, states, r, o))
        u = u + o
    final = u

    dv = top
    shards = [None, None]
    small_sums = [None, None]
    for l in (1, 0):
        w_in, w_gate, w_out = weights[l]
        layer = layers[l]
        u, rho, a, pz, px, og, y, states, r, o = saved[l]
        do_own = (dv * r).astype(bf16)
        kappa = r * r * jnp.sum(dv.astype(bf16).astype(f32) * o, axis=2, keepdims=True) / DI
        do = spread_all([do_own[s] for s in range(streams)])
        stat = spread_all([kappa[s, :, 0] for s in range(streams)])
        stats = jnp.stack([jnp.ones_like(stat), stat], axis=1)
        d_out = dot_nn(do, w_out)
        dz, dx, acc_x, acc_bc, acc_dt = scan_backward(order, pz, px, y, states, d_out, stats, layer, sums)
        da_part = (dot_nt(dz, w_gate) + dot_nt(dx, w_in)).astype(bf16)
        size = 4 * T
        da = jnp.stack([collect(da_part[s * size : (s + 1) * size], *AXES[s]) for s in range(streams)])
        grad_out = dot_tn(do, og).astype(bf16)
        grad_gate = dot_tn(a, dz).astype(bf16)
        grad_in = dot_tn(a, dx).astype(bf16)
        shards[l] = tuple(
            lax.psum_scatter(g, "dp", scatter_dimension=0, tiled=True) for g in (grad_out, grad_gate, grad_in)
        )
        scaled = da * layer["norm"][None]
        du = dv + rho * scaled - u * rho**3 * jnp.mean(scaled * u, axis=2, keepdims=True)
        grad_norm = jnp.sum(da * u * rho, axis=(0, 1))
        small_sums[l] = jnp.concatenate(
            [
                acc_x.reshape(-1),
                acc_bc.reshape(-1),
                jnp.sum(acc_dt, axis=1),
                grad_norm,
            ]
        )
        dv = du

    packed = jnp.stack(small_sums)
    packed = jnp.sum(lax.all_gather(packed, "dp", axis=0), axis=0)
    everyone = lax.all_gather(packed, ("section", "tensor"), axis=0)
    mine = lax.dynamic_index_in_dim(everyone, x, 1, keepdims=False)
    end_x, end_bc = 8 * width, 8 * width + 8 * 2 * N
    end_dt = end_bc + 2 * HP
    over_all = jnp.sum(mine, axis=0)
    halves = lax.dynamic_index_in_dim(mine.reshape(2, 2, -1), yy, 1, keepdims=False)
    by_x = halves[:, :end_x].reshape(2, 8, width).transpose(1, 0, 2).reshape(8, 2 * width)
    by_dt = halves[:, end_bc:end_dt].reshape(2, 2, HP)[:, :, :head_count].transpose(1, 0, 2).reshape(2, 2 * head_count)
    grad_conv_value = by_x[:5]
    grad_gate_gain = by_x[5]
    grad_skip = jnp.sum(by_x[6].reshape(2 * head_count, P_SIZE), axis=1)
    grad_heads = jnp.stack([by_dt[1], by_dt[0] * -jnp.exp(head_params[0, 1]), grad_skip])
    bc_all = over_all[end_x:end_bc].reshape(8, 2 * N)[:5]
    grad_conv_shared = lax.dynamic_slice_in_dim(bc_all, yy * N, N, 1)
    grad_norm = over_all[end_dt:]

    def home(per_layer):
        kept = jnp.where(x == 0, per_layer[0], per_layer[1])
        other = swap(jnp.where(x == 0, per_layer[1], per_layer[0]), "section")
        return jnp.concatenate(
            [jnp.where(x == 0, kept, other), jnp.where(x == 0, other, kept)], axis=1
        ).astype(f32)

    grad_out = home([shards[l][0] for l in range(2)])
    grad_gate = home([shards[l][1] for l in range(2)])
    grad_value = home([shards[l][2][:, :width] for l in range(2)])
    at_dt = width + 2 * N
    grad_step = home([shards[l][2][:, at_dt : at_dt + head_count] for l in range(2)])
    shared_sums = jnp.stack([shards[l][2][:, width:at_dt].astype(f32) for l in range(2)])
    shared_sums = lax.psum(shared_sums, ("section", "tensor"))
    grad_shared = lax.dynamic_slice_in_dim(
        lax.dynamic_index_in_dim(shared_sums, x, 0, keepdims=False), yy * N, N, 1
    )

    mine = jnp.where(x == 0, dv, final)
    other = swap(jnp.where(x == 0, final, dv).astype(bf16), "section").astype(f32)
    relay = jnp.concatenate([jnp.where(x == 0, mine, other), jnp.where(x == 0, other, mine)], axis=1)
    return (
        relay[None, None],
        grad_norm[None],
        grad_gate[None],
        grad_value[None],
        grad_shared[None],
        grad_step[None],
        grad_conv_value[None],
        grad_conv_shared[None],
        grad_heads[None],
        grad_gate_gain[None],
        grad_out[None],
    )


def solution(mesh):
    placed = (
        P("dp", None, "tensor", None),
        P("dp", None),
        P("dp", None),
        P("section", None),
        P("section", "dp", "tensor"),
        P("section", "dp", "tensor"),
        P("section", "dp", "tensor"),
        P("section", "dp", "tensor"),
        P("section", None, "tensor"),
        P("section", None, "tensor"),
        P("section", None, "tensor"),
        P("section", "tensor"),
        P("section", "dp", "tensor"),
        P("dp", None, "tensor", None),
    )
    return jax.shard_map(
        local,
        mesh=mesh,
        in_specs=placed,
        out_specs=(
            P("section", "dp", None, "tensor", None),
            P("section", None),
            P("section", "dp", "tensor"),
            P("section", "dp", "tensor"),
            P("section", "dp", "tensor"),
            P("section", "dp", "tensor"),
            P("section", None, "tensor"),
            P("section", None, "tensor"),
            P("section", None, "tensor"),
            P("section", "tensor"),
            P("section", "dp", "tensor"),
        ),
        check_vma=False,
    )
```

```python
import functools

import jax
import jax.numpy as jnp
import numpy as np
from jax import lax
from jax.experimental import pallas as pl
from jax.experimental.pallas import tpu as pltpu
from jax.sharding import PartitionSpec as P

DI = 3072
P_SIZE = 64
N = 128
T = 128
LANES = 128
HP = 16
eps = 1e-05
bf16 = jnp.bfloat16
f32 = jnp.float32


def dot_nn(a, b):
    return lax.dot_general(a, b, (((1,), (0,)), ((), ())), preferred_element_type=f32)


def dot_nt(a, b):
    return lax.dot_general(a, b, (((1,), (1,)), ((), ())), preferred_element_type=f32)


def dot_tn(a, b):
    return lax.dot_general(a, b, (((0,), (0,)), ((), ())), preferred_element_type=f32)


def sigmoid(v):
    return 0.5 + 0.5 * jnp.tanh(0.5 * v)


def shifted(cat):
    return (
        pltpu.roll(cat, 3, 0)[8:],
        pltpu.roll(cat, 2, 0)[8:],
        pltpu.roll(cat, 1, 0)[8:],
        cat[8:],
    )


def conv(parts, taps):
    total = taps[4:5]
    for j in range(4):
        total = total + taps[j : j + 1] * parts[j]
    return total


def conv_back(ds, after, taps):
    cat = jnp.concatenate([ds, after], axis=0)
    rows = cat.shape[0]
    total = taps[3:4] * ds
    for j in range(3):
        total = total + taps[j : j + 1] * pltpu.roll(cat, rows - (3 - j), 0)[: ds.shape[0]]
    return total


def lane_ids(shape):
    return lax.broadcasted_iota(jnp.int32, shape, len(shape) - 1)


def running_sum(v, lane):
    step = 1
    while step < LANES:
        v = v + jnp.where(lane >= step, pltpu.roll(v, step, 1), 0.0)
        step *= 2
    return v


def running_sum_back(v, lane):
    step = 1
    while step < LANES:
        v = v + jnp.where(lane < LANES - step, pltpu.roll(v, LANES - step, 1), 0.0)
        step *= 2
    return v


def parts_of(v):
    high = v.astype(bf16)
    rest = v - high.astype(f32)
    middle = rest.astype(bf16)
    return high, middle, (rest - middle.astype(f32)).astype(bf16)


def prepare_steps(pre_dt, heads, rows_ref, cols_ref):
    chunks = pre_dt.shape[0] // T
    logits = jnp.concatenate(
        [jnp.transpose(pre_dt[c * T : (c + 1) * T])[:HP] + heads[:, 0:1] for c in range(chunks)], axis=0
    )
    small = jnp.exp(-jnp.abs(logits))
    log_part = jnp.where(small < 1e-3, small * (1.0 - small * (0.5 - small / 3.0)), jnp.log(1.0 + small))
    steps = jnp.maximum(logits, 0.0) + log_part
    decays = jnp.concatenate([heads[:, 1:2]] * chunks, axis=0)
    run = running_sum(steps * decays, lane_ids(steps.shape))
    for c in range(chunks):
        at = slice(c * HP, (c + 1) * HP)
        rows_ref[c, 0:HP] = logits[at]
        rows_ref[c, HP : 2 * HP] = steps[at]
        rows_ref[c, 2 * HP : 3 * HP] = run[at]
        split = [part.astype(f32) for part in parts_of(run[at]) + parts_of(steps[at])]
        split.append(jnp.zeros((LANES - 6 * HP, T), f32))
        cols_ref[c] = jnp.transpose(jnp.concatenate(split, axis=0)).astype(bf16)


def eights(v):
    return jnp.sum(v.reshape(v.shape[0] // 8, 8, v.shape[1]), axis=0)


def fwd_kernel(
    order, px, halo, pre_dt, taps_x, taps_bc, heads, skip, gain, spread_run, spread_steps,
    og_ref, y_ref, s_ref, sq_ref, rows_ref, cols_ref, state,
):
    s_id, k = pl.program_id(0), pl.program_id(1)
    width = y_ref.shape[1]
    pairs = width // LANES
    bc_at, z_at = width, width + 2 * N + LANES

    @pl.when((s_id == 0) & (k == 0))
    def _():
        prepare_steps(pre_dt[...], heads[...], rows_ref, cols_ref)

    @pl.when(k == 0)
    def _():
        state[...] = jnp.zeros_like(state)

    block = order[s_id * 4 + k]
    keep = jnp.where(k > 0, 1.0, 0.0)
    lane = lane_ids((T, LANES))
    low = lane < P_SIZE
    row = lax.broadcasted_iota(jnp.int32, (T, T), 0)
    run = rows_ref[block, 2 * HP : 3 * HP]
    cols = cols_ref[block]
    runs_wide = dot_nn(cols, spread_run[...])
    steps_wide = dot_nn(cols, spread_steps[...])
    bc_cat = jnp.concatenate([halo[:, bc_at : bc_at + 2 * N] * keep, px[:, bc_at : bc_at + 2 * N]], axis=0)
    s_bc = conv(shifted(bc_cat), taps_bc[...])
    bc = s_bc * sigmoid(s_bc)
    keys = bc[:, :N]
    keys_t = jnp.transpose(keys).astype(bf16)
    reads = bc[:, N:].astype(bf16)
    scores = jnp.where(row >= lane, dot_nt(reads, keys.astype(bf16)), 0.0)
    squares = jnp.zeros((T, LANES), f32)
    for p in range(pairs):
        at = slice(p * LANES, (p + 1) * LANES)
        x_cat = jnp.concatenate([halo[:, at] * keep, px[:, at]], axis=0)
        s_x = conv(shifted(x_cat), taps_x[:, at])
        xs = s_x * sigmoid(s_x)
        xd = xs * steps_wide[:, at]
        xr = xd.astype(bf16)
        mixes = []
        wide = []
        for h in (2 * p, 2 * p + 1):
            ci = runs_wide[:, h * LANES : (h + 1) * LANES]
            mixes.append((jnp.exp(jnp.minimum(ci - run[h : h + 1], 0.0)) * scores).astype(bf16))
            wide.append(ci)
        c_pair = jnp.where(low, wide[0], wide[1])
        e_pair = jnp.exp(c_pair)
        zero = jnp.zeros_like(xr)
        y = dot_nn(
            jnp.concatenate(mixes, axis=1),
            jnp.concatenate([jnp.where(low, xr, zero), jnp.where(low, zero, xr)], axis=0),
        )
        entering = state[:, at]
        entering_r = entering.astype(bf16)
        s_ref[0, :, at] = entering_r
        y = y + e_pair * dot_nn(reads, entering_r)
        left = (xd * jnp.exp(c_pair[T - 1 : T] - c_pair)).astype(bf16)
        state[:, at] = e_pair[T - 1 : T] * entering + dot_nn(keys_t, left)
        y_ref[:, at] = y
        z = px[:, z_at + p * LANES : z_at + (p + 1) * LANES]
        g = (y + skip[:, at] * xs) * (z * sigmoid(z))
        squares = squares + g * g
        og_ref[:, at] = (g * gain[:, at]).astype(bf16)
    sq_ref[0] = jnp.broadcast_to(jnp.sum(jnp.transpose(squares), axis=0, keepdims=True), (8, T))


def bwd_kernel(
    order, px, halo, y_ref, s_ref, d_ref, stats, rows_ref, cols_ref,
    taps_x, taps_bc, heads, skip, gain, spread_run, spread_steps, sums,
    pre_ref, acc_x, acc_bc, acc_dt,
    back, after_x, after_bc, d_scores, head_sums_ref, part_x, part_bc,
):
    s_id, k = pl.program_id(0), pl.program_id(1)
    width = y_ref.shape[1]
    pairs = width // LANES
    bc_at, dt_at, z_at = width, width + 2 * N, width + 2 * N + LANES

    @pl.when(k == 0)
    def _():
        back[...] = jnp.zeros_like(back)
        after_x[...] = jnp.zeros_like(after_x)
        after_bc[...] = jnp.zeros_like(after_bc)

    @pl.when((k == 0) & (s_id == 0))
    def _():
        part_x[...] = jnp.zeros_like(part_x)
        part_bc[...] = jnp.zeros_like(part_bc)
        acc_dt[...] = jnp.zeros_like(acc_dt)

    block = order[s_id * 4 + 3 - k]
    place = block - s_id * 4
    dx_ref = pre_ref.at[pl.ds(pl.multiple_of(place * T, T), T)]
    keep = jnp.where(k < 3, 1.0, 0.0)
    lane = lane_ids((T, LANES))
    low = lane < P_SIZE
    row = lax.broadcasted_iota(jnp.int32, (T, T), 0)
    seen_t = lane >= row
    last = row == T - 1
    run = rows_ref[block, 2 * HP : 3 * HP]
    cols = cols_ref[block]
    runs_wide = dot_nn(cols, spread_run[...])
    steps_wide = dot_nn(cols, spread_steps[...])
    bc_cat = jnp.concatenate([halo[:, bc_at : bc_at + 2 * N] * keep, px[:, bc_at : bc_at + 2 * N]], axis=0)
    bc_parts = shifted(bc_cat)
    s_bc = conv(bc_parts, taps_bc[...])
    sig_bc = sigmoid(s_bc)
    bc = s_bc * sig_bc
    keys, reads = bc[:, :N].astype(bf16), bc[:, N:].astype(bf16)
    reads_t = jnp.transpose(bc[:, N:]).astype(bf16)
    scores_t = jnp.where(seen_t, dot_nt(keys, reads), 0.0)
    d_scores[...] = jnp.zeros_like(d_scores)
    d_reads = jnp.zeros((T, N), f32)
    d_keys = jnp.zeros((T, N), f32)
    head_sums = jnp.zeros((T, LANES), f32)
    stat_cols = jnp.transpose(stats[0])
    row_scale = jnp.broadcast_to(stat_cols[:, 0:1], (T, LANES))
    row_stat = jnp.broadcast_to(stat_cols[:, 1:2], (T, LANES))
    for p in range(pairs):
        at = slice(p * LANES, (p + 1) * LANES)
        x_cat = jnp.concatenate([halo[:, at] * keep, px[:, at]], axis=0)
        x_parts = shifted(x_cat)
        s_x = conv(x_parts, taps_x[:, at])
        sig_x = sigmoid(s_x)
        xs = s_x * sig_x
        steps_pair = steps_wide[:, at]
        xd = xs * steps_pair
        xr = xd.astype(bf16)
        z = px[:, z_at + p * LANES : z_at + (p + 1) * LANES]
        sig_z = sigmoid(z)
        silu_z = z * sig_z
        y = y_ref[:, at]
        y_all = y + skip[:, at] * xs
        g = y_all * silu_z
        dr = d_ref[:, at] * row_scale
        dg = gain[:, at] * dr - g * row_stat
        part_x[40:48, at] += eights(dr * g)
        dx_ref[:, z_at + p * LANES : z_at + (p + 1) * LANES] = (
            dg * y_all * (sig_z + silu_z * (1.0 - sig_z))
        ).astype(bf16)
        dy = dg * silu_z
        dyr = dy.astype(bf16)
        part_x[48:56, at] += eights(dy * xs)
        zero = jnp.zeros_like(xr)
        mixes_t = []
        wide = []
        total = d_scores[...]
        for i, h in enumerate((2 * p, 2 * p + 1)):
            cj = runs_wide[:, h * LANES : (h + 1) * LANES]
            decay = jnp.exp(jnp.minimum(run[h : h + 1] - cj, 0.0))
            mixes_t.append((decay * scores_t).astype(bf16))
            x_one = jnp.where(low, xr, zero) if i == 0 else jnp.where(low, zero, xr)
            total = total + decay * dot_nt(x_one, dyr)
            wide.append(cj)
        d_scores[...] = total
        c_pair = jnp.where(low, wide[0], wide[1])
        e_pair = jnp.exp(c_pair)
        e_left = jnp.exp(c_pair[T - 1 : T] - c_pair)
        dx_in = dot_nn(
            jnp.concatenate(mixes_t, axis=1),
            jnp.concatenate([jnp.where(low, dyr, zero), jnp.where(low, zero, dyr)], axis=0),
        )
        returning = back[:, at]
        returning_r = returning.astype(bf16)
        entering_r = s_ref[0, :, at]
        dx_out = e_left * dot_nn(keys, returning_r)
        dye = (dy * e_pair).astype(bf16)
        d_reads = d_reads + dot_nt(dye, entering_r)
        d_keys = d_keys + dot_nt((xd * e_left).astype(bf16), returning_r)
        e_last = e_pair[T - 1 : T]
        back[:, at] = e_last * returning + dot_nn(reads_t, dye)
        across = e_last * jnp.sum(returning * entering_r.astype(f32), axis=0, keepdims=True)
        xf, dyf = xr.astype(f32), dyr.astype(f32)
        two = xf * dx_in
        three = xd * dx_out
        one = dyf * y - two + jnp.where(last, across, 0.0)
        high = one.astype(bf16)
        rest = (one - high.astype(f32)).astype(bf16)
        head_sums = head_sums + dot_nn(
            jnp.concatenate([high, rest, (two + three).astype(bf16), three.astype(bf16)], axis=1),
            sums[4 * p * LANES : 4 * (p + 1) * LANES],
        )
        dxs = steps_pair * (dx_in + dx_out) + skip[:, at] * dy
        ds = dxs * (sig_x + xs * (1.0 - sig_x))
        for j in range(4):
            part_x[8 * j : 8 * j + 8, at] += eights(ds * x_parts[j])
        part_x[32:40, at] += eights(ds)
        dx_ref[:, at] = conv_back(ds, after_x[:, at], taps_x[:, at]).astype(bf16)
        after_x[:, at] = ds[:8]
    head_sums_ref[pl.ds(pl.multiple_of(place * T, T), T)] = head_sums
    ds_t = jnp.where(seen_t, d_scores[...], 0.0)
    d_keys = d_keys + dot_nn(ds_t.astype(bf16), reads)
    d_reads = d_reads + dot_nn(jnp.transpose(ds_t).astype(bf16), keys)
    ds_bc = jnp.concatenate([d_keys, d_reads], axis=1) * (sig_bc + bc * (1.0 - sig_bc))
    for j in range(4):
        part_bc[8 * j : 8 * j + 8] += eights(ds_bc * bc_parts[j])
    part_bc[32:40] += eights(ds_bc)
    dx_ref[:, bc_at : bc_at + 2 * N] = conv_back(ds_bc, after_bc[...], taps_bc[...]).astype(bf16)
    after_bc[...] = ds_bc[:8]

    @pl.when(k == 3)
    def _():
        head_cols = heads[...]
        turned = [jnp.transpose(head_sums_ref[c * T : (c + 1) * T]) for c in range(4)]
        one, both, three = (
            jnp.concatenate([t[i * HP : (i + 1) * HP] for t in turned], axis=0) for i in range(3)
        )
        logits = jnp.concatenate([rows_ref[s_id * 4 + c, 0:HP] for c in range(4)], axis=0)
        steps = jnp.concatenate([rows_ref[s_id * 4 + c, HP : 2 * HP] for c in range(4)], axis=0)
        decay_rate = jnp.concatenate([head_cols[:, 1:2]] * 4, axis=0)
        lane_h = lane_ids(one.shape)
        d_decay = running_sum_back(one, lane_h) + running_sum(three, lane_h) - three
        exact = jnp.exp(jnp.minimum(logits, 0.0)) / (1.0 + jnp.exp(-jnp.abs(logits)))
        ratio = jnp.where(logits < -15.0, 1.0, exact / jnp.maximum(steps, 1e-30))
        d_pre = both * ratio + decay_rate * d_decay * exact
        d_rate = steps * d_decay
        for c in range(4):
            at = slice(c * HP, (c + 1) * HP)
            acc_dt[0:HP] += d_rate[at]
            acc_dt[HP : 2 * HP] += d_pre[at]
            padded = jnp.concatenate([d_pre[at], jnp.zeros((LANES - HP, T), f32)], axis=0)
            pre_ref[c * T : (c + 1) * T, dt_at : dt_at + LANES] = jnp.transpose(padded).astype(bf16)

    @pl.when((k == 3) & (s_id == pl.num_programs(0) - 1))
    def _():
        acc_x[...] = jnp.zeros_like(acc_x)
        acc_bc[...] = jnp.zeros_like(acc_bc)
        for j in range(7):
            acc_x[j : j + 1] = jnp.sum(part_x[8 * j : 8 * j + 8], axis=0, keepdims=True)
        for j in range(5):
            acc_bc[j : j + 1] = jnp.sum(part_bc[8 * j : 8 * j + 8], axis=0, keepdims=True)


def hbm(*arrays):
    return [pltpu.with_memory_space_constraint(array, pltpu.HBM) for array in arrays]


def whole_spec(array):
    return pl.BlockSpec(array.shape, lambda s, k, order: (0,) * array.ndim)


def scan_forward(order, px, layer, fixed_arrays):
    rows, width = px.shape[0], layer["skip"].shape[1]
    steps = rows // T
    here = lambda s, k, order: (order[s * 4 + k], 0)
    before = lambda s, k, order: (order[s * 4 + jnp.maximum(k - 1, 0)] * (T // 8) + (T // 8 - 1), 0)
    small = (layer["taps_x"], layer["taps_bc"], layer["heads"], layer["skip"], layer["gain"]) + fixed_arrays[:2]
    whole = lambda s, k, order: (0, 0, 0)
    return pl.pallas_call(
        fwd_kernel,
        grid_spec=pltpu.PrefetchScalarGridSpec(
            num_scalar_prefetch=1,
            grid=(steps // 4, 4),
            in_specs=[
                pl.BlockSpec((T, px.shape[1]), here),
                pl.BlockSpec((8, width + 2 * N), before),
                pl.BlockSpec((rows, LANES), lambda s, k, order: (0, (width + 2 * N) // LANES)),
            ]
            + [whole_spec(m) for m in small],
            out_specs=[
                pl.BlockSpec((T, width), here),
                pl.BlockSpec((T, width), here),
                pl.BlockSpec((1, N, width), lambda s, k, order: (s * 4 + k, 0, 0)),
                pl.BlockSpec((1, 8, T), lambda s, k, order: (order[s * 4 + k], 0, 0)),
                pl.BlockSpec((steps, 3 * HP, T), whole),
                pl.BlockSpec((steps, T, LANES), whole),
            ],
            scratch_shapes=[pltpu.VMEM((N, width), f32)],
        ),
        out_shape=[
            pltpu.HBM((rows, width), bf16),
            pltpu.HBM((rows, width), f32),
            pltpu.HBM((steps, N, width), bf16),
            jax.ShapeDtypeStruct((steps, 8, T), f32),
            pltpu.HBM((steps, 3 * HP, T), f32),
            pltpu.HBM((steps, T, LANES), bf16),
        ],
        compiler_params=pltpu.CompilerParams(vmem_limit_bytes=40 * 2**20),
        cost_estimate=pl.CostEstimate(flops=12 * 10**9, bytes_accessed=14 * 2**20, transcendentals=5 * 10**6),
        name="scan_forward",
    )(order, *hbm(px, px, px), *small[:5], *hbm(*small[5:]))


def scan_backward(order, px, y, states, d_out, stats, row_steps, col_steps, layer, fixed_arrays):
    rows, width = y.shape
    steps = rows // T
    here = lambda s, k, order: (order[s * 4 + 3 - k], 0)
    before = lambda s, k, order: (order[s * 4 + jnp.maximum(2 - k, 0)] * (T // 8) + (T // 8 - 1), 0)
    small = (row_steps, col_steps, layer["taps_x"], layer["taps_bc"], layer["heads"], layer["skip"], layer["gain"])
    small = small + fixed_arrays
    fixed = lambda s, k, order: (0, 0)
    return pl.pallas_call(
        bwd_kernel,
        grid_spec=pltpu.PrefetchScalarGridSpec(
            num_scalar_prefetch=1,
            grid=(steps // 4, 4),
            in_specs=[
                pl.BlockSpec((T, px.shape[1]), here),
                pl.BlockSpec((8, width + 2 * N), before),
                pl.BlockSpec((T, width), here),
                pl.BlockSpec((1, N, width), lambda s, k, order: (s * 4 + 3 - k, 0, 0)),
                pl.BlockSpec((T, width), here),
                pl.BlockSpec((1, 8, T), lambda s, k, order: (order[s * 4 + 3 - k], 0, 0)),
            ]
            + [whole_spec(m) for m in small],
            out_specs=[
                pl.BlockSpec((4 * T, px.shape[1]), lambda s, k, order: (s, 0)),
                pl.BlockSpec((8, width), fixed),
                pl.BlockSpec((8, 2 * N), fixed),
                pl.BlockSpec((2 * HP, T), fixed),
            ],
            scratch_shapes=[
                pltpu.VMEM((N, width), f32),
                pltpu.VMEM((8, width), f32),
                pltpu.VMEM((8, 2 * N), f32),
                pltpu.VMEM((T, T), f32),
                pltpu.VMEM((4 * T, LANES), f32),
                pltpu.VMEM((56, width), f32),
                pltpu.VMEM((40, 2 * N), f32),
            ],
        ),
        out_shape=[
            pltpu.HBM((rows, px.shape[1]), bf16),
            jax.ShapeDtypeStruct((8, width), f32),
            jax.ShapeDtypeStruct((8, 2 * N), f32),
            jax.ShapeDtypeStruct((2 * HP, T), f32),
        ],
        compiler_params=pltpu.CompilerParams(vmem_limit_bytes=40 * 2**20),
        cost_estimate=pl.CostEstimate(flops=24 * 10**9, bytes_accessed=24 * 2**20, transcendentals=10**7),
        name="scan_backward",
    )(order, *hbm(px, px, y, states, d_out), stats, *hbm(*small[:2]), *small[2:7], *hbm(*small[7:]))


def dots_kernel(do, w_out, og, d_ref, dots_ref):
    d_ref[...] = dot_nn(do[...], w_out[...])
    for c in range(do.shape[0] // T):
        at = slice(c * T, (c + 1) * T)
        total = jnp.zeros((T, LANES), f32)
        for p in range(0, og.shape[1], LANES):
            total = total + d_ref[at, p : p + LANES] * og[at, p : p + LANES].astype(f32)
        dots_ref[c] = jnp.broadcast_to(jnp.sum(jnp.transpose(total), axis=0, keepdims=True), (8, T))


def rows_and_dots(do, w_out, og):
    rows, width = og.shape
    size = rows // 2
    return pl.pallas_call(
        dots_kernel,
        grid=(2,),
        in_specs=[
            pl.BlockSpec((size, do.shape[1]), lambda i: (i, 0)),
            pl.BlockSpec(w_out.shape, lambda i: (0, 0), pipeline_mode=pl.Buffered(1)),
            pl.BlockSpec((size, width), lambda i: (i, 0)),
        ],
        out_specs=[
            pl.BlockSpec((size, width), lambda i: (i, 0)),
            pl.BlockSpec((size // T, 8, T), lambda i: (i, 0, 0)),
        ],
        out_shape=[pltpu.HBM((rows, width), f32), jax.ShapeDtypeStruct((rows // T, 8, T), f32)],
        compiler_params=pltpu.CompilerParams(vmem_limit_bytes=40 * 2**20),
        cost_estimate=pl.CostEstimate(flops=4 * 10**9, bytes_accessed=10 * 2**20, transcendentals=0),
        name="rows_and_dots",
    )(*hbm(do, w_out, og))


def rows_kernel(rows, w, *outs):
    product = dot_nt(rows[...], w[...]).astype(bf16)
    size = product.shape[0] // len(outs)
    for i, out in enumerate(outs):
        out[...] = product[i * size : (i + 1) * size]


def rows_product(rows, w):
    count, size = rows.shape[0], rows.shape[0] // 4
    wide = w.shape[0] // 3
    return pl.pallas_call(
        rows_kernel,
        grid=(3,),
        in_specs=[
            pl.BlockSpec(rows.shape, lambda i: (0, 0), pipeline_mode=pl.Buffered(1)),
            pl.BlockSpec((wide, w.shape[1]), lambda i: (i, 0)),
        ],
        out_specs=[pl.BlockSpec((size, wide), lambda i: (0, i))] * 4,
        out_shape=[jax.ShapeDtypeStruct((size, w.shape[0]), bf16)] * 4,
        compiler_params=pltpu.CompilerParams(vmem_limit_bytes=40 * 2**20),
        cost_estimate=pl.CostEstimate(
            flops=4 * count * w.shape[0] * w.shape[1], bytes_accessed=2 * (rows.size + w.size), transcendentals=0
        ),
        name="rows_product",
    )(*hbm(rows, w))


def fixed_tables(width):
    heads = width // P_SIZE
    column, lane = np.indices((LANES, heads * LANES))
    spread_run = (column < 3 * HP) & (column % HP == lane // LANES)
    column, lane = np.indices((LANES, width))
    spread_steps = (column >= 3 * HP) & (column < 6 * HP) & (column % HP == lane // P_SIZE)
    feature, target = np.indices((4 * width, LANES))
    part, head = (feature // LANES) % 4, 2 * (feature // (4 * LANES)) + (feature % LANES) // P_SIZE
    sums = target == np.array([0, 0, 1, 2])[part] * HP + head
    return tuple(jnp.asarray(m, bf16) for m in (spread_run, spread_steps, sums))


tied = lax.optimization_barrier


def swap(value, axis):
    return lax.ppermute(value, axis, [(0, 1), (1, 0)])


AXES = (("section", "tensor"), ("tensor", "section"))


def spread_first(value):
    return [swap(value[s], axes[0]) for s, axes in enumerate(AXES)]


def join_first(value, received):
    return [jnp.concatenate([value[s], received[s]], axis=0) for s in range(len(AXES))]


def spread_second(twos):
    return [swap(two, axes[1]) for two, axes in zip(twos, AXES)]


def join_second(twos, received):
    return jnp.concatenate([part for pair in zip(twos, received) for part in pair], axis=0)


def spread_all(*values):
    received = tied([spread_first(value) for value in values])
    twos = [join_first(value, r) for value, r in zip(values, received)]
    received = tied([spread_second(pair) for pair in twos])
    return [join_second(pair, r) for pair, r in zip(twos, received)]


def local(
    block_input,
    plan,
    lengths,
    norm_gain,
    gate_proj,
    value_proj,
    shared_proj,
    step_proj,
    conv_value,
    conv_shared,
    head_params,
    gate_gain,
    out_proj,
    cotangent,
):
    x = lax.axis_index("section")
    yy = lax.axis_index("tensor")
    streams = block_input.shape[1]
    model_width = block_input.shape[3]
    width = gate_proj.shape[2] // 2
    head_count = step_proj.shape[2] // 2
    rows_here = gate_proj.shape[1]

    def both(value):
        other = swap(value, "section")
        return jnp.where(x == 0, value, other), jnp.where(x == 0, other, value)

    def quarters(value):
        size = value.shape[-1] // 2
        axis = value.ndim - 1
        kept = lax.dynamic_slice_in_dim(value, x * size, size, axis)
        other = swap(lax.dynamic_slice_in_dim(value, (1 - x) * size, size, axis), "section")
        return jnp.where(x == 0, kept, other), jnp.where(x == 0, other, kept)

    shared_other = swap(shared_proj[0], "tensor")
    shared_full = jnp.where(
        yy == 0,
        jnp.concatenate([shared_proj[0], shared_other], axis=1),
        jnp.concatenate([shared_other, shared_proj[0]], axis=1),
    )

    def quarter_of(value, which):
        return lax.dynamic_slice_in_dim(value, which * (value.shape[1] // 2), value.shape[1] // 2, 1)

    def packed_in(which):
        steps = jnp.pad(quarter_of(step_proj[0], which), ((0, 0), (0, LANES - head_count)))
        return jnp.concatenate([steps, quarter_of(value_proj[0], which), quarter_of(gate_proj[0], which)], axis=1)

    in_kept, in_other = packed_in(x), swap(packed_in(1 - x), "section")
    shared_section = swap(shared_full, "section")
    out_kept, out_other = quarter_of(out_proj[0], x), swap(quarter_of(out_proj[0], 1 - x), "section")
    weights = []
    for l in range(2):
        shared_l = jnp.where(x == l, shared_full, shared_section)
        rest = jnp.where(x == l, in_kept, in_other)
        packed = jnp.concatenate(
            [rest[:, LANES : LANES + width], shared_l, rest[:, :LANES], rest[:, LANES + width :]], axis=1
        )
        weights.append(
            (
                lax.all_gather(packed, "dp", axis=0, tiled=True),
                lax.all_gather(jnp.where(x == l, out_kept, out_other), "dp", axis=0, tiled=True),
            )
        )

    taps_x_two = quarters(jnp.pad(conv_value[0], ((0, 3), (0, 0))))
    shared_taps_other = swap(conv_shared[0], "tensor")
    taps_bc_full = jnp.where(
        yy == 0,
        jnp.concatenate([conv_shared[0], shared_taps_other], axis=1),
        jnp.concatenate([shared_taps_other, conv_shared[0]], axis=1),
    )
    taps_bc_two = both(jnp.pad(taps_bc_full, ((0, 3), (0, 0))))
    heads_two = quarters(head_params[0])
    gain_two = quarters(gate_gain)
    norm_two = both(norm_gain)
    layers = []
    for l in range(2):
        head_rows = heads_two[l]
        columns_of = jnp.stack([head_rows[0], -jnp.exp(head_rows[1])], axis=1)
        layers.append(
            dict(
                taps_x=taps_x_two[l],
                taps_bc=taps_bc_two[l],
                heads=jnp.pad(columns_of, ((0, HP - head_count), (0, LANES - 2))),
                skip=jnp.repeat(head_rows[2], P_SIZE)[None],
                gain=gain_two[l],
                norm=norm_two[l],
                decay=columns_of[:, 1],
            )
        )
    tables = fixed_tables(width)

    chunk = jnp.arange(4, dtype=jnp.int32)
    x_bit, y_bit = (chunk & 1) ^ x, (chunk >> 1) ^ yy
    order = jnp.concatenate([2 * y_bit + x_bit, 4 + 2 * x_bit + y_bit]).astype(jnp.int32)

    def own_rows(value):
        half = value.shape[1] // 2
        return lax.dynamic_slice_in_dim(value, x * half, half, 1)

    first_rows = (2 * yy + x) * T
    positions = first_rows + lax.broadcasted_iota(jnp.int32, (T, 1), 0)
    valid = jnp.sum(jnp.where(plan[0][:, None] == jnp.arange(streams)[None, :], lengths[0][:, None], 0), axis=0)
    keep = (positions[None] < valid[:, None, None]).astype(f32)
    u = own_rows(block_input[0]).astype(f32)
    top = own_rows(cotangent[0]).astype(f32) * keep

    size = 4 * T

    def send_half(parts):
        return [swap(parts[2 * s + 1], AXES[s][1]) for s in range(streams)]

    def add_half(parts, received):
        return [parts[2 * s].astype(f32) + received[s].astype(f32) for s in range(streams)]

    def send_quarter(twos, kind):
        return [swap(two[size // 4 :].astype(kind), AXES[s][0]) for s, two in enumerate(twos)]

    def add_quarter(twos, received):
        return jnp.stack([two[: size // 4] + other.astype(f32) for two, other in zip(twos, received)])

    saved = []
    for l in range(2):
        w_in, w_out = weights[l]
        layer = layers[l]
        rho = lax.rsqrt(jnp.mean(u * u, axis=2, keepdims=True) + eps)
        a_own = (u * rho * layer["norm"][None]).astype(bf16)
        (a,) = spread_all(a_own)
        if l == 0:
            top_rounded, a = tied((top.astype(bf16), a))
            top_received = spread_first(top_rounded)
        pre = dot_nn(a, w_in)
        if l == 0:
            pre, top_received = tied((pre, top_received))
            top_twos = join_first(top_rounded, top_received)
            top_received = spread_second(top_twos)
        og, y, states, squares, row_steps, col_steps = scan_forward(order, pre, layer, tables)
        if l == 1:
            og, do_top = tied((og, do_top))
        sq = squares[:, 0, :]
        saved.append((u, rho, a, pre, og, y, states, sq, row_steps, col_steps))
        if l == 0:
            o_part, sq_part = rows_product(og, w_out), list(sq.reshape(4, size // 2))
            o_part, top_received = tied((o_part, top_received))
            do_top = join_second(top_twos, top_received)
            received = send_half(o_part)
            twos = add_half(o_part, received)
            sq_twos = add_half(sq_part, send_half(sq_part))
            o = add_quarter(twos, send_quarter(twos, bf16))
            total = add_quarter(sq_twos, send_quarter(sq_twos, f32))[:, :, None]
            r_first = lax.rsqrt(total / DI + eps)
            o_first = o * r_first
            u = u + o_first

    def summed_rows(rows_sums):
        count = rows_sums.shape[0]
        total = rows_sums.reshape(count, streams, 2, 2, T)
        for flips, pairs in (((1, 0), (2, 3, 0, 1)), ((0, 1), (1, 0, 3, 2)), ((1, 1), (3, 2, 1, 0))):
            other = lax.ppermute(rows_sums, ("section", "tensor"), list(enumerate(pairs)))
            other = other.reshape(count, streams, 2, 2, T)
            turned = []
            for s in range(streams):
                piece = other[:, s]
                for axis in (0, 1):
                    if flips[0 if AXES[s][axis] == "section" else 1]:
                        piece = jnp.flip(piece, axis=2 - axis)
                turned.append(piece)
            total = total + jnp.stack(turned, axis=1)
        return total.reshape(count, -1)

    def rows_of_stats(scale, stat):
        pair = jnp.stack([scale.reshape(-1, T), stat.reshape(-1, T)], axis=1)
        return jnp.pad(pair, ((0, 0), (0, 6), (0, 0)))

    u, rho, a, pre, og, y, states, sq, row_steps, col_steps = saved[1]
    d_out, dots = rows_and_dots(do_top, weights[1][1], og)
    square_sums, dots = tied((summed_rows(sq.reshape(1, -1)), dots[:, 0, :].reshape(-1)))
    r_last = lax.rsqrt(square_sums[0] / DI + eps)
    scaled_og = (og.astype(f32) * r_last[:, None]).astype(bf16)
    grad_out_last = dot_tn(do_top, scaled_og).astype(bf16)
    dot_sums, grad_out_last = tied((summed_rows(dots[None]), grad_out_last))
    stats_last = rows_of_stats(r_last, r_last**3 * dot_sums[0] / DI)

    shards = [None, None]

    def pack(acc_x, acc_bc, acc_dt, da_part, a, layer):
        norm = sum(
            jnp.sum(part.astype(f32) * a[i * part.shape[0] : (i + 1) * part.shape[0]].astype(f32), axis=0)
            for i, part in enumerate(da_part)
        ) / layer["norm"][0]
        return jnp.concatenate([acc_x.reshape(-1), acc_bc.reshape(-1), jnp.sum(acc_dt, axis=1), norm])

    def sum_steps():
        devices = lax.axis_size("dp")
        same = lambda value: value
        if devices & (devices - 1):
            return [lambda value: jnp.sum(lax.all_gather(value, "dp", axis=0), axis=0), same, same]

        def add_other(value, step):
            return value + lax.ppermute(value, "dp", [(i, i ^ step) for i in range(devices)])

        steps = [functools.partial(add_other, step=1 << i) for i in range(devices.bit_length() - 1)]
        return steps + [same] * max(0, 3 - len(steps))

    def input_gradient(l, dv, da):
        u, rho = saved[l][0], saved[l][1]
        scaled = da * layers[l]["norm"][None]
        return dv + rho * scaled - u * rho**3 * jnp.mean(scaled * u, axis=2, keepdims=True)

    shard_out = lax.psum_scatter(grad_out_last, "dp", scatter_dimension=0, tiled=True)
    d_pre, acc_x, acc_bc, acc_dt = scan_backward(
        order, pre, y, states, d_out, stats_last, row_steps, col_steps, layers[1], tables
    )
    da_part = rows_product(d_pre, weights[1][0])
    d_pre, da_part = tied((d_pre, da_part))
    grad_in = dot_tn(a, d_pre).astype(bf16)
    small_last = pack(acc_x, acc_bc, acc_dt, da_part, a, layers[1])
    received, grad_after, small_last, shard_out, og = tied(
        (send_half(da_part), grad_in, small_last, shard_out, og)
    )
    o_part = rows_product(og, weights[1][1])
    small_last = small_last + 0.0 * grad_after[0, 0].astype(f32)
    twos = add_half(da_part, received)
    da = add_quarter(twos, send_quarter(twos, bf16))
    shards[1] = (shard_out, lax.psum_scatter(grad_in, "dp", scatter_dimension=0, tiled=True))
    dv = input_gradient(1, top, da)

    do_own = (dv * r_first).astype(bf16)
    kappa = r_first[:, :, 0] ** 2 * jnp.sum(dv * o_first, axis=2) / DI
    do, stat = spread_all(do_own, kappa)
    do, o_part = tied((do, o_part))
    u, rho, a, pre, og, y, states, sq, row_steps, col_steps = saved[0]
    w_in, w_out = weights[0]
    stats = rows_of_stats(jnp.ones_like(stat), stat)
    d_out = dot_nn(do, w_out)
    do, d_out = tied((do, d_out))
    grad_out = dot_tn(do, og).astype(bf16)
    grad_out, shards[1] = tied((grad_out, shards[1]))
    d_out, grad_out = tied((d_out, grad_out))
    shard_out = lax.psum_scatter(grad_out, "dp", scatter_dimension=0, tiled=True)
    d_pre, acc_x, acc_bc, acc_dt = scan_backward(
        order, pre, y, states, d_out, stats, row_steps, col_steps, layers[0], tables
    )
    d_pre, o_received = tied((d_pre, send_half(o_part)))
    o_twos = add_half(o_part, o_received)
    grad_in = dot_tn(a, d_pre).astype(bf16)
    d_pre, grad_in = tied((d_pre, grad_in))
    da_part = rows_product(d_pre, w_in)
    da_part, o_received, shard_out = tied((da_part, send_quarter(o_twos, bf16), shard_out))
    r_own = jnp.stack([r_last[s * size : s * size + T] for s in range(streams)])
    final = saved[1][0] + add_quarter(o_twos, o_received) * r_own[:, :, None]
    small = jnp.stack([pack(acc_x, acc_bc, acc_dt, da_part, a, layers[0]), small_last])
    received, small = tied((send_half(da_part), small))
    twos = add_half(da_part, received)
    steps = sum_steps()
    received, small = tied((send_quarter(twos, bf16), steps[0](small)))
    da = add_quarter(twos, received)
    dv = input_gradient(0, dv, da)
    shard_in = lax.psum_scatter(grad_in, "dp", scatter_dimension=0, tiled=True)
    ends_other = swap(jnp.where(x == 0, final, dv).astype(bf16), "section")
    for step in steps[1:]:
        small = step(small)

    partners = ((2, 3, 0, 1), (1, 0, 3, 2), (3, 2, 1, 0))

    def mine_and_partners(first, last):
        return jnp.where(x == 0, first, last), jnp.where(x == 0, last, first)

    kept, sent = mine_and_partners(small[0], small[1])
    other = swap(sent, "section")
    of_section = jnp.stack(mine_and_partners(kept, other))
    other = swap(of_section, "tensor")

    out_kept, out_sent = mine_and_partners(shard_out, shards[1][0])
    out_other = swap(out_sent, "section")
    mine = jnp.stack([jnp.where(yy == 0, of_section, other), jnp.where(yy == 0, other, of_section)], axis=1)
    mine = mine.reshape(4, -1)
    end_x, end_bc = 8 * width, 8 * width + 8 * 2 * N
    end_dt = end_bc + 2 * HP
    over_all = jnp.sum(mine, axis=0)
    halves = lax.dynamic_index_in_dim(mine.reshape(2, 2, -1), yy, 1, keepdims=False)
    by_x = halves[:, :end_x].reshape(2, 8, width).transpose(1, 0, 2).reshape(8, 2 * width)
    by_dt = halves[:, end_bc:end_dt].reshape(2, 2, HP)[:, :, :head_count].transpose(1, 0, 2).reshape(2, 2 * head_count)
    grad_conv_value = by_x[:5]
    grad_gate_gain = by_x[5]
    grad_skip = jnp.sum(by_x[6].reshape(2 * head_count, P_SIZE), axis=1)
    grad_heads = jnp.stack([by_dt[1], by_dt[0] * -jnp.exp(head_params[0, 1]), grad_skip])
    bc_all = over_all[end_x:end_bc].reshape(8, 2 * N)[:5]
    grad_conv_shared = lax.dynamic_slice_in_dim(bc_all, yy * N, N, 1)
    grad_norm = over_all[end_dt:]

    mine = jnp.where(x == 0, dv, final)
    other = ends_other.astype(f32)
    relay = jnp.concatenate([jnp.where(x == 0, mine, other), jnp.where(x == 0, other, mine)], axis=1)
    grad_out = jnp.concatenate(mine_and_partners(out_kept, out_other), axis=1).astype(f32)

    done = (relay, grad_out, grad_norm, grad_conv_value, grad_conv_shared, grad_heads, grad_gate_gain)
    shard_in, done = tied((shard_in, done))
    relay, grad_out, grad_norm, grad_conv_value, grad_conv_shared, grad_heads, grad_gate_gain = done
    in_kept, in_sent = mine_and_partners(shard_in, shards[1][1])
    bc_at, dt_at, z_at = width, width + 2 * N, width + 2 * N + LANES

    def half_of(value, which):
        return lax.dynamic_slice_in_dim(value, bc_at + which * N, N, 1)

    in_other = swap(in_sent, "section")
    bc_tensor = swap(half_of(in_kept, 1 - yy), "tensor")
    bc_diagonal = lax.ppermute(half_of(in_sent, 1 - yy), ("section", "tensor"), list(enumerate(partners[2])))
    in_other, bc_tensor, bc_diagonal = tied((in_other, bc_tensor, bc_diagonal))

    def both_halves(first, last):
        return jnp.concatenate(mine_and_partners(in_kept[:, first:last], in_other[:, first:last]), axis=1).astype(f32)

    grad_value = both_halves(0, width)
    grad_gate = both_halves(z_at, z_at + width)
    grad_step = both_halves(dt_at, dt_at + head_count)
    grad_shared = sum(
        part.astype(f32) for part in (half_of(in_kept, yy), half_of(in_other, yy), bc_tensor, bc_diagonal)
    )

    return (
        relay[None, None],
        grad_norm[None],
        grad_gate[None],
        grad_value[None],
        grad_shared[None],
        grad_step[None],
        grad_conv_value[None],
        grad_conv_shared[None],
        grad_heads[None],
        grad_gate_gain[None],
        grad_out[None],
    )


def solution(mesh):
    placed = (
        P("dp", None, "tensor", None),
        P("dp", None),
        P("dp", None),
        P("section", None),
        P("section", "dp", "tensor"),
        P("section", "dp", "tensor"),
        P("section", "dp", "tensor"),
        P("section", "dp", "tensor"),
        P("section", None, "tensor"),
        P("section", None, "tensor"),
        P("section", None, "tensor"),
        P("section", "tensor"),
        P("section", "dp", "tensor"),
        P("dp", None, "tensor", None),
    )
    return jax.shard_map(
        local,
        mesh=mesh,
        in_specs=placed,
        out_specs=(
            P("section", "dp", None, "tensor", None),
            P("section", None),
            P("section", "dp", "tensor"),
            P("section", "dp", "tensor"),
            P("section", "dp", "tensor"),
            P("section", "dp", "tensor"),
            P("section", None, "tensor"),
            P("section", None, "tensor"),
            P("section", None, "tensor"),
            P("section", "tensor"),
            P("section", "dp", "tensor"),
        ),
        check_vma=False,
    )
```

```python
import functools

import jax
import jax.numpy as jnp
import numpy as np
from jax import lax
from jax.experimental import pallas as pl
from jax.experimental.pallas import tpu as pltpu
from jax.sharding import PartitionSpec as P

DI = 3072
P_SIZE = 64
N = 128
T = 128
LANES = 128
HP = 16
eps = 1e-05
bf16 = jnp.bfloat16
f32 = jnp.float32


def dot_nn(a, b):
    return lax.dot_general(a, b, (((1,), (0,)), ((), ())), preferred_element_type=f32)


def dot_nt(a, b):
    return lax.dot_general(a, b, (((1,), (1,)), ((), ())), preferred_element_type=f32)


def dot_tn(a, b):
    return lax.dot_general(a, b, (((0,), (0,)), ((), ())), preferred_element_type=f32)


def sigmoid(v):
    return 0.5 + 0.5 * jnp.tanh(0.5 * v)


def shifted(cat):
    return (
        pltpu.roll(cat, 3, 0)[8:],
        pltpu.roll(cat, 2, 0)[8:],
        pltpu.roll(cat, 1, 0)[8:],
        cat[8:],
    )


def conv(parts, taps):
    total = taps[4:5]
    for j in range(4):
        total = total + taps[j : j + 1] * parts[j]
    return total


def shifted_back(ds, after):
    cat = jnp.concatenate([ds, after], axis=0)
    rows = cat.shape[0]
    return [pltpu.roll(cat, rows - (3 - j), 0)[: ds.shape[0]] for j in range(3)] + [ds]


def conv_back(later, taps):
    total = taps[3:4] * later[3]
    for j in range(3):
        total = total + taps[j : j + 1] * later[j]
    return total


def lane_ids(shape):
    return lax.broadcasted_iota(jnp.int32, shape, len(shape) - 1)


def running_sum(v, lane):
    step = 1
    while step < LANES:
        v = v + jnp.where(lane >= step, pltpu.roll(v, step, 1), 0.0)
        step *= 2
    return v


def running_sum_back(v, lane):
    step = 1
    while step < LANES:
        v = v + jnp.where(lane < LANES - step, pltpu.roll(v, LANES - step, 1), 0.0)
        step *= 2
    return v


def parts_of(v):
    high = v.astype(bf16)
    rest = v - high.astype(f32)
    middle = rest.astype(bf16)
    return high, middle, (rest - middle.astype(f32)).astype(bf16)


def prepare_steps(pre_dt, heads, rows_ref, cols_ref):
    chunks = pre_dt.shape[0] // T
    logits = jnp.concatenate(
        [jnp.transpose(pre_dt[c * T : (c + 1) * T])[:HP] + heads[:, 0:1] for c in range(chunks)], axis=0
    )
    small = jnp.exp(-jnp.abs(logits))
    log_part = jnp.where(small < 1e-3, small * (1.0 - small * (0.5 - small / 3.0)), jnp.log(1.0 + small))
    steps = jnp.maximum(logits, 0.0) + log_part
    decays = jnp.concatenate([heads[:, 1:2]] * chunks, axis=0)
    run = running_sum(steps * decays, lane_ids(steps.shape))
    for c in range(chunks):
        at = slice(c * HP, (c + 1) * HP)
        rows_ref[c, 0:HP] = logits[at]
        rows_ref[c, HP : 2 * HP] = steps[at]
        rows_ref[c, 2 * HP : 3 * HP] = run[at]
        split = [part.astype(f32) for part in parts_of(run[at]) + parts_of(steps[at])]
        split.append(jnp.zeros((LANES - 6 * HP, T), f32))
        cols_ref[c] = jnp.transpose(jnp.concatenate(split, axis=0)).astype(bf16)


def eights(v):
    return jnp.sum(v.reshape(v.shape[0] // 8, 8, v.shape[1]), axis=0)


def fwd_kernel(
    order, px, halo, pre_dt, taps_x, taps_bc, heads, skip, gain, spread_run, spread_steps,
    og_ref, y_ref, conv_ref, s_ref, sq_ref, rows_ref, cols_ref, state,
):
    s_id, k = pl.program_id(0), pl.program_id(1)
    width = y_ref.shape[1]
    pairs = width // LANES
    bc_at, z_at = width, width + 2 * N + LANES

    @pl.when((s_id == 0) & (k == 0))
    def _():
        prepare_steps(pre_dt[...], heads[...], rows_ref, cols_ref)

    @pl.when(k == 0)
    def _():
        state[...] = jnp.zeros_like(state)

    block = order[s_id * 4 + k]
    keep = jnp.where(k > 0, 1.0, 0.0)
    lane = lane_ids((T, LANES))
    low = lane < P_SIZE
    row = lax.broadcasted_iota(jnp.int32, (T, T), 0)
    run = rows_ref[block, 2 * HP : 3 * HP]
    cols = cols_ref[block]
    runs_wide = dot_nn(cols, spread_run[...])
    steps_wide = dot_nn(cols, spread_steps[...])
    bc_cat = jnp.concatenate([halo[:, bc_at : bc_at + 2 * N] * keep, px[:, bc_at : bc_at + 2 * N]], axis=0)
    s_bc = conv(shifted(bc_cat), taps_bc[...])
    bc = s_bc * sigmoid(s_bc)
    keys = bc[:, :N]
    keys_t = jnp.transpose(keys).astype(bf16)
    reads = bc[:, N:].astype(bf16)
    scores = jnp.where(row >= lane, dot_nt(reads, keys.astype(bf16)), 0.0)
    squares = jnp.zeros((T, LANES), f32)
    for p in range(pairs):
        at = slice(p * LANES, (p + 1) * LANES)
        x_cat = jnp.concatenate([halo[:, at] * keep, px[:, at]], axis=0)
        s_x = conv(shifted(x_cat), taps_x[:, at])
        conv_ref[:, at] = s_x
        xs = s_x * sigmoid(s_x)
        xd = xs * steps_wide[:, at]
        xr = xd.astype(bf16)
        mixes = []
        wide = []
        for h in (2 * p, 2 * p + 1):
            ci = runs_wide[:, h * LANES : (h + 1) * LANES]
            mixes.append((jnp.exp(jnp.minimum(ci - run[h : h + 1], 0.0)) * scores).astype(bf16))
            wide.append(ci)
        c_pair = jnp.where(low, wide[0], wide[1])
        e_pair = jnp.exp(c_pair)
        zero = jnp.zeros_like(xr)
        y = dot_nn(
            jnp.concatenate(mixes, axis=1),
            jnp.concatenate([jnp.where(low, xr, zero), jnp.where(low, zero, xr)], axis=0),
        )
        entering = state[:, at]
        entering_r = entering.astype(bf16)
        s_ref[0, :, at] = entering_r
        y = y + e_pair * dot_nn(reads, entering_r)
        left = (xd * jnp.exp(c_pair[T - 1 : T] - c_pair)).astype(bf16)
        state[:, at] = e_pair[T - 1 : T] * entering + dot_nn(keys_t, left)
        y_ref[:, at] = y
        z = px[:, z_at + p * LANES : z_at + (p + 1) * LANES]
        g = (y + skip[:, at] * xs) * (z * sigmoid(z))
        squares = squares + g * g
        og_ref[:, at] = (g * gain[:, at]).astype(bf16)
    sq_ref[0] = jnp.broadcast_to(jnp.sum(jnp.transpose(squares), axis=0, keepdims=True), (8, T))


def bwd_kernel(
    order, px, halo, conv_ref, y_ref, s_ref, d_ref, stats, rows_ref, cols_ref,
    taps_x, taps_bc, heads, skip, gain, spread_run, spread_steps, sums,
    pre_ref, acc_x, acc_bc, acc_dt,
    back, after_x, after_bc, d_scores, head_sums_ref, part_x, part_bc,
):
    s_id, k = pl.program_id(0), pl.program_id(1)
    width = y_ref.shape[1]
    pairs = width // LANES
    bc_at, dt_at, z_at = width, width + 2 * N, width + 2 * N + LANES

    @pl.when(k == 0)
    def _():
        back[...] = jnp.zeros_like(back)
        after_x[...] = jnp.zeros_like(after_x)
        after_bc[...] = jnp.zeros_like(after_bc)

    @pl.when((k == 0) & (s_id == 0))
    def _():
        part_x[...] = jnp.zeros_like(part_x)
        part_bc[...] = jnp.zeros_like(part_bc)
        acc_dt[...] = jnp.zeros_like(acc_dt)

    block = order[s_id * 4 + 3 - k]
    place = block - s_id * 4
    dx_ref = pre_ref.at[pl.ds(pl.multiple_of(place * T, T), T)]
    keep = jnp.where(k < 3, 1.0, 0.0)
    lane = lane_ids((T, LANES))
    low = lane < P_SIZE
    row = lax.broadcasted_iota(jnp.int32, (T, T), 0)
    seen_t = lane >= row
    last = row == T - 1
    run = rows_ref[block, 2 * HP : 3 * HP]
    cols = cols_ref[block]
    runs_wide = dot_nn(cols, spread_run[...])
    steps_wide = dot_nn(cols, spread_steps[...])
    bc_cat = jnp.concatenate([halo[:, bc_at : bc_at + 2 * N] * keep, px[:, bc_at : bc_at + 2 * N]], axis=0)
    bc_parts = shifted(bc_cat)
    s_bc = conv(bc_parts, taps_bc[...])
    sig_bc = sigmoid(s_bc)
    bc = s_bc * sig_bc
    keys, reads = bc[:, :N].astype(bf16), bc[:, N:].astype(bf16)
    reads_t = jnp.transpose(bc[:, N:]).astype(bf16)
    scores_t = jnp.where(seen_t, dot_nt(keys, reads), 0.0)
    d_scores[...] = jnp.zeros_like(d_scores)
    d_reads = jnp.zeros((T, N), f32)
    d_keys = jnp.zeros((T, N), f32)
    head_sums = jnp.zeros((T, LANES), f32)
    stat_cols = jnp.transpose(stats[0])
    row_scale = jnp.broadcast_to(stat_cols[:, 0:1], (T, LANES))
    row_stat = jnp.broadcast_to(stat_cols[:, 1:2], (T, LANES))
    for p in range(pairs):
        at = slice(p * LANES, (p + 1) * LANES)
        s_x = conv_ref[:, at]
        sig_x = sigmoid(s_x)
        xs = s_x * sig_x
        steps_pair = steps_wide[:, at]
        xd = xs * steps_pair
        xr = xd.astype(bf16)
        z = px[:, z_at + p * LANES : z_at + (p + 1) * LANES]
        sig_z = sigmoid(z)
        silu_z = z * sig_z
        y = y_ref[:, at]
        y_all = y + skip[:, at] * xs
        g = y_all * silu_z
        dr = d_ref[:, at] * row_scale
        dg = gain[:, at] * dr - g * row_stat
        part_x[40:48, at] += eights(dr * g)
        dx_ref[:, z_at + p * LANES : z_at + (p + 1) * LANES] = (
            dg * y_all * (sig_z + silu_z * (1.0 - sig_z))
        ).astype(bf16)
        dy = dg * silu_z
        dyr = dy.astype(bf16)
        part_x[48:56, at] += eights(dy * xs)
        zero = jnp.zeros_like(xr)
        mixes_t = []
        wide = []
        total = d_scores[...]
        for i, h in enumerate((2 * p, 2 * p + 1)):
            cj = runs_wide[:, h * LANES : (h + 1) * LANES]
            decay = jnp.exp(jnp.minimum(run[h : h + 1] - cj, 0.0))
            mixes_t.append((decay * scores_t).astype(bf16))
            x_one = jnp.where(low, xr, zero) if i == 0 else jnp.where(low, zero, xr)
            total = total + decay * dot_nt(x_one, dyr)
            wide.append(cj)
        d_scores[...] = total
        c_pair = jnp.where(low, wide[0], wide[1])
        e_pair = jnp.exp(c_pair)
        e_left = jnp.exp(c_pair[T - 1 : T] - c_pair)
        dx_in = dot_nn(
            jnp.concatenate(mixes_t, axis=1),
            jnp.concatenate([jnp.where(low, dyr, zero), jnp.where(low, zero, dyr)], axis=0),
        )
        returning = back[:, at]
        returning_r = returning.astype(bf16)
        entering_r = s_ref[0, :, at]
        dx_out = e_left * dot_nn(keys, returning_r)
        dye = (dy * e_pair).astype(bf16)
        d_reads = d_reads + dot_nt(dye, entering_r)
        d_keys = d_keys + dot_nt((xd * e_left).astype(bf16), returning_r)
        e_last = e_pair[T - 1 : T]
        back[:, at] = e_last * returning + dot_nn(reads_t, dye)
        across = e_last * jnp.sum(returning * entering_r.astype(f32), axis=0, keepdims=True)
        xf, dyf = xr.astype(f32), dyr.astype(f32)
        two = xf * dx_in
        three = xd * dx_out
        one = dyf * y - two + jnp.where(last, across, 0.0)
        high = one.astype(bf16)
        rest = (one - high.astype(f32)).astype(bf16)
        head_sums = head_sums + dot_nn(
            jnp.concatenate([high, rest, (two + three).astype(bf16), three.astype(bf16)], axis=1),
            sums[4 * p * LANES : 4 * (p + 1) * LANES],
        )
        dxs = steps_pair * (dx_in + dx_out) + skip[:, at] * dy
        ds = dxs * (sig_x + xs * (1.0 - sig_x))
        later = shifted_back(ds, after_x[:, at])
        pre_x = px[:, at]
        for j in range(4):
            part_x[8 * j : 8 * j + 8, at] += eights(later[j] * pre_x)
        part_x[32:40, at] += eights(ds)
        dx_ref[:, at] = conv_back(later, taps_x[:, at]).astype(bf16)
        after_x[:, at] = ds[:8]
    head_sums_ref[pl.ds(pl.multiple_of(place * T, T), T)] = head_sums
    ds_t = jnp.where(seen_t, d_scores[...], 0.0)
    d_keys = d_keys + dot_nn(ds_t.astype(bf16), reads)
    d_reads = d_reads + dot_nn(jnp.transpose(ds_t).astype(bf16), keys)
    ds_bc = jnp.concatenate([d_keys, d_reads], axis=1) * (sig_bc + bc * (1.0 - sig_bc))
    for j in range(4):
        part_bc[8 * j : 8 * j + 8] += eights(ds_bc * bc_parts[j])
    part_bc[32:40] += eights(ds_bc)
    dx_ref[:, bc_at : bc_at + 2 * N] = conv_back(shifted_back(ds_bc, after_bc[...]), taps_bc[...]).astype(bf16)
    after_bc[...] = ds_bc[:8]

    @pl.when(k == 3)
    def _():
        head_cols = heads[...]
        turned = [jnp.transpose(head_sums_ref[c * T : (c + 1) * T]) for c in range(4)]
        one, both, three = (
            jnp.concatenate([t[i * HP : (i + 1) * HP] for t in turned], axis=0) for i in range(3)
        )
        logits = jnp.concatenate([rows_ref[s_id * 4 + c, 0:HP] for c in range(4)], axis=0)
        steps = jnp.concatenate([rows_ref[s_id * 4 + c, HP : 2 * HP] for c in range(4)], axis=0)
        decay_rate = jnp.concatenate([head_cols[:, 1:2]] * 4, axis=0)
        lane_h = lane_ids(one.shape)
        d_decay = running_sum_back(one, lane_h) + running_sum(three, lane_h) - three
        exact = jnp.exp(jnp.minimum(logits, 0.0)) / (1.0 + jnp.exp(-jnp.abs(logits)))
        ratio = jnp.where(logits < -15.0, 1.0, exact / jnp.maximum(steps, 1e-30))
        d_pre = both * ratio + decay_rate * d_decay * exact
        d_rate = steps * d_decay
        for c in range(4):
            at = slice(c * HP, (c + 1) * HP)
            acc_dt[0:HP] += d_rate[at]
            acc_dt[HP : 2 * HP] += d_pre[at]
            padded = jnp.concatenate([d_pre[at], jnp.zeros((LANES - HP, T), f32)], axis=0)
            pre_ref[c * T : (c + 1) * T, dt_at : dt_at + LANES] = jnp.transpose(padded).astype(bf16)

    @pl.when((k == 3) & (s_id == pl.num_programs(0) - 1))
    def _():
        acc_x[...] = jnp.zeros_like(acc_x)
        acc_bc[...] = jnp.zeros_like(acc_bc)
        for j in range(7):
            acc_x[j : j + 1] = jnp.sum(part_x[8 * j : 8 * j + 8], axis=0, keepdims=True)
        for j in range(5):
            acc_bc[j : j + 1] = jnp.sum(part_bc[8 * j : 8 * j + 8], axis=0, keepdims=True)


def hbm(*arrays):
    return [pltpu.with_memory_space_constraint(array, pltpu.HBM) for array in arrays]


def whole_spec(array):
    return pl.BlockSpec(array.shape, lambda s, k, order: (0,) * array.ndim)


def scan_forward(order, px, layer, fixed_arrays):
    rows, width = px.shape[0], layer["skip"].shape[1]
    steps = rows // T
    here = lambda s, k, order: (order[s * 4 + k], 0)
    before = lambda s, k, order: (order[s * 4 + jnp.maximum(k - 1, 0)] * (T // 8) + (T // 8 - 1), 0)
    small = (layer["taps_x"], layer["taps_bc"], layer["heads"], layer["skip"], layer["gain"]) + fixed_arrays[:2]
    whole = lambda s, k, order: (0, 0, 0)
    return pl.pallas_call(
        fwd_kernel,
        grid_spec=pltpu.PrefetchScalarGridSpec(
            num_scalar_prefetch=1,
            grid=(steps // 4, 4),
            in_specs=[
                pl.BlockSpec((T, px.shape[1]), here),
                pl.BlockSpec((8, width + 2 * N), before),
                pl.BlockSpec((rows, LANES), lambda s, k, order: (0, (width + 2 * N) // LANES)),
            ]
            + [whole_spec(m) for m in small],
            out_specs=[
                pl.BlockSpec((T, width), here),
                pl.BlockSpec((T, width), here),
                pl.BlockSpec((T, width), here),
                pl.BlockSpec((1, N, width), lambda s, k, order: (s * 4 + k, 0, 0)),
                pl.BlockSpec((1, 8, T), lambda s, k, order: (order[s * 4 + k], 0, 0)),
                pl.BlockSpec((steps, 3 * HP, T), whole),
                pl.BlockSpec((steps, T, LANES), whole),
            ],
            scratch_shapes=[pltpu.VMEM((N, width), f32)],
        ),
        out_shape=[
            pltpu.HBM((rows, width), bf16),
            pltpu.HBM((rows, width), f32),
            pltpu.HBM((rows, width), f32),
            pltpu.HBM((steps, N, width), bf16),
            jax.ShapeDtypeStruct((steps, 8, T), f32),
            pltpu.HBM((steps, 3 * HP, T), f32),
            pltpu.HBM((steps, T, LANES), bf16),
        ],
        compiler_params=pltpu.CompilerParams(vmem_limit_bytes=40 * 2**20),
        cost_estimate=pl.CostEstimate(flops=12 * 10**9, bytes_accessed=14 * 2**20, transcendentals=5 * 10**6),
        name="scan_forward",
    )(order, *hbm(px, px, px), *small[:5], *hbm(*small[5:]))


def scan_backward(order, px, conv_x, y, states, d_out, stats, row_steps, col_steps, layer, fixed_arrays):
    rows, width = y.shape
    steps = rows // T
    here = lambda s, k, order: (order[s * 4 + 3 - k], 0)
    before = lambda s, k, order: (order[s * 4 + jnp.maximum(2 - k, 0)] * (T // 8) + (T // 8 - 1), 0)
    small = (row_steps, col_steps, layer["taps_x"], layer["taps_bc"], layer["heads"], layer["skip"], layer["gain"])
    small = small + fixed_arrays
    fixed = lambda s, k, order: (0, 0)
    return pl.pallas_call(
        bwd_kernel,
        grid_spec=pltpu.PrefetchScalarGridSpec(
            num_scalar_prefetch=1,
            grid=(steps // 4, 4),
            in_specs=[
                pl.BlockSpec((T, px.shape[1]), here),
                pl.BlockSpec((8, width + 2 * N), before),
                pl.BlockSpec((T, width), here),
                pl.BlockSpec((T, width), here),
                pl.BlockSpec((1, N, width), lambda s, k, order: (s * 4 + 3 - k, 0, 0)),
                pl.BlockSpec((T, width), here),
                pl.BlockSpec((1, 8, T), lambda s, k, order: (order[s * 4 + 3 - k], 0, 0)),
            ]
            + [whole_spec(m) for m in small],
            out_specs=[
                pl.BlockSpec((4 * T, px.shape[1]), lambda s, k, order: (s, 0)),
                pl.BlockSpec((8, width), fixed),
                pl.BlockSpec((8, 2 * N), fixed),
                pl.BlockSpec((2 * HP, T), fixed),
            ],
            scratch_shapes=[
                pltpu.VMEM((N, width), f32),
                pltpu.VMEM((8, width), f32),
                pltpu.VMEM((8, 2 * N), f32),
                pltpu.VMEM((T, T), f32),
                pltpu.VMEM((4 * T, LANES), f32),
                pltpu.VMEM((56, width), f32),
                pltpu.VMEM((40, 2 * N), f32),
            ],
        ),
        out_shape=[
            pltpu.HBM((rows, px.shape[1]), bf16),
            jax.ShapeDtypeStruct((8, width), f32),
            jax.ShapeDtypeStruct((8, 2 * N), f32),
            jax.ShapeDtypeStruct((2 * HP, T), f32),
        ],
        compiler_params=pltpu.CompilerParams(vmem_limit_bytes=40 * 2**20),
        cost_estimate=pl.CostEstimate(flops=24 * 10**9, bytes_accessed=24 * 2**20, transcendentals=10**7),
        name="scan_backward",
    )(order, *hbm(px, px, conv_x, y, states, d_out), stats, *hbm(*small[:2]), *small[2:7], *hbm(*small[7:]))


def dots_kernel(do, w_out, og, d_ref, dots_ref):
    d_ref[...] = dot_nn(do[...], w_out[...])
    for c in range(do.shape[0] // T):
        at = slice(c * T, (c + 1) * T)
        total = jnp.zeros((T, LANES), f32)
        for p in range(0, og.shape[1], LANES):
            total = total + d_ref[at, p : p + LANES] * og[at, p : p + LANES].astype(f32)
        dots_ref[c] = jnp.broadcast_to(jnp.sum(jnp.transpose(total), axis=0, keepdims=True), (8, T))


def rows_and_dots(do, w_out, og):
    rows, width = og.shape
    size = rows // 2
    return pl.pallas_call(
        dots_kernel,
        grid=(2,),
        in_specs=[
            pl.BlockSpec((size, do.shape[1]), lambda i: (i, 0)),
            pl.BlockSpec(w_out.shape, lambda i: (0, 0), pipeline_mode=pl.Buffered(1)),
            pl.BlockSpec((size, width), lambda i: (i, 0)),
        ],
        out_specs=[
            pl.BlockSpec((size, width), lambda i: (i, 0)),
            pl.BlockSpec((size // T, 8, T), lambda i: (i, 0, 0)),
        ],
        out_shape=[pltpu.HBM((rows, width), f32), jax.ShapeDtypeStruct((rows // T, 8, T), f32)],
        compiler_params=pltpu.CompilerParams(vmem_limit_bytes=40 * 2**20),
        cost_estimate=pl.CostEstimate(flops=4 * 10**9, bytes_accessed=10 * 2**20, transcendentals=0),
        name="rows_and_dots",
    )(*hbm(do, w_out, og))


def rows_kernel(rows, w, *outs):
    product = dot_nt(rows[...], w[...]).astype(bf16)
    size = product.shape[0] // len(outs)
    for i, out in enumerate(outs):
        out[...] = product[i * size : (i + 1) * size]


def rows_product(rows, w):
    count, size = rows.shape[0], rows.shape[0] // 4
    wide = w.shape[0] // 3
    return pl.pallas_call(
        rows_kernel,
        grid=(3,),
        in_specs=[
            pl.BlockSpec(rows.shape, lambda i: (0, 0), pipeline_mode=pl.Buffered(1)),
            pl.BlockSpec((wide, w.shape[1]), lambda i: (i, 0)),
        ],
        out_specs=[pl.BlockSpec((size, wide), lambda i: (0, i))] * 4,
        out_shape=[jax.ShapeDtypeStruct((size, w.shape[0]), bf16)] * 4,
        compiler_params=pltpu.CompilerParams(vmem_limit_bytes=40 * 2**20),
        cost_estimate=pl.CostEstimate(
            flops=4 * count * w.shape[0] * w.shape[1], bytes_accessed=2 * (rows.size + w.size), transcendentals=0
        ),
        name="rows_product",
    )(*hbm(rows, w))


def fixed_tables(width):
    heads = width // P_SIZE
    column, lane = np.indices((LANES, heads * LANES))
    spread_run = (column < 3 * HP) & (column % HP == lane // LANES)
    column, lane = np.indices((LANES, width))
    spread_steps = (column >= 3 * HP) & (column < 6 * HP) & (column % HP == lane // P_SIZE)
    feature, target = np.indices((4 * width, LANES))
    part, head = (feature // LANES) % 4, 2 * (feature // (4 * LANES)) + (feature % LANES) // P_SIZE
    sums = target == np.array([0, 0, 1, 2])[part] * HP + head
    return tuple(jnp.asarray(m, bf16) for m in (spread_run, spread_steps, sums))


tied = lax.optimization_barrier


def swap(value, axis):
    return lax.ppermute(value, axis, [(0, 1), (1, 0)])


AXES = (("section", "tensor"), ("tensor", "section"))


def spread_first(value):
    return [swap(value[s], axes[0]) for s, axes in enumerate(AXES)]


def join_first(value, received):
    return [jnp.concatenate([value[s], received[s]], axis=0) for s in range(len(AXES))]


def spread_second(twos):
    return [swap(two, axes[1]) for two, axes in zip(twos, AXES)]


def join_second(twos, received):
    return jnp.concatenate([part for pair in zip(twos, received) for part in pair], axis=0)


def spread_all(*values):
    received = tied([spread_first(value) for value in values])
    twos = [join_first(value, r) for value, r in zip(values, received)]
    received = tied([spread_second(pair) for pair in twos])
    return [join_second(pair, r) for pair, r in zip(twos, received)]


def local(
    block_input,
    plan,
    lengths,
    norm_gain,
    gate_proj,
    value_proj,
    shared_proj,
    step_proj,
    conv_value,
    conv_shared,
    head_params,
    gate_gain,
    out_proj,
    cotangent,
):
    x = lax.axis_index("section")
    yy = lax.axis_index("tensor")
    streams = block_input.shape[1]
    model_width = block_input.shape[3]
    width = gate_proj.shape[2] // 2
    head_count = step_proj.shape[2] // 2
    rows_here = gate_proj.shape[1]

    def both(value):
        other = swap(value, "section")
        return jnp.where(x == 0, value, other), jnp.where(x == 0, other, value)

    def quarters(value):
        size = value.shape[-1] // 2
        axis = value.ndim - 1
        kept = lax.dynamic_slice_in_dim(value, x * size, size, axis)
        other = swap(lax.dynamic_slice_in_dim(value, (1 - x) * size, size, axis), "section")
        return jnp.where(x == 0, kept, other), jnp.where(x == 0, other, kept)

    shared_other = swap(shared_proj[0], "tensor")
    shared_full = jnp.where(
        yy == 0,
        jnp.concatenate([shared_proj[0], shared_other], axis=1),
        jnp.concatenate([shared_other, shared_proj[0]], axis=1),
    )

    def quarter_of(value, which):
        return lax.dynamic_slice_in_dim(value, which * (value.shape[1] // 2), value.shape[1] // 2, 1)

    def packed_in(which):
        steps = jnp.pad(quarter_of(step_proj[0], which), ((0, 0), (0, LANES - head_count)))
        return jnp.concatenate([steps, quarter_of(value_proj[0], which), quarter_of(gate_proj[0], which)], axis=1)

    in_kept, in_other = packed_in(x), swap(packed_in(1 - x), "section")
    shared_section = swap(shared_full, "section")
    out_kept, out_other = quarter_of(out_proj[0], x), swap(quarter_of(out_proj[0], 1 - x), "section")
    weights = []
    for l in range(2):
        shared_l = jnp.where(x == l, shared_full, shared_section)
        rest = jnp.where(x == l, in_kept, in_other)
        packed = jnp.concatenate(
            [rest[:, LANES : LANES + width], shared_l, rest[:, :LANES], rest[:, LANES + width :]], axis=1
        )
        weights.append(
            (
                lax.all_gather(packed, "dp", axis=0, tiled=True),
                lax.all_gather(jnp.where(x == l, out_kept, out_other), "dp", axis=0, tiled=True),
            )
        )

    taps_x_two = quarters(jnp.pad(conv_value[0], ((0, 3), (0, 0))))
    shared_taps_other = swap(conv_shared[0], "tensor")
    taps_bc_full = jnp.where(
        yy == 0,
        jnp.concatenate([conv_shared[0], shared_taps_other], axis=1),
        jnp.concatenate([shared_taps_other, conv_shared[0]], axis=1),
    )
    taps_bc_two = both(jnp.pad(taps_bc_full, ((0, 3), (0, 0))))
    heads_two = quarters(head_params[0])
    gain_two = quarters(gate_gain)
    norm_two = both(norm_gain)
    layers = []
    for l in range(2):
        head_rows = heads_two[l]
        columns_of = jnp.stack([head_rows[0], -jnp.exp(head_rows[1])], axis=1)
        layers.append(
            dict(
                taps_x=taps_x_two[l],
                taps_bc=taps_bc_two[l],
                heads=jnp.pad(columns_of, ((0, HP - head_count), (0, LANES - 2))),
                skip=jnp.repeat(head_rows[2], P_SIZE)[None],
                gain=gain_two[l],
                norm=norm_two[l],
                decay=columns_of[:, 1],
            )
        )
    tables = fixed_tables(width)

    chunk = jnp.arange(4, dtype=jnp.int32)
    x_bit, y_bit = (chunk & 1) ^ x, (chunk >> 1) ^ yy
    order = jnp.concatenate([2 * y_bit + x_bit, 4 + 2 * x_bit + y_bit]).astype(jnp.int32)

    def own_rows(value):
        half = value.shape[1] // 2
        return lax.dynamic_slice_in_dim(value, x * half, half, 1)

    first_rows = (2 * yy + x) * T
    positions = first_rows + lax.broadcasted_iota(jnp.int32, (T, 1), 0)
    valid = jnp.sum(jnp.where(plan[0][:, None] == jnp.arange(streams)[None, :], lengths[0][:, None], 0), axis=0)
    keep = (positions[None] < valid[:, None, None]).astype(f32)
    u = own_rows(block_input[0]).astype(f32)
    top = own_rows(cotangent[0]).astype(f32) * keep

    size = 4 * T

    def send_half(parts):
        return [swap(parts[2 * s + 1], AXES[s][1]) for s in range(streams)]

    def add_half(parts, received):
        return [parts[2 * s].astype(f32) + received[s].astype(f32) for s in range(streams)]

    def send_quarter(twos, kind):
        return [swap(two[size // 4 :].astype(kind), AXES[s][0]) for s, two in enumerate(twos)]

    def add_quarter(twos, received):
        return jnp.stack([two[: size // 4] + other.astype(f32) for two, other in zip(twos, received)])

    saved = []
    for l in range(2):
        w_in, w_out = weights[l]
        layer = layers[l]
        rho = lax.rsqrt(jnp.mean(u * u, axis=2, keepdims=True) + eps)
        a_own = (u * rho * layer["norm"][None]).astype(bf16)
        (a,) = spread_all(a_own)
        if l == 0:
            top_rounded, a = tied((top.astype(bf16), a))
            top_received = spread_first(top_rounded)
        pre = dot_nn(a, w_in)
        if l == 0:
            pre, top_received = tied((pre, top_received))
            top_twos = join_first(top_rounded, top_received)
            top_received = spread_second(top_twos)
        og, y, conv_x, states, squares, row_steps, col_steps = scan_forward(order, pre, layer, tables)
        if l == 1:
            og, do_top = tied((og, do_top))
        sq = squares[:, 0, :]
        saved.append((u, rho, a, pre, og, y, conv_x, states, sq, row_steps, col_steps))
        if l == 0:
            o_part, sq_part = rows_product(og, w_out), list(sq.reshape(4, size // 2))
            o_part, top_received = tied((o_part, top_received))
            do_top = join_second(top_twos, top_received)
            received, sq_received = tied((send_half(o_part), send_half(sq_part)))
            twos, sq_twos = add_half(o_part, received), add_half(sq_part, sq_received)
            o = add_quarter(twos, send_quarter(twos, bf16))
            total = add_quarter(sq_twos, send_quarter(sq_twos, f32))[:, :, None]
            r_first = lax.rsqrt(total / DI + eps)
            o_first = o * r_first
            u = u + o_first

    def summed_rows(rows_sums):
        count = rows_sums.shape[0]
        total = rows_sums.reshape(count, streams, 2, 2, T)
        for flips, pairs in (((1, 0), (2, 3, 0, 1)), ((0, 1), (1, 0, 3, 2)), ((1, 1), (3, 2, 1, 0))):
            other = lax.ppermute(rows_sums, ("section", "tensor"), list(enumerate(pairs)))
            other = other.reshape(count, streams, 2, 2, T)
            turned = []
            for s in range(streams):
                piece = other[:, s]
                for axis in (0, 1):
                    if flips[0 if AXES[s][axis] == "section" else 1]:
                        piece = jnp.flip(piece, axis=2 - axis)
                turned.append(piece)
            total = total + jnp.stack(turned, axis=1)
        return total.reshape(count, -1)

    def rows_of_stats(scale, stat):
        pair = jnp.stack([scale.reshape(-1, T), stat.reshape(-1, T)], axis=1)
        return jnp.pad(pair, ((0, 0), (0, 6), (0, 0)))

    u, rho, a, pre, og, y, conv_x, states, sq, row_steps, col_steps = saved[1]
    d_out, dots = rows_and_dots(do_top, weights[1][1], og)
    square_sums, dots = tied((summed_rows(sq.reshape(1, -1)), dots[:, 0, :].reshape(-1)))
    r_last = lax.rsqrt(square_sums[0] / DI + eps)
    scaled_og = (og.astype(f32) * r_last[:, None]).astype(bf16)
    grad_out_last = dot_tn(do_top, scaled_og).astype(bf16)
    dot_sums, grad_out_last = tied((summed_rows(dots[None]), grad_out_last))
    stats_last = rows_of_stats(r_last, r_last**3 * dot_sums[0] / DI)

    shards = [None, None]

    def pack(acc_x, acc_bc, acc_dt, da_part, a, layer):
        norm = sum(
            jnp.sum(part.astype(f32) * a[i * part.shape[0] : (i + 1) * part.shape[0]].astype(f32), axis=0)
            for i, part in enumerate(da_part)
        ) / layer["norm"][0]
        return jnp.concatenate([acc_x.reshape(-1), acc_bc.reshape(-1), jnp.sum(acc_dt, axis=1), norm])

    def sum_steps():
        devices = lax.axis_size("dp")
        if devices & (devices - 1):
            return [lambda value: jnp.sum(lax.all_gather(value, "dp", axis=0), axis=0), lambda value: value]

        def add_others(value, masks):
            return value + sum(
                lax.ppermute(value, "dp", [(i, i ^ mask) for i in range(devices)]) for mask in masks
            )

        steps, bit = [], 1
        while bit < devices:
            four = bit > 1 and 2 * bit < devices
            steps.append(functools.partial(add_others, masks=(bit, 2 * bit, 3 * bit) if four else (bit,)))
            bit *= 4 if four else 2
        return steps + [lambda value: value] * max(0, 2 - len(steps))

    def input_gradient(l, dv, da):
        u, rho = saved[l][0], saved[l][1]
        scaled = da * layers[l]["norm"][None]
        return dv + rho * scaled - u * rho**3 * jnp.mean(scaled * u, axis=2, keepdims=True)

    shard_out = lax.psum_scatter(grad_out_last, "dp", scatter_dimension=0, tiled=True)
    d_pre, acc_x, acc_bc, acc_dt = scan_backward(
        order, pre, conv_x, y, states, d_out, stats_last, row_steps, col_steps, layers[1], tables
    )
    da_part = rows_product(d_pre, weights[1][0])
    d_pre, da_part = tied((d_pre, da_part))
    grad_in = dot_tn(a, d_pre).astype(bf16)
    small_last = pack(acc_x, acc_bc, acc_dt, da_part, a, layers[1])
    received, grad_after, small_last, shard_out, og = tied(
        (send_half(da_part), grad_in, small_last, shard_out, og)
    )
    o_part = rows_product(og, weights[1][1])
    small_last = small_last + 0.0 * grad_after[0, 0].astype(f32)
    twos = add_half(da_part, received)
    da = add_quarter(twos, send_quarter(twos, bf16))
    shards[1] = (shard_out, lax.psum_scatter(grad_in, "dp", scatter_dimension=0, tiled=True))
    dv = input_gradient(1, top, da)

    do_own = (dv * r_first).astype(bf16)
    kappa = r_first[:, :, 0] ** 2 * jnp.sum(dv * o_first, axis=2) / DI
    do, stat = spread_all(do_own, kappa)
    do, o_part = tied((do, o_part))
    u, rho, a, pre, og, y, conv_x, states, sq, row_steps, col_steps = saved[0]
    w_in, w_out = weights[0]
    stats = rows_of_stats(jnp.ones_like(stat), stat)
    d_out = dot_nn(do, w_out)
    do, d_out = tied((do, d_out))
    grad_out = dot_tn(do, og).astype(bf16)
    grad_out, shards[1] = tied((grad_out, shards[1]))
    d_out, grad_out = tied((d_out, grad_out))
    shard_out = lax.psum_scatter(grad_out, "dp", scatter_dimension=0, tiled=True)
    d_pre, acc_x, acc_bc, acc_dt = scan_backward(
        order, pre, conv_x, y, states, d_out, stats, row_steps, col_steps, layers[0], tables
    )
    d_pre, o_received = tied((d_pre, send_half(o_part)))
    grad_in = dot_tn(a, d_pre).astype(bf16)
    d_pre, grad_after, o_received = tied((d_pre, grad_in, o_received))
    o_twos = add_half(o_part, o_received)
    da_part = rows_product(d_pre, w_in)
    da_part, o_received, shard_out = tied((da_part, send_quarter(o_twos, bf16), shard_out))
    r_own = jnp.stack([r_last[s * size : s * size + T] for s in range(streams)])
    final = saved[1][0] + add_quarter(o_twos, o_received) * r_own[:, :, None]
    small = jnp.stack([pack(acc_x, acc_bc, acc_dt, da_part, a, layers[0]), small_last])
    received, small = tied((send_half(da_part), small))
    twos = add_half(da_part, received)
    steps = sum_steps()
    received, small = tied((send_quarter(twos, bf16), steps[0](small)))
    for step in steps[1:]:
        small = step(small)
    da = add_quarter(twos, received)
    dv = input_gradient(0, dv, da)
    shard_in = lax.psum_scatter(grad_in, "dp", scatter_dimension=0, tiled=True)
    ends_other = swap(jnp.where(x == 0, final, dv).astype(bf16), "section")

    partners = ((2, 3, 0, 1), (1, 0, 3, 2), (3, 2, 1, 0))

    def mine_and_partners(first, last):
        return jnp.where(x == 0, first, last), jnp.where(x == 0, last, first)

    kept, sent = mine_and_partners(small[0], small[1])
    from_section = swap(sent, "section")
    from_tensor = swap(kept, "tensor")
    from_diagonal = lax.ppermute(sent, ("section", "tensor"), list(enumerate(partners[2])))

    out_kept, out_sent = mine_and_partners(shard_out, shards[1][0])
    out_other = swap(out_sent, "section")
    ends_other, from_section, from_tensor, from_diagonal = tied(
        (ends_other, from_section, from_tensor, from_diagonal)
    )
    own_row = jnp.stack(mine_and_partners(kept, from_section))
    other_row = jnp.stack(mine_and_partners(from_tensor, from_diagonal))
    mine = jnp.stack([jnp.where(yy == 0, own_row, other_row), jnp.where(yy == 0, other_row, own_row)], axis=1)
    mine = mine.reshape(4, -1)
    end_x, end_bc = 8 * width, 8 * width + 8 * 2 * N
    end_dt = end_bc + 2 * HP
    over_all = jnp.sum(mine, axis=0)
    halves = lax.dynamic_index_in_dim(mine.reshape(2, 2, -1), yy, 1, keepdims=False)
    by_x = halves[:, :end_x].reshape(2, 8, width).transpose(1, 0, 2).reshape(8, 2 * width)
    by_dt = halves[:, end_bc:end_dt].reshape(2, 2, HP)[:, :, :head_count].transpose(1, 0, 2).reshape(2, 2 * head_count)
    grad_conv_value = by_x[:5]
    grad_gate_gain = by_x[5]
    grad_skip = jnp.sum(by_x[6].reshape(2 * head_count, P_SIZE), axis=1)
    grad_heads = jnp.stack([by_dt[1], by_dt[0] * -jnp.exp(head_params[0, 1]), grad_skip])
    bc_all = over_all[end_x:end_bc].reshape(8, 2 * N)[:5]
    grad_conv_shared = lax.dynamic_slice_in_dim(bc_all, yy * N, N, 1)
    grad_norm = over_all[end_dt:]

    mine = jnp.where(x == 0, dv, final)
    other = ends_other.astype(f32)
    relay = jnp.concatenate([jnp.where(x == 0, mine, other), jnp.where(x == 0, other, mine)], axis=1)
    grad_out = jnp.concatenate(mine_and_partners(out_kept, out_other), axis=1).astype(f32)

    shard_in, relay, grad_out = tied((shard_in, relay, grad_out))
    in_kept, in_sent = mine_and_partners(shard_in, shards[1][1])
    bc_at, dt_at, z_at = width, width + 2 * N, width + 2 * N + LANES

    def half_of(value, which):
        return lax.dynamic_slice_in_dim(value, bc_at + which * N, N, 1)

    in_other = swap(in_sent, "section")
    bc_tensor = swap(half_of(in_kept, 1 - yy), "tensor")
    bc_diagonal = lax.ppermute(half_of(in_sent, 1 - yy), ("section", "tensor"), list(enumerate(partners[2])))
    in_other, bc_tensor, bc_diagonal = tied((in_other, bc_tensor, bc_diagonal))

    def both_halves(first, last):
        return jnp.concatenate(mine_and_partners(in_kept[:, first:last], in_other[:, first:last]), axis=1).astype(f32)

    grad_value = both_halves(0, width)
    grad_gate = both_halves(z_at, z_at + width)
    grad_step = both_halves(dt_at, dt_at + head_count)
    grad_shared = sum(
        part.astype(f32) for part in (half_of(in_kept, yy), half_of(in_other, yy), bc_tensor, bc_diagonal)
    )

    return (
        relay[None, None],
        grad_norm[None],
        grad_gate[None],
        grad_value[None],
        grad_shared[None],
        grad_step[None],
        grad_conv_value[None],
        grad_conv_shared[None],
        grad_heads[None],
        grad_gate_gain[None],
        grad_out[None],
    )


def solution(mesh):
    placed = (
        P("dp", None, "tensor", None),
        P("dp", None),
        P("dp", None),
        P("section", None),
        P("section", "dp", "tensor"),
        P("section", "dp", "tensor"),
        P("section", "dp", "tensor"),
        P("section", "dp", "tensor"),
        P("section", None, "tensor"),
        P("section", None, "tensor"),
        P("section", None, "tensor"),
        P("section", "tensor"),
        P("section", "dp", "tensor"),
        P("dp", None, "tensor", None),
    )
    return jax.shard_map(
        local,
        mesh=mesh,
        in_specs=placed,
        out_specs=(
            P("section", "dp", None, "tensor", None),
            P("section", None),
            P("section", "dp", "tensor"),
            P("section", "dp", "tensor"),
            P("section", "dp", "tensor"),
            P("section", "dp", "tensor"),
            P("section", None, "tensor"),
            P("section", None, "tensor"),
            P("section", None, "tensor"),
            P("section", "tensor"),
            P("section", "dp", "tensor"),
        ),
        check_vma=False,
    )
```

```python
import functools

import jax
import jax.numpy as jnp
import numpy as np
from jax import lax
from jax.experimental import pallas as pl
from jax.experimental.pallas import tpu as pltpu
from jax.sharding import PartitionSpec as P

DI = 3072
P_SIZE = 64
N = 128
T = 128
LANES = 128
HP = 16
eps = 1e-05
bf16 = jnp.bfloat16
f32 = jnp.float32


def dot_nn(a, b):
    return lax.dot_general(a, b, (((1,), (0,)), ((), ())), preferred_element_type=f32)


def dot_nt(a, b):
    return lax.dot_general(a, b, (((1,), (1,)), ((), ())), preferred_element_type=f32)


def dot_tn(a, b):
    return lax.dot_general(a, b, (((0,), (0,)), ((), ())), preferred_element_type=f32)


def sigmoid(v):
    return 0.5 + 0.5 * jnp.tanh(0.5 * v)


def shifted(cat):
    return (
        pltpu.roll(cat, 3, 0)[8:],
        pltpu.roll(cat, 2, 0)[8:],
        pltpu.roll(cat, 1, 0)[8:],
        cat[8:],
    )


def conv(parts, taps):
    total = taps[4:5]
    for j in range(4):
        total = total + taps[j : j + 1] * parts[j]
    return total


def shifted_back(ds, after):
    cat = jnp.concatenate([ds, after], axis=0)
    rows = cat.shape[0]
    return [pltpu.roll(cat, rows - (3 - j), 0)[: ds.shape[0]] for j in range(3)] + [ds]


def conv_back(later, taps):
    total = taps[3:4] * later[3]
    for j in range(3):
        total = total + taps[j : j + 1] * later[j]
    return total


def lane_ids(shape):
    return lax.broadcasted_iota(jnp.int32, shape, len(shape) - 1)


def running_sum(v, lane):
    step = 1
    while step < LANES:
        v = v + jnp.where(lane >= step, pltpu.roll(v, step, 1), 0.0)
        step *= 2
    return v


def running_sum_back(v, lane):
    step = 1
    while step < LANES:
        v = v + jnp.where(lane < LANES - step, pltpu.roll(v, LANES - step, 1), 0.0)
        step *= 2
    return v


def parts_of(v):
    high = v.astype(bf16)
    rest = v - high.astype(f32)
    middle = rest.astype(bf16)
    return high, middle, (rest - middle.astype(f32)).astype(bf16)


def prepare_steps(pre_dt, heads, rows_ref, cols_ref):
    chunks = pre_dt.shape[0] // T
    logits = jnp.concatenate(
        [jnp.transpose(pre_dt[c * T : (c + 1) * T])[:HP] + heads[:, 0:1] for c in range(chunks)], axis=0
    )
    small = jnp.exp(-jnp.abs(logits))
    log_part = jnp.where(small < 1e-3, small * (1.0 - small * (0.5 - small / 3.0)), jnp.log(1.0 + small))
    steps = jnp.maximum(logits, 0.0) + log_part
    decays = jnp.concatenate([heads[:, 1:2]] * chunks, axis=0)
    run = running_sum(steps * decays, lane_ids(steps.shape))
    for c in range(chunks):
        at = slice(c * HP, (c + 1) * HP)
        rows_ref[c, 0:HP] = logits[at]
        rows_ref[c, HP : 2 * HP] = steps[at]
        rows_ref[c, 2 * HP : 3 * HP] = run[at]
        split = [part.astype(f32) for part in parts_of(run[at]) + parts_of(steps[at])]
        split.append(jnp.zeros((LANES - 6 * HP, T), f32))
        cols_ref[c] = jnp.transpose(jnp.concatenate(split, axis=0)).astype(bf16)


def eights(v):
    return jnp.sum(v.reshape(v.shape[0] // 8, 8, v.shape[1]), axis=0)


def fwd_kernel(
    order, px, halo, pre_dt, taps_x, taps_bc, heads, skip, gain, spread_run, spread_steps,
    og_ref, y_ref, conv_ref, s_ref, sq_ref, rows_ref, cols_ref, state,
):
    s_id, k = pl.program_id(0), pl.program_id(1)
    width = y_ref.shape[1]
    pairs = width // LANES
    bc_at, z_at = width, width + 2 * N + LANES

    @pl.when((s_id == 0) & (k == 0))
    def _():
        prepare_steps(pre_dt[...], heads[...], rows_ref, cols_ref)

    @pl.when(k == 0)
    def _():
        state[...] = jnp.zeros_like(state)

    block = order[s_id * 4 + k]
    keep = jnp.where(k > 0, 1.0, 0.0)
    lane = lane_ids((T, LANES))
    low = lane < P_SIZE
    row = lax.broadcasted_iota(jnp.int32, (T, T), 0)
    run = rows_ref[block, 2 * HP : 3 * HP]
    cols = cols_ref[block]
    runs_wide = dot_nn(cols, spread_run[...])
    steps_wide = dot_nn(cols, spread_steps[...])
    bc_cat = jnp.concatenate([halo[:, bc_at : bc_at + 2 * N] * keep, px[:, bc_at : bc_at + 2 * N]], axis=0)
    s_bc = conv(shifted(bc_cat), taps_bc[...])
    bc = s_bc * sigmoid(s_bc)
    keys = bc[:, :N]
    keys_t = jnp.transpose(keys).astype(bf16)
    reads = bc[:, N:].astype(bf16)
    scores = jnp.where(row >= lane, dot_nt(reads, keys.astype(bf16)), 0.0)
    squares = jnp.zeros((T, LANES), f32)
    for p in range(pairs):
        at = slice(p * LANES, (p + 1) * LANES)
        x_cat = jnp.concatenate([halo[:, at] * keep, px[:, at]], axis=0)
        s_x = conv(shifted(x_cat), taps_x[:, at])
        conv_ref[:, at] = s_x
        xs = s_x * sigmoid(s_x)
        xd = xs * steps_wide[:, at]
        xr = xd.astype(bf16)
        mixes = []
        wide = []
        for h in (2 * p, 2 * p + 1):
            ci = runs_wide[:, h * LANES : (h + 1) * LANES]
            mixes.append((jnp.exp(jnp.minimum(ci - run[h : h + 1], 0.0)) * scores).astype(bf16))
            wide.append(ci)
        c_pair = jnp.where(low, wide[0], wide[1])
        e_pair = jnp.exp(c_pair)
        zero = jnp.zeros_like(xr)
        y = dot_nn(
            jnp.concatenate(mixes, axis=1),
            jnp.concatenate([jnp.where(low, xr, zero), jnp.where(low, zero, xr)], axis=0),
        )
        entering = state[:, at]
        entering_r = entering.astype(bf16)
        s_ref[0, :, at] = entering_r
        y = y + e_pair * dot_nn(reads, entering_r)
        left = (xd * jnp.exp(c_pair[T - 1 : T] - c_pair)).astype(bf16)
        state[:, at] = e_pair[T - 1 : T] * entering + dot_nn(keys_t, left)
        y_ref[:, at] = y
        z = px[:, z_at + p * LANES : z_at + (p + 1) * LANES]
        g = (y + skip[:, at] * xs) * (z * sigmoid(z))
        squares = squares + g * g
        og_ref[:, at] = (g * gain[:, at]).astype(bf16)
    sq_ref[0] = jnp.broadcast_to(jnp.sum(jnp.transpose(squares), axis=0, keepdims=True), (8, T))


def bwd_kernel(
    order, px, halo, conv_ref, y_ref, s_ref, d_ref, stats, rows_ref, cols_ref,
    taps_x, taps_bc, heads, skip, gain, spread_run, spread_steps, sums,
    pre_ref, acc_x, acc_bc, acc_dt,
    back, after_x, after_bc, d_scores, head_sums_ref, part_x, part_bc,
):
    s_id, k = pl.program_id(0), pl.program_id(1)
    width = y_ref.shape[1]
    pairs = width // LANES
    bc_at, dt_at, z_at = width, width + 2 * N, width + 2 * N + LANES

    @pl.when(k == 0)
    def _():
        back[...] = jnp.zeros_like(back)
        after_x[...] = jnp.zeros_like(after_x)
        after_bc[...] = jnp.zeros_like(after_bc)

    @pl.when((k == 0) & (s_id == 0))
    def _():
        part_x[...] = jnp.zeros_like(part_x)
        part_bc[...] = jnp.zeros_like(part_bc)
        acc_dt[...] = jnp.zeros_like(acc_dt)

    block = order[s_id * 4 + 3 - k]
    place = block - s_id * 4
    dx_ref = pre_ref.at[pl.ds(pl.multiple_of(place * T, T), T)]
    keep = jnp.where(k < 3, 1.0, 0.0)
    lane = lane_ids((T, LANES))
    low = lane < P_SIZE
    row = lax.broadcasted_iota(jnp.int32, (T, T), 0)
    seen_t = lane >= row
    last = row == T - 1
    run = rows_ref[block, 2 * HP : 3 * HP]
    cols = cols_ref[block]
    runs_wide = dot_nn(cols, spread_run[...])
    steps_wide = dot_nn(cols, spread_steps[...])
    bc_cat = jnp.concatenate([halo[:, bc_at : bc_at + 2 * N] * keep, px[:, bc_at : bc_at + 2 * N]], axis=0)
    bc_parts = shifted(bc_cat)
    s_bc = conv(bc_parts, taps_bc[...])
    sig_bc = sigmoid(s_bc)
    bc = s_bc * sig_bc
    keys, reads = bc[:, :N].astype(bf16), bc[:, N:].astype(bf16)
    reads_t = jnp.transpose(bc[:, N:]).astype(bf16)
    scores_t = jnp.where(seen_t, dot_nt(keys, reads), 0.0)
    d_scores[...] = jnp.zeros_like(d_scores)
    d_reads = jnp.zeros((T, N), f32)
    d_keys = jnp.zeros((T, N), f32)
    head_sums = jnp.zeros((T, LANES), f32)
    stat_cols = jnp.transpose(stats[0])
    row_scale = jnp.broadcast_to(stat_cols[:, 0:1], (T, LANES))
    row_stat = jnp.broadcast_to(stat_cols[:, 1:2], (T, LANES))
    for p in range(pairs):
        at = slice(p * LANES, (p + 1) * LANES)
        s_x = conv_ref[:, at]
        sig_x = sigmoid(s_x)
        xs = s_x * sig_x
        steps_pair = steps_wide[:, at]
        xd = xs * steps_pair
        xr = xd.astype(bf16)
        z = px[:, z_at + p * LANES : z_at + (p + 1) * LANES]
        sig_z = sigmoid(z)
        silu_z = z * sig_z
        y = y_ref[:, at]
        y_all = y + skip[:, at] * xs
        g = y_all * silu_z
        dr = d_ref[:, at] * row_scale
        dg = gain[:, at] * dr - g * row_stat
        part_x[40:48, at] += eights(dr * g)
        dx_ref[:, z_at + p * LANES : z_at + (p + 1) * LANES] = (
            dg * y_all * (sig_z + silu_z * (1.0 - sig_z))
        ).astype(bf16)
        dy = dg * silu_z
        dyr = dy.astype(bf16)
        part_x[48:56, at] += eights(dy * xs)
        zero = jnp.zeros_like(xr)
        mixes_t = []
        wide = []
        total = d_scores[...]
        for i, h in enumerate((2 * p, 2 * p + 1)):
            cj = runs_wide[:, h * LANES : (h + 1) * LANES]
            decay = jnp.exp(jnp.minimum(run[h : h + 1] - cj, 0.0))
            mixes_t.append((decay * scores_t).astype(bf16))
            x_one = jnp.where(low, xr, zero) if i == 0 else jnp.where(low, zero, xr)
            total = total + decay * dot_nt(x_one, dyr)
            wide.append(cj)
        d_scores[...] = total
        c_pair = jnp.where(low, wide[0], wide[1])
        e_pair = jnp.exp(c_pair)
        e_left = jnp.exp(c_pair[T - 1 : T] - c_pair)
        dx_in = dot_nn(
            jnp.concatenate(mixes_t, axis=1),
            jnp.concatenate([jnp.where(low, dyr, zero), jnp.where(low, zero, dyr)], axis=0),
        )
        returning = back[:, at]
        returning_r = returning.astype(bf16)
        entering_r = s_ref[0, :, at]
        dx_out = e_left * dot_nn(keys, returning_r)
        dye = (dy * e_pair).astype(bf16)
        d_reads = d_reads + dot_nt(dye, entering_r)
        d_keys = d_keys + dot_nt((xd * e_left).astype(bf16), returning_r)
        e_last = e_pair[T - 1 : T]
        back[:, at] = e_last * returning + dot_nn(reads_t, dye)
        across = e_last * jnp.sum(returning * entering_r.astype(f32), axis=0, keepdims=True)
        xf, dyf = xr.astype(f32), dyr.astype(f32)
        two = xf * dx_in
        three = xd * dx_out
        one = dyf * y - two + jnp.where(last, across, 0.0)
        high = one.astype(bf16)
        rest = (one - high.astype(f32)).astype(bf16)
        head_sums = head_sums + dot_nn(
            jnp.concatenate([high, rest, (two + three).astype(bf16), three.astype(bf16)], axis=1),
            sums[4 * p * LANES : 4 * (p + 1) * LANES],
        )
        dxs = steps_pair * (dx_in + dx_out) + skip[:, at] * dy
        ds = dxs * (sig_x + xs * (1.0 - sig_x))
        later = shifted_back(ds, after_x[:, at])
        pre_x = px[:, at]
        for j in range(4):
            part_x[8 * j : 8 * j + 8, at] += eights(later[j] * pre_x)
        part_x[32:40, at] += eights(ds)
        dx_ref[:, at] = conv_back(later, taps_x[:, at]).astype(bf16)
        after_x[:, at] = ds[:8]
    head_sums_ref[pl.ds(pl.multiple_of(place * T, T), T)] = head_sums
    ds_t = jnp.where(seen_t, d_scores[...], 0.0)
    d_keys = d_keys + dot_nn(ds_t.astype(bf16), reads)
    d_reads = d_reads + dot_nn(jnp.transpose(ds_t).astype(bf16), keys)
    ds_bc = jnp.concatenate([d_keys, d_reads], axis=1) * (sig_bc + bc * (1.0 - sig_bc))
    for j in range(4):
        part_bc[8 * j : 8 * j + 8] += eights(ds_bc * bc_parts[j])
    part_bc[32:40] += eights(ds_bc)
    dx_ref[:, bc_at : bc_at + 2 * N] = conv_back(shifted_back(ds_bc, after_bc[...]), taps_bc[...]).astype(bf16)
    after_bc[...] = ds_bc[:8]

    @pl.when(k == 3)
    def _():
        head_cols = heads[...]
        turned = [jnp.transpose(head_sums_ref[c * T : (c + 1) * T]) for c in range(4)]
        one, both, three = (
            jnp.concatenate([t[i * HP : (i + 1) * HP] for t in turned], axis=0) for i in range(3)
        )
        logits = jnp.concatenate([rows_ref[s_id * 4 + c, 0:HP] for c in range(4)], axis=0)
        steps = jnp.concatenate([rows_ref[s_id * 4 + c, HP : 2 * HP] for c in range(4)], axis=0)
        decay_rate = jnp.concatenate([head_cols[:, 1:2]] * 4, axis=0)
        lane_h = lane_ids(one.shape)
        d_decay = running_sum_back(one, lane_h) + running_sum(three, lane_h) - three
        exact = jnp.exp(jnp.minimum(logits, 0.0)) / (1.0 + jnp.exp(-jnp.abs(logits)))
        ratio = jnp.where(logits < -15.0, 1.0, exact / jnp.maximum(steps, 1e-30))
        d_pre = both * ratio + decay_rate * d_decay * exact
        d_rate = steps * d_decay
        for c in range(4):
            at = slice(c * HP, (c + 1) * HP)
            acc_dt[0:HP] += d_rate[at]
            acc_dt[HP : 2 * HP] += d_pre[at]
            padded = jnp.concatenate([d_pre[at], jnp.zeros((LANES - HP, T), f32)], axis=0)
            pre_ref[c * T : (c + 1) * T, dt_at : dt_at + LANES] = jnp.transpose(padded).astype(bf16)

    @pl.when((k == 3) & (s_id == pl.num_programs(0) - 1))
    def _():
        acc_x[...] = jnp.zeros_like(acc_x)
        acc_bc[...] = jnp.zeros_like(acc_bc)
        for j in range(7):
            acc_x[j : j + 1] = jnp.sum(part_x[8 * j : 8 * j + 8], axis=0, keepdims=True)
        for j in range(5):
            acc_bc[j : j + 1] = jnp.sum(part_bc[8 * j : 8 * j + 8], axis=0, keepdims=True)


def hbm(*arrays):
    return [pltpu.with_memory_space_constraint(array, pltpu.HBM) for array in arrays]


def whole_spec(array):
    return pl.BlockSpec(array.shape, lambda s, k, order: (0,) * array.ndim)


def scan_forward(order, px, layer, fixed_arrays):
    rows, width = px.shape[0], layer["skip"].shape[1]
    steps = rows // T
    here = lambda s, k, order: (order[s * 4 + k], 0)
    before = lambda s, k, order: (order[s * 4 + jnp.maximum(k - 1, 0)] * (T // 8) + (T // 8 - 1), 0)
    small = (layer["taps_x"], layer["taps_bc"], layer["heads"], layer["skip"], layer["gain"]) + fixed_arrays[:2]
    whole = lambda s, k, order: (0, 0, 0)
    return pl.pallas_call(
        fwd_kernel,
        grid_spec=pltpu.PrefetchScalarGridSpec(
            num_scalar_prefetch=1,
            grid=(steps // 4, 4),
            in_specs=[
                pl.BlockSpec((T, px.shape[1]), here),
                pl.BlockSpec((8, width + 2 * N), before),
                pl.BlockSpec((rows, LANES), lambda s, k, order: (0, (width + 2 * N) // LANES)),
            ]
            + [whole_spec(m) for m in small],
            out_specs=[
                pl.BlockSpec((T, width), here),
                pl.BlockSpec((T, width), here),
                pl.BlockSpec((T, width), here),
                pl.BlockSpec((1, N, width), lambda s, k, order: (s * 4 + k, 0, 0)),
                pl.BlockSpec((1, 8, T), lambda s, k, order: (order[s * 4 + k], 0, 0)),
                pl.BlockSpec((steps, 3 * HP, T), whole),
                pl.BlockSpec((steps, T, LANES), whole),
            ],
            scratch_shapes=[pltpu.VMEM((N, width), f32)],
        ),
        out_shape=[
            pltpu.HBM((rows, width), bf16),
            pltpu.HBM((rows, width), f32),
            pltpu.HBM((rows, width), f32),
            pltpu.HBM((steps, N, width), bf16),
            jax.ShapeDtypeStruct((steps, 8, T), f32),
            pltpu.HBM((steps, 3 * HP, T), f32),
            pltpu.HBM((steps, T, LANES), bf16),
        ],
        compiler_params=pltpu.CompilerParams(vmem_limit_bytes=40 * 2**20),
        cost_estimate=pl.CostEstimate(flops=12 * 10**9, bytes_accessed=14 * 2**20, transcendentals=5 * 10**6),
        name="scan_forward",
    )(order, px, px, px, *small)


def scan_backward(order, px, conv_x, y, states, d_out, stats, row_steps, col_steps, layer, fixed_arrays):
    rows, width = y.shape
    steps = rows // T
    here = lambda s, k, order: (order[s * 4 + 3 - k], 0)
    before = lambda s, k, order: (order[s * 4 + jnp.maximum(2 - k, 0)] * (T // 8) + (T // 8 - 1), 0)
    small = (row_steps, col_steps, layer["taps_x"], layer["taps_bc"], layer["heads"], layer["skip"], layer["gain"])
    small = small + fixed_arrays
    fixed = lambda s, k, order: (0, 0)
    return pl.pallas_call(
        bwd_kernel,
        grid_spec=pltpu.PrefetchScalarGridSpec(
            num_scalar_prefetch=1,
            grid=(steps // 4, 4),
            in_specs=[
                pl.BlockSpec((T, px.shape[1]), here),
                pl.BlockSpec((8, width + 2 * N), before),
                pl.BlockSpec((T, width), here),
                pl.BlockSpec((T, width), here),
                pl.BlockSpec((1, N, width), lambda s, k, order: (s * 4 + 3 - k, 0, 0)),
                pl.BlockSpec((T, width), here),
                pl.BlockSpec((1, 8, T), lambda s, k, order: (order[s * 4 + 3 - k], 0, 0)),
            ]
            + [whole_spec(m) for m in small],
            out_specs=[
                pl.BlockSpec((4 * T, px.shape[1]), lambda s, k, order: (s, 0)),
                pl.BlockSpec((8, width), fixed),
                pl.BlockSpec((8, 2 * N), fixed),
                pl.BlockSpec((2 * HP, T), fixed),
            ],
            scratch_shapes=[
                pltpu.VMEM((N, width), f32),
                pltpu.VMEM((8, width), f32),
                pltpu.VMEM((8, 2 * N), f32),
                pltpu.VMEM((T, T), f32),
                pltpu.VMEM((4 * T, LANES), f32),
                pltpu.VMEM((56, width), f32),
                pltpu.VMEM((40, 2 * N), f32),
            ],
        ),
        out_shape=[
            pltpu.HBM((rows, px.shape[1]), bf16),
            jax.ShapeDtypeStruct((8, width), f32),
            jax.ShapeDtypeStruct((8, 2 * N), f32),
            jax.ShapeDtypeStruct((2 * HP, T), f32),
        ],
        compiler_params=pltpu.CompilerParams(vmem_limit_bytes=40 * 2**20),
        cost_estimate=pl.CostEstimate(flops=24 * 10**9, bytes_accessed=24 * 2**20, transcendentals=10**7),
        name="scan_backward",
    )(order, *hbm(px, px, conv_x, y, states, d_out), stats, *hbm(*small[:2]), *small[2:7], *hbm(*small[7:]))


def dots_kernel(do, w_out, og, d_ref, dots_ref):
    d_ref[...] = dot_nn(do[...], w_out[...])
    for c in range(do.shape[0] // T):
        at = slice(c * T, (c + 1) * T)
        total = jnp.zeros((T, LANES), f32)
        for p in range(0, og.shape[1], LANES):
            total = total + d_ref[at, p : p + LANES] * og[at, p : p + LANES].astype(f32)
        dots_ref[c] = jnp.broadcast_to(jnp.sum(jnp.transpose(total), axis=0, keepdims=True), (8, T))


def rows_and_dots(do, w_out, og):
    rows, width = og.shape
    size = rows // 2
    return pl.pallas_call(
        dots_kernel,
        grid=(2,),
        in_specs=[
            pl.BlockSpec((size, do.shape[1]), lambda i: (i, 0)),
            pl.BlockSpec(w_out.shape, lambda i: (0, 0), pipeline_mode=pl.Buffered(1)),
            pl.BlockSpec((size, width), lambda i: (i, 0)),
        ],
        out_specs=[
            pl.BlockSpec((size, width), lambda i: (i, 0)),
            pl.BlockSpec((size // T, 8, T), lambda i: (i, 0, 0)),
        ],
        out_shape=[pltpu.HBM((rows, width), f32), jax.ShapeDtypeStruct((rows // T, 8, T), f32)],
        compiler_params=pltpu.CompilerParams(vmem_limit_bytes=40 * 2**20),
        cost_estimate=pl.CostEstimate(flops=4 * 10**9, bytes_accessed=10 * 2**20, transcendentals=0),
        name="rows_and_dots",
    )(*hbm(do, w_out, og))


def rows_kernel(rows, w, *outs):
    product = dot_nt(rows[...], w[...]).astype(bf16)
    size = product.shape[0] // len(outs)
    for i, out in enumerate(outs):
        out[...] = product[i * size : (i + 1) * size]


def rows_product(rows, w):
    count, size = rows.shape[0], rows.shape[0] // 4
    wide = w.shape[0] // 3
    return pl.pallas_call(
        rows_kernel,
        grid=(3,),
        in_specs=[
            pl.BlockSpec(rows.shape, lambda i: (0, 0), pipeline_mode=pl.Buffered(1)),
            pl.BlockSpec((wide, w.shape[1]), lambda i: (i, 0)),
        ],
        out_specs=[pl.BlockSpec((size, wide), lambda i: (0, i))] * 4,
        out_shape=[jax.ShapeDtypeStruct((size, w.shape[0]), bf16)] * 4,
        compiler_params=pltpu.CompilerParams(vmem_limit_bytes=40 * 2**20),
        cost_estimate=pl.CostEstimate(
            flops=4 * count * w.shape[0] * w.shape[1], bytes_accessed=2 * (rows.size + w.size), transcendentals=0
        ),
        name="rows_product",
    )(*hbm(rows, w))


def fixed_tables(width):
    heads = width // P_SIZE
    column, lane = np.indices((LANES, heads * LANES))
    spread_run = (column < 3 * HP) & (column % HP == lane // LANES)
    column, lane = np.indices((LANES, width))
    spread_steps = (column >= 3 * HP) & (column < 6 * HP) & (column % HP == lane // P_SIZE)
    feature, target = np.indices((4 * width, LANES))
    part, head = (feature // LANES) % 4, 2 * (feature // (4 * LANES)) + (feature % LANES) // P_SIZE
    sums = target == np.array([0, 0, 1, 2])[part] * HP + head
    return tuple(jnp.asarray(m, bf16) for m in (spread_run, spread_steps, sums))


tied = lax.optimization_barrier


def swap(value, axis):
    return lax.ppermute(value, axis, [(0, 1), (1, 0)])


AXES = (("section", "tensor"), ("tensor", "section"))


def spread_first(value):
    return [swap(value[s], axes[0]) for s, axes in enumerate(AXES)]


def join_first(value, received):
    return [jnp.concatenate([value[s], received[s]], axis=0) for s in range(len(AXES))]


def spread_second(twos):
    return [swap(two, axes[1]) for two, axes in zip(twos, AXES)]


def join_second(twos, received):
    return jnp.concatenate([part for pair in zip(twos, received) for part in pair], axis=0)


def spread_all(*values):
    received = tied([spread_first(value) for value in values])
    twos = [join_first(value, r) for value, r in zip(values, received)]
    received = tied([spread_second(pair) for pair in twos])
    return [join_second(pair, r) for pair, r in zip(twos, received)]


def local(
    block_input,
    plan,
    lengths,
    norm_gain,
    gate_proj,
    value_proj,
    shared_proj,
    step_proj,
    conv_value,
    conv_shared,
    head_params,
    gate_gain,
    out_proj,
    cotangent,
):
    x = lax.axis_index("section")
    yy = lax.axis_index("tensor")
    streams = block_input.shape[1]
    model_width = block_input.shape[3]
    width = gate_proj.shape[2] // 2
    head_count = step_proj.shape[2] // 2
    rows_here = gate_proj.shape[1]

    def both(value):
        other = swap(value, "section")
        return jnp.where(x == 0, value, other), jnp.where(x == 0, other, value)

    def quarters(value):
        size = value.shape[-1] // 2
        axis = value.ndim - 1
        kept = lax.dynamic_slice_in_dim(value, x * size, size, axis)
        other = swap(lax.dynamic_slice_in_dim(value, (1 - x) * size, size, axis), "section")
        return jnp.where(x == 0, kept, other), jnp.where(x == 0, other, kept)

    shared_other = swap(shared_proj[0], "tensor")
    shared_full = jnp.where(
        yy == 0,
        jnp.concatenate([shared_proj[0], shared_other], axis=1),
        jnp.concatenate([shared_other, shared_proj[0]], axis=1),
    )

    def quarter_of(value, which):
        return lax.dynamic_slice_in_dim(value, which * (value.shape[1] // 2), value.shape[1] // 2, 1)

    def packed_in(which):
        steps = jnp.pad(quarter_of(step_proj[0], which), ((0, 0), (0, LANES - head_count)))
        return jnp.concatenate([steps, quarter_of(value_proj[0], which), quarter_of(gate_proj[0], which)], axis=1)

    in_kept, in_other = packed_in(x), swap(packed_in(1 - x), "section")
    shared_section = swap(shared_full, "section")
    out_kept, out_other = quarter_of(out_proj[0], x), swap(quarter_of(out_proj[0], 1 - x), "section")
    weights = []
    for l in range(2):
        shared_l = jnp.where(x == l, shared_full, shared_section)
        rest = jnp.where(x == l, in_kept, in_other)
        packed = jnp.concatenate(
            [rest[:, LANES : LANES + width], shared_l, rest[:, :LANES], rest[:, LANES + width :]], axis=1
        )
        weights.append(
            (
                lax.all_gather(packed, "dp", axis=0, tiled=True),
                lax.all_gather(jnp.where(x == l, out_kept, out_other), "dp", axis=0, tiled=True),
            )
        )

    taps_x_two = quarters(jnp.pad(conv_value[0], ((0, 3), (0, 0))))
    shared_taps_other = swap(conv_shared[0], "tensor")
    taps_bc_full = jnp.where(
        yy == 0,
        jnp.concatenate([conv_shared[0], shared_taps_other], axis=1),
        jnp.concatenate([shared_taps_other, conv_shared[0]], axis=1),
    )
    taps_bc_two = both(jnp.pad(taps_bc_full, ((0, 3), (0, 0))))
    heads_two = quarters(head_params[0])
    gain_two = quarters(gate_gain)
    norm_two = both(norm_gain)
    layers = []
    for l in range(2):
        head_rows = heads_two[l]
        columns_of = jnp.stack([head_rows[0], -jnp.exp(head_rows[1])], axis=1)
        layers.append(
            dict(
                taps_x=taps_x_two[l],
                taps_bc=taps_bc_two[l],
                heads=jnp.pad(columns_of, ((0, HP - head_count), (0, LANES - 2))),
                skip=jnp.repeat(head_rows[2], P_SIZE)[None],
                gain=gain_two[l],
                norm=norm_two[l],
                decay=columns_of[:, 1],
            )
        )
    tables = fixed_tables(width)

    chunk = jnp.arange(4, dtype=jnp.int32)
    x_bit, y_bit = (chunk & 1) ^ x, (chunk >> 1) ^ yy
    order = jnp.concatenate([2 * y_bit + x_bit, 4 + 2 * x_bit + y_bit]).astype(jnp.int32)

    def own_rows(value):
        half = value.shape[1] // 2
        return lax.dynamic_slice_in_dim(value, x * half, half, 1)

    first_rows = (2 * yy + x) * T
    positions = first_rows + lax.broadcasted_iota(jnp.int32, (T, 1), 0)
    valid = jnp.sum(jnp.where(plan[0][:, None] == jnp.arange(streams)[None, :], lengths[0][:, None], 0), axis=0)
    keep = (positions[None] < valid[:, None, None]).astype(f32)
    u = own_rows(block_input[0]).astype(f32)
    top = own_rows(cotangent[0]).astype(f32) * keep

    size = 4 * T

    def send_half(parts):
        return [swap(parts[2 * s + 1], AXES[s][1]) for s in range(streams)]

    def add_half(parts, received):
        return [parts[2 * s].astype(f32) + received[s].astype(f32) for s in range(streams)]

    def send_quarter(twos, kind):
        return [swap(two[size // 4 :].astype(kind), AXES[s][0]) for s, two in enumerate(twos)]

    def add_quarter(twos, received):
        return jnp.stack([two[: size // 4] + other.astype(f32) for two, other in zip(twos, received)])

    saved = []
    for l in range(2):
        w_in, w_out = weights[l]
        layer = layers[l]
        rho = lax.rsqrt(jnp.mean(u * u, axis=2, keepdims=True) + eps)
        a_own = (u * rho * layer["norm"][None]).astype(bf16)
        (a,) = spread_all(a_own)
        if l == 0:
            top_rounded, a = tied((top.astype(bf16), a))
            top_received = spread_first(top_rounded)
        pre = dot_nn(a, w_in)
        if l == 0:
            pre, top_received = tied((pre, top_received))
            top_twos = join_first(top_rounded, top_received)
            top_received = spread_second(top_twos)
        og, y, conv_x, states, squares, row_steps, col_steps = scan_forward(order, pre, layer, tables)
        if l == 1:
            og, do_top = tied((og, do_top))
        sq = squares[:, 0, :]
        saved.append((u, rho, a, pre, og, y, conv_x, states, sq, row_steps, col_steps))
        if l == 0:
            o_part, sq_part = rows_product(og, w_out), list(sq.reshape(4, size // 2))
            o_part, top_received = tied((o_part, top_received))
            do_top = join_second(top_twos, top_received)
            received, sq_received = tied((send_half(o_part), send_half(sq_part)))
            twos, sq_twos = add_half(o_part, received), add_half(sq_part, sq_received)
            o = add_quarter(twos, send_quarter(twos, bf16))
            total = add_quarter(sq_twos, send_quarter(sq_twos, f32))[:, :, None]
            r_first = lax.rsqrt(total / DI + eps)
            o_first = o * r_first
            u = u + o_first

    def summed_rows(rows_sums):
        count = rows_sums.shape[0]
        total = rows_sums.reshape(count, streams, 2, 2, T)
        for flips, pairs in (((1, 0), (2, 3, 0, 1)), ((0, 1), (1, 0, 3, 2)), ((1, 1), (3, 2, 1, 0))):
            other = lax.ppermute(rows_sums, ("section", "tensor"), list(enumerate(pairs)))
            other = other.reshape(count, streams, 2, 2, T)
            turned = []
            for s in range(streams):
                piece = other[:, s]
                for axis in (0, 1):
                    if flips[0 if AXES[s][axis] == "section" else 1]:
                        piece = jnp.flip(piece, axis=2 - axis)
                turned.append(piece)
            total = total + jnp.stack(turned, axis=1)
        return total.reshape(count, -1)

    def rows_of_stats(scale, stat):
        pair = jnp.stack([scale.reshape(-1, T), stat.reshape(-1, T)], axis=1)
        return jnp.pad(pair, ((0, 0), (0, 6), (0, 0)))

    u, rho, a, pre, og, y, conv_x, states, sq, row_steps, col_steps = saved[1]
    d_out, dots = rows_and_dots(do_top, weights[1][1], og)
    square_sums, dots = tied((summed_rows(sq.reshape(1, -1)), dots[:, 0, :].reshape(-1)))
    r_last = lax.rsqrt(square_sums[0] / DI + eps)
    scaled_og = (og.astype(f32) * r_last[:, None]).astype(bf16)
    grad_out_last = dot_tn(do_top, scaled_og).astype(bf16)
    dot_sums, grad_out_last = tied((summed_rows(dots[None]), grad_out_last))
    stats_last = rows_of_stats(r_last, r_last**3 * dot_sums[0] / DI)

    shards = [None, None]

    def pack(acc_x, acc_bc, acc_dt, da_part, a, layer):
        norm = sum(
            jnp.sum(part.astype(f32) * a[i * part.shape[0] : (i + 1) * part.shape[0]].astype(f32), axis=0)
            for i, part in enumerate(da_part)
        ) / layer["norm"][0]
        return jnp.concatenate([acc_x[:7].reshape(-1), acc_bc[:5].reshape(-1), jnp.sum(acc_dt, axis=1), norm])

    def sum_steps():
        devices = lax.axis_size("dp")
        if devices & (devices - 1):
            return [lambda value: jnp.sum(lax.all_gather(value, "dp", axis=0), axis=0), lambda value: value]

        def add_others(value, masks):
            return value + sum(
                lax.ppermute(value, "dp", [(i, i ^ mask) for i in range(devices)]) for mask in masks
            )

        steps, bit = [], 1
        while bit < devices:
            four = bit > 1 and 2 * bit < devices
            steps.append(functools.partial(add_others, masks=(bit, 2 * bit, 3 * bit) if four else (bit,)))
            bit *= 4 if four else 2
        return steps + [lambda value: value] * max(0, 2 - len(steps))

    def input_gradient(l, dv, da):
        u, rho = saved[l][0], saved[l][1]
        scaled = da * layers[l]["norm"][None]
        return dv + rho * scaled - u * rho**3 * jnp.mean(scaled * u, axis=2, keepdims=True)

    shard_out = lax.psum_scatter(grad_out_last, "dp", scatter_dimension=0, tiled=True)
    d_pre, acc_x, acc_bc, acc_dt = scan_backward(
        order, pre, conv_x, y, states, d_out, stats_last, row_steps, col_steps, layers[1], tables
    )
    da_part = rows_product(d_pre, weights[1][0])
    d_pre, da_part = tied((d_pre, da_part))
    grad_in = dot_tn(a, d_pre).astype(bf16)
    small_last = pack(acc_x, acc_bc, acc_dt, da_part, a, layers[1])
    received, grad_after, small_last, shard_out, og = tied(
        (send_half(da_part), grad_in, small_last, shard_out, og)
    )
    o_part = rows_product(og, weights[1][1])
    small_last = small_last + 0.0 * grad_after[0, 0].astype(f32)
    twos = add_half(da_part, received)
    da = add_quarter(twos, send_quarter(twos, bf16))
    shards[1] = (shard_out, lax.psum_scatter(grad_in, "dp", scatter_dimension=0, tiled=True))
    dv = input_gradient(1, top, da)

    do_own = (dv * r_first).astype(bf16)
    kappa = r_first[:, :, 0] ** 2 * jnp.sum(dv * o_first, axis=2) / DI
    do, stat = spread_all(do_own, kappa)
    do, o_part = tied((do, o_part))
    u, rho, a, pre, og, y, conv_x, states, sq, row_steps, col_steps = saved[0]
    w_in, w_out = weights[0]
    stats = rows_of_stats(jnp.ones_like(stat), stat)
    d_out = dot_nn(do, w_out)
    do, d_out = tied((do, d_out))
    grad_out = dot_tn(do, og).astype(bf16)
    grad_out, shards[1] = tied((grad_out, shards[1]))
    d_out, grad_out = tied((d_out, grad_out))
    shard_out = lax.psum_scatter(grad_out, "dp", scatter_dimension=0, tiled=True)
    d_pre, acc_x, acc_bc, acc_dt = scan_backward(
        order, pre, conv_x, y, states, d_out, stats, row_steps, col_steps, layers[0], tables
    )
    d_pre, o_received = tied((d_pre, send_half(o_part)))
    grad_in = dot_tn(a, d_pre).astype(bf16)
    d_pre, grad_after, o_received = tied((d_pre, grad_in, o_received))
    o_twos = add_half(o_part, o_received)
    da_part = rows_product(d_pre, w_in)
    da_part, o_received, shard_out = tied((da_part, send_quarter(o_twos, bf16), shard_out))
    r_own = jnp.stack([r_last[s * size : s * size + T] for s in range(streams)])
    final = saved[1][0] + add_quarter(o_twos, o_received) * r_own[:, :, None]
    small = jnp.stack([pack(acc_x, acc_bc, acc_dt, da_part, a, layers[0]), small_last])
    received, small = tied((send_half(da_part), small))
    twos = add_half(da_part, received)
    steps = sum_steps()
    received, small = tied((send_quarter(twos, bf16), steps[0](small)))
    for step in steps[1:]:
        small = step(small)
    da = add_quarter(twos, received)
    dv = input_gradient(0, dv, da)
    shard_in = lax.psum_scatter(grad_in, "dp", scatter_dimension=0, tiled=True)
    ends_other = swap(jnp.where(x == 0, final, dv).astype(bf16), "section")

    partners = ((2, 3, 0, 1), (1, 0, 3, 2), (3, 2, 1, 0))

    def mine_and_partners(first, last):
        return jnp.where(x == 0, first, last), jnp.where(x == 0, last, first)

    kept, sent = mine_and_partners(small[0], small[1])
    from_section = swap(sent, "section")
    from_tensor = swap(kept, "tensor")
    from_diagonal = lax.ppermute(sent, ("section", "tensor"), list(enumerate(partners[2])))

    out_kept, out_sent = mine_and_partners(shard_out, shards[1][0])
    out_other = swap(out_sent, "section")
    ends_other, from_section, from_tensor, from_diagonal = tied(
        (ends_other, from_section, from_tensor, from_diagonal)
    )
    own_row = jnp.stack(mine_and_partners(kept, from_section))
    other_row = jnp.stack(mine_and_partners(from_tensor, from_diagonal))
    mine = jnp.stack([jnp.where(yy == 0, own_row, other_row), jnp.where(yy == 0, other_row, own_row)], axis=1)
    mine = mine.reshape(4, -1)
    end_x, end_bc = 7 * width, 7 * width + 5 * 2 * N
    end_dt = end_bc + 2 * HP
    over_all = jnp.sum(mine, axis=0)
    halves = lax.dynamic_index_in_dim(mine.reshape(2, 2, -1), yy, 1, keepdims=False)
    by_x = halves[:, :end_x].reshape(2, 7, width).transpose(1, 0, 2).reshape(7, 2 * width)
    by_dt = halves[:, end_bc:end_dt].reshape(2, 2, HP)[:, :, :head_count].transpose(1, 0, 2).reshape(2, 2 * head_count)
    grad_conv_value = by_x[:5]
    grad_gate_gain = by_x[5]
    grad_skip = jnp.sum(by_x[6].reshape(2 * head_count, P_SIZE), axis=1)
    grad_heads = jnp.stack([by_dt[1], by_dt[0] * -jnp.exp(head_params[0, 1]), grad_skip])
    bc_all = over_all[end_x:end_bc].reshape(5, 2 * N)
    grad_conv_shared = lax.dynamic_slice_in_dim(bc_all, yy * N, N, 1)
    grad_norm = over_all[end_dt:]

    mine = jnp.where(x == 0, dv, final)
    other = ends_other.astype(f32)
    relay = jnp.concatenate([jnp.where(x == 0, mine, other), jnp.where(x == 0, other, mine)], axis=1)
    grad_out = jnp.concatenate(mine_and_partners(out_kept, out_other), axis=1).astype(f32)

    shard_in, relay, grad_out = tied((shard_in, relay, grad_out))
    in_kept, in_sent = mine_and_partners(shard_in, shards[1][1])
    bc_at, dt_at, z_at = width, width + 2 * N, width + 2 * N + LANES

    def half_of(value, which):
        return lax.dynamic_slice_in_dim(value, bc_at + which * N, N, 1)

    in_other = swap(in_sent, "section")
    bc_tensor = swap(half_of(in_kept, 1 - yy), "tensor")
    bc_diagonal = lax.ppermute(half_of(in_sent, 1 - yy), ("section", "tensor"), list(enumerate(partners[2])))
    in_other, bc_tensor, bc_diagonal = tied((in_other, bc_tensor, bc_diagonal))

    def both_halves(first, last):
        return jnp.concatenate(mine_and_partners(in_kept[:, first:last], in_other[:, first:last]), axis=1).astype(f32)

    grad_value = both_halves(0, width)
    grad_gate = both_halves(z_at, z_at + width)
    grad_step = both_halves(dt_at, dt_at + head_count)
    grad_shared = sum(
        part.astype(f32) for part in (half_of(in_kept, yy), half_of(in_other, yy), bc_tensor, bc_diagonal)
    )

    return (
        relay[None, None],
        grad_norm[None],
        grad_gate[None],
        grad_value[None],
        grad_shared[None],
        grad_step[None],
        grad_conv_value[None],
        grad_conv_shared[None],
        grad_heads[None],
        grad_gate_gain[None],
        grad_out[None],
    )


def solution(mesh):
    placed = (
        P("dp", None, "tensor", None),
        P("dp", None),
        P("dp", None),
        P("section", None),
        P("section", "dp", "tensor"),
        P("section", "dp", "tensor"),
        P("section", "dp", "tensor"),
        P("section", "dp", "tensor"),
        P("section", None, "tensor"),
        P("section", None, "tensor"),
        P("section", None, "tensor"),
        P("section", "tensor"),
        P("section", "dp", "tensor"),
        P("dp", None, "tensor", None),
    )
    return jax.shard_map(
        local,
        mesh=mesh,
        in_specs=placed,
        out_specs=(
            P("section", "dp", None, "tensor", None),
            P("section", None),
            P("section", "dp", "tensor"),
            P("section", "dp", "tensor"),
            P("section", "dp", "tensor"),
            P("section", "dp", "tensor"),
            P("section", None, "tensor"),
            P("section", None, "tensor"),
            P("section", None, "tensor"),
            P("section", "tensor"),
            P("section", "dp", "tensor"),
        ),
        check_vma=False,
    )
```

```python
import functools

import jax
import jax.numpy as jnp
import numpy as np
from jax import lax
from jax.experimental import pallas as pl
from jax.experimental.pallas import tpu as pltpu
from jax.sharding import PartitionSpec as P

DI = 3072
P_SIZE = 64
N = 128
T = 128
LANES = 128
HP = 16
eps = 1e-05
bf16 = jnp.bfloat16
f32 = jnp.float32


def dot_nn(a, b):
    return lax.dot_general(a, b, (((1,), (0,)), ((), ())), preferred_element_type=f32)


def dot_nt(a, b):
    return lax.dot_general(a, b, (((1,), (1,)), ((), ())), preferred_element_type=f32)


def dot_tn(a, b):
    return lax.dot_general(a, b, (((0,), (0,)), ((), ())), preferred_element_type=f32)


def sigmoid(v):
    return 0.5 + 0.5 * jnp.tanh(0.5 * v)


def shifted(cat):
    return (
        pltpu.roll(cat, 3, 0)[8:],
        pltpu.roll(cat, 2, 0)[8:],
        pltpu.roll(cat, 1, 0)[8:],
        cat[8:],
    )


def conv(parts, taps):
    total = taps[4:5]
    for j in range(4):
        total = total + taps[j : j + 1] * parts[j]
    return total


def shifted_back(ds, after):
    cat = jnp.concatenate([ds, after], axis=0)
    rows = cat.shape[0]
    return [pltpu.roll(cat, rows - (3 - j), 0)[: ds.shape[0]] for j in range(3)] + [ds]


def conv_back(later, taps):
    total = taps[3:4] * later[3]
    for j in range(3):
        total = total + taps[j : j + 1] * later[j]
    return total


def lane_ids(shape):
    return lax.broadcasted_iota(jnp.int32, shape, len(shape) - 1)


def running_sum(v, lane):
    step = 1
    while step < LANES:
        v = v + jnp.where(lane >= step, pltpu.roll(v, step, 1), 0.0)
        step *= 2
    return v


def running_sum_back(v, lane):
    step = 1
    while step < LANES:
        v = v + jnp.where(lane < LANES - step, pltpu.roll(v, LANES - step, 1), 0.0)
        step *= 2
    return v


def parts_of(v):
    high = v.astype(bf16)
    rest = v - high.astype(f32)
    middle = rest.astype(bf16)
    return high, middle, (rest - middle.astype(f32)).astype(bf16)


def prepare_steps(pre_dt, heads, rows_ref, cols_ref):
    chunks = pre_dt.shape[0] // T
    logits = jnp.concatenate(
        [jnp.transpose(pre_dt[c * T : (c + 1) * T])[:HP] + heads[:, 0:1] for c in range(chunks)], axis=0
    )
    small = jnp.exp(-jnp.abs(logits))
    log_part = jnp.where(small < 1e-3, small * (1.0 - small * (0.5 - small / 3.0)), jnp.log(1.0 + small))
    steps = jnp.maximum(logits, 0.0) + log_part
    decays = jnp.concatenate([heads[:, 1:2]] * chunks, axis=0)
    run = running_sum(steps * decays, lane_ids(steps.shape))
    for c in range(chunks):
        at = slice(c * HP, (c + 1) * HP)
        rows_ref[c, 0:HP] = logits[at]
        rows_ref[c, HP : 2 * HP] = steps[at]
        rows_ref[c, 2 * HP : 3 * HP] = run[at]
        split = [part.astype(f32) for part in parts_of(run[at]) + parts_of(steps[at])]
        split.append(jnp.zeros((LANES - 6 * HP, T), f32))
        cols_ref[c] = jnp.transpose(jnp.concatenate(split, axis=0)).astype(bf16)


def eights(v):
    return jnp.sum(v.reshape(v.shape[0] // 8, 8, v.shape[1]), axis=0)


def fwd_kernel(
    order, px, halo, pre_dt, taps_x, taps_bc, heads, skip, gain, spread_run, spread_steps,
    og_ref, y_ref, conv_ref, s_ref, sq_ref, rows_ref, cols_ref, state,
):
    s_id, k = pl.program_id(0), pl.program_id(1)
    width = y_ref.shape[1]
    pairs = width // LANES
    bc_at, z_at = width, width + 2 * N + LANES

    @pl.when((s_id == 0) & (k == 0))
    def _():
        prepare_steps(pre_dt[...], heads[...], rows_ref, cols_ref)

    @pl.when(k == 0)
    def _():
        state[...] = jnp.zeros_like(state)

    block = order[s_id * 4 + k]
    keep = jnp.where(k > 0, 1.0, 0.0)
    lane = lane_ids((T, LANES))
    low = lane < P_SIZE
    row = lax.broadcasted_iota(jnp.int32, (T, T), 0)
    run = rows_ref[block, 2 * HP : 3 * HP]
    cols = cols_ref[block]
    runs_wide = dot_nn(cols, spread_run[...])
    steps_wide = dot_nn(cols, spread_steps[...])
    bc_cat = jnp.concatenate([halo[:, bc_at : bc_at + 2 * N] * keep, px[:, bc_at : bc_at + 2 * N]], axis=0)
    s_bc = conv(shifted(bc_cat), taps_bc[...])
    bc = s_bc * sigmoid(s_bc)
    keys = bc[:, :N]
    keys_t = jnp.transpose(keys).astype(bf16)
    reads = bc[:, N:].astype(bf16)
    scores = jnp.where(row >= lane, dot_nt(reads, keys.astype(bf16)), 0.0)
    squares = jnp.zeros((T, LANES), f32)
    for p in range(pairs):
        at = slice(p * LANES, (p + 1) * LANES)
        x_cat = jnp.concatenate([halo[:, at] * keep, px[:, at]], axis=0)
        s_x = conv(shifted(x_cat), taps_x[:, at])
        conv_ref[:, at] = s_x
        xs = s_x * sigmoid(s_x)
        xd = xs * steps_wide[:, at]
        xr = xd.astype(bf16)
        mixes = []
        wide = []
        for h in (2 * p, 2 * p + 1):
            ci = runs_wide[:, h * LANES : (h + 1) * LANES]
            mixes.append((jnp.exp(jnp.minimum(ci - run[h : h + 1], 0.0)) * scores).astype(bf16))
            wide.append(ci)
        c_pair = jnp.where(low, wide[0], wide[1])
        e_pair = jnp.exp(c_pair)
        zero = jnp.zeros_like(xr)
        y = dot_nn(
            jnp.concatenate(mixes, axis=1),
            jnp.concatenate([jnp.where(low, xr, zero), jnp.where(low, zero, xr)], axis=0),
        )
        entering = state[:, at]
        entering_r = entering.astype(bf16)
        s_ref[0, :, at] = entering_r
        y = y + e_pair * dot_nn(reads, entering_r)
        left = (xd * jnp.exp(c_pair[T - 1 : T] - c_pair)).astype(bf16)
        state[:, at] = e_pair[T - 1 : T] * entering + dot_nn(keys_t, left)
        y_ref[:, at] = y
        z = px[:, z_at + p * LANES : z_at + (p + 1) * LANES]
        g = (y + skip[:, at] * xs) * (z * sigmoid(z))
        squares = squares + g * g
        og_ref[:, at] = (g * gain[:, at]).astype(bf16)
    sq_ref[0] = jnp.broadcast_to(jnp.sum(jnp.transpose(squares), axis=0, keepdims=True), (8, T))


def bwd_kernel(
    order, px, halo, conv_ref, y_ref, s_ref, d_ref, stats, rows_ref, cols_ref,
    taps_x, taps_bc, heads, skip, gain, spread_run, spread_steps, sums,
    pre_ref, acc_x, acc_bc, acc_dt,
    back, after_x, after_bc, d_scores, head_sums_ref, part_x, part_bc,
):
    s_id, k = pl.program_id(0), pl.program_id(1)
    width = y_ref.shape[1]
    pairs = width // LANES
    bc_at, dt_at, z_at = width, width + 2 * N, width + 2 * N + LANES

    @pl.when(k == 0)
    def _():
        back[...] = jnp.zeros_like(back)
        after_x[...] = jnp.zeros_like(after_x)
        after_bc[...] = jnp.zeros_like(after_bc)

    @pl.when((k == 0) & (s_id == 0))
    def _():
        part_x[...] = jnp.zeros_like(part_x)
        part_bc[...] = jnp.zeros_like(part_bc)
        acc_dt[...] = jnp.zeros_like(acc_dt)

    block = order[s_id * 4 + 3 - k]
    place = block - s_id * 4
    dx_ref = pre_ref.at[pl.ds(pl.multiple_of(place * T, T), T)]
    keep = jnp.where(k < 3, 1.0, 0.0)
    lane = lane_ids((T, LANES))
    low = lane < P_SIZE
    row = lax.broadcasted_iota(jnp.int32, (T, T), 0)
    seen_t = lane >= row
    last = row == T - 1
    run = rows_ref[block, 2 * HP : 3 * HP]
    cols = cols_ref[block]
    runs_wide = dot_nn(cols, spread_run[...])
    steps_wide = dot_nn(cols, spread_steps[...])
    bc_cat = jnp.concatenate([halo[:, bc_at : bc_at + 2 * N] * keep, px[:, bc_at : bc_at + 2 * N]], axis=0)
    bc_parts = shifted(bc_cat)
    s_bc = conv(bc_parts, taps_bc[...])
    sig_bc = sigmoid(s_bc)
    bc = s_bc * sig_bc
    keys, reads = bc[:, :N].astype(bf16), bc[:, N:].astype(bf16)
    reads_t = jnp.transpose(bc[:, N:]).astype(bf16)
    scores_t = jnp.where(seen_t, dot_nt(keys, reads), 0.0)
    d_scores[...] = jnp.zeros_like(d_scores)
    d_reads = jnp.zeros((T, N), f32)
    d_keys = jnp.zeros((T, N), f32)
    head_sums = jnp.zeros((T, LANES), f32)
    stat_cols = jnp.transpose(stats[0])
    row_scale = jnp.broadcast_to(stat_cols[:, 0:1], (T, LANES))
    row_stat = jnp.broadcast_to(stat_cols[:, 1:2], (T, LANES))
    for p in range(pairs):
        at = slice(p * LANES, (p + 1) * LANES)
        s_x = conv_ref[:, at]
        sig_x = sigmoid(s_x)
        xs = s_x * sig_x
        steps_pair = steps_wide[:, at]
        xd = xs * steps_pair
        xr = xd.astype(bf16)
        z = px[:, z_at + p * LANES : z_at + (p + 1) * LANES]
        sig_z = sigmoid(z)
        silu_z = z * sig_z
        y = y_ref[:, at]
        y_all = y + skip[:, at] * xs
        g = y_all * silu_z
        dr = d_ref[:, at] * row_scale
        dg = gain[:, at] * dr - g * row_stat
        part_x[40:48, at] += eights(dr * g)
        dx_ref[:, z_at + p * LANES : z_at + (p + 1) * LANES] = (
            dg * y_all * (sig_z + silu_z * (1.0 - sig_z))
        ).astype(bf16)
        dy = dg * silu_z
        dyr = dy.astype(bf16)
        part_x[48:56, at] += eights(dy * xs)
        zero = jnp.zeros_like(xr)
        mixes_t = []
        wide = []
        total = d_scores[...]
        for i, h in enumerate((2 * p, 2 * p + 1)):
            cj = runs_wide[:, h * LANES : (h + 1) * LANES]
            decay = jnp.exp(jnp.minimum(run[h : h + 1] - cj, 0.0))
            mixes_t.append((decay * scores_t).astype(bf16))
            x_one = jnp.where(low, xr, zero) if i == 0 else jnp.where(low, zero, xr)
            total = total + decay * dot_nt(x_one, dyr)
            wide.append(cj)
        d_scores[...] = total
        c_pair = jnp.where(low, wide[0], wide[1])
        e_pair = jnp.exp(c_pair)
        e_left = jnp.exp(c_pair[T - 1 : T] - c_pair)
        dx_in = dot_nn(
            jnp.concatenate(mixes_t, axis=1),
            jnp.concatenate([jnp.where(low, dyr, zero), jnp.where(low, zero, dyr)], axis=0),
        )
        returning = back[:, at]
        returning_r = returning.astype(bf16)
        entering_r = s_ref[0, :, at]
        dx_out = e_left * dot_nn(keys, returning_r)
        dye = (dy * e_pair).astype(bf16)
        d_reads = d_reads + dot_nt(dye, entering_r)
        d_keys = d_keys + dot_nt((xd * e_left).astype(bf16), returning_r)
        e_last = e_pair[T - 1 : T]
        back[:, at] = e_last * returning + dot_nn(reads_t, dye)
        across = e_last * jnp.sum(returning * entering_r.astype(f32), axis=0, keepdims=True)
        xf, dyf = xr.astype(f32), dyr.astype(f32)
        two = xf * dx_in
        three = xd * dx_out
        one = dyf * y - two + jnp.where(last, across, 0.0)
        high = one.astype(bf16)
        rest = (one - high.astype(f32)).astype(bf16)
        head_sums = head_sums + dot_nn(
            jnp.concatenate([high, rest, (two + three).astype(bf16), three.astype(bf16)], axis=1),
            sums[4 * p * LANES : 4 * (p + 1) * LANES],
        )
        dxs = steps_pair * (dx_in + dx_out) + skip[:, at] * dy
        ds = dxs * (sig_x + xs * (1.0 - sig_x))
        later = shifted_back(ds, after_x[:, at])
        pre_x = px[:, at]
        for j in range(4):
            part_x[8 * j : 8 * j + 8, at] += eights(later[j] * pre_x)
        part_x[32:40, at] += eights(ds)
        dx_ref[:, at] = conv_back(later, taps_x[:, at]).astype(bf16)
        after_x[:, at] = ds[:8]
    head_sums_ref[pl.ds(pl.multiple_of(place * T, T), T)] = head_sums
    ds_t = jnp.where(seen_t, d_scores[...], 0.0)
    d_keys = d_keys + dot_nn(ds_t.astype(bf16), reads)
    d_reads = d_reads + dot_nn(jnp.transpose(ds_t).astype(bf16), keys)
    ds_bc = jnp.concatenate([d_keys, d_reads], axis=1) * (sig_bc + bc * (1.0 - sig_bc))
    for j in range(4):
        part_bc[8 * j : 8 * j + 8] += eights(ds_bc * bc_parts[j])
    part_bc[32:40] += eights(ds_bc)
    dx_ref[:, bc_at : bc_at + 2 * N] = conv_back(shifted_back(ds_bc, after_bc[...]), taps_bc[...]).astype(bf16)
    after_bc[...] = ds_bc[:8]

    @pl.when(k == 3)
    def _():
        head_cols = heads[...]
        turned = [jnp.transpose(head_sums_ref[c * T : (c + 1) * T]) for c in range(4)]
        one, both, three = (
            jnp.concatenate([t[i * HP : (i + 1) * HP] for t in turned], axis=0) for i in range(3)
        )
        logits = jnp.concatenate([rows_ref[s_id * 4 + c, 0:HP] for c in range(4)], axis=0)
        steps = jnp.concatenate([rows_ref[s_id * 4 + c, HP : 2 * HP] for c in range(4)], axis=0)
        decay_rate = jnp.concatenate([head_cols[:, 1:2]] * 4, axis=0)
        lane_h = lane_ids(one.shape)
        d_decay = running_sum_back(one, lane_h) + running_sum(three, lane_h) - three
        exact = jnp.exp(jnp.minimum(logits, 0.0)) / (1.0 + jnp.exp(-jnp.abs(logits)))
        ratio = jnp.where(logits < -15.0, 1.0, exact / jnp.maximum(steps, 1e-30))
        d_pre = both * ratio + decay_rate * d_decay * exact
        d_rate = steps * d_decay
        for c in range(4):
            at = slice(c * HP, (c + 1) * HP)
            acc_dt[0:HP] += d_rate[at]
            acc_dt[HP : 2 * HP] += d_pre[at]
            padded = jnp.concatenate([d_pre[at], jnp.zeros((LANES - HP, T), f32)], axis=0)
            pre_ref[c * T : (c + 1) * T, dt_at : dt_at + LANES] = jnp.transpose(padded).astype(bf16)

    @pl.when((k == 3) & (s_id == pl.num_programs(0) - 1))
    def _():
        acc_x[...] = jnp.zeros_like(acc_x)
        acc_bc[...] = jnp.zeros_like(acc_bc)
        for j in range(7):
            acc_x[j : j + 1] = jnp.sum(part_x[8 * j : 8 * j + 8], axis=0, keepdims=True)
        for j in range(5):
            acc_bc[j : j + 1] = jnp.sum(part_bc[8 * j : 8 * j + 8], axis=0, keepdims=True)


def hbm(*arrays):
    return [pltpu.with_memory_space_constraint(array, pltpu.HBM) for array in arrays]


def whole_spec(array):
    return pl.BlockSpec(array.shape, lambda s, k, order: (0,) * array.ndim)


def scan_forward(order, px, layer, fixed_arrays):
    rows, width = px.shape[0], layer["skip"].shape[1]
    steps = rows // T
    here = lambda s, k, order: (order[s * 4 + k], 0)
    before = lambda s, k, order: (order[s * 4 + jnp.maximum(k - 1, 0)] * (T // 8) + (T // 8 - 1), 0)
    small = (layer["taps_x"], layer["taps_bc"], layer["heads"], layer["skip"], layer["gain"]) + fixed_arrays[:2]
    whole = lambda s, k, order: (0, 0, 0)
    return pl.pallas_call(
        fwd_kernel,
        grid_spec=pltpu.PrefetchScalarGridSpec(
            num_scalar_prefetch=1,
            grid=(steps // 4, 4),
            in_specs=[
                pl.BlockSpec((T, px.shape[1]), here),
                pl.BlockSpec((8, width + 2 * N), before),
                pl.BlockSpec((rows, LANES), lambda s, k, order: (0, (width + 2 * N) // LANES)),
            ]
            + [whole_spec(m) for m in small],
            out_specs=[
                pl.BlockSpec((T, width), here),
                pl.BlockSpec((T, width), here),
                pl.BlockSpec((T, width), here),
                pl.BlockSpec((1, N, width), lambda s, k, order: (s * 4 + k, 0, 0)),
                pl.BlockSpec((1, 8, T), lambda s, k, order: (order[s * 4 + k], 0, 0)),
                pl.BlockSpec((steps, 3 * HP, T), whole),
                pl.BlockSpec((steps, T, LANES), whole),
            ],
            scratch_shapes=[pltpu.VMEM((N, width), f32)],
        ),
        out_shape=[
            pltpu.HBM((rows, width), bf16),
            pltpu.HBM((rows, width), f32),
            pltpu.HBM((rows, width), f32),
            pltpu.HBM((steps, N, width), bf16),
            jax.ShapeDtypeStruct((steps, 8, T), f32),
            pltpu.HBM((steps, 3 * HP, T), f32),
            pltpu.HBM((steps, T, LANES), bf16),
        ],
        compiler_params=pltpu.CompilerParams(vmem_limit_bytes=40 * 2**20),
        cost_estimate=pl.CostEstimate(flops=12 * 10**9, bytes_accessed=14 * 2**20, transcendentals=5 * 10**6),
        name="scan_forward",
    )(order, px, px, px, *small)


def scan_backward(order, px, conv_x, y, states, d_out, stats, row_steps, col_steps, layer, fixed_arrays):
    rows, width = y.shape
    steps = rows // T
    here = lambda s, k, order: (order[s * 4 + 3 - k], 0)
    before = lambda s, k, order: (order[s * 4 + jnp.maximum(2 - k, 0)] * (T // 8) + (T // 8 - 1), 0)
    small = (row_steps, col_steps, layer["taps_x"], layer["taps_bc"], layer["heads"], layer["skip"], layer["gain"])
    small = small + fixed_arrays
    fixed = lambda s, k, order: (0, 0)
    return pl.pallas_call(
        bwd_kernel,
        grid_spec=pltpu.PrefetchScalarGridSpec(
            num_scalar_prefetch=1,
            grid=(steps // 4, 4),
            in_specs=[
                pl.BlockSpec((T, px.shape[1]), here),
                pl.BlockSpec((8, width + 2 * N), before),
                pl.BlockSpec((T, width), here),
                pl.BlockSpec((T, width), here),
                pl.BlockSpec((1, N, width), lambda s, k, order: (s * 4 + 3 - k, 0, 0)),
                pl.BlockSpec((T, width), here),
                pl.BlockSpec((1, 8, T), lambda s, k, order: (order[s * 4 + 3 - k], 0, 0)),
            ]
            + [whole_spec(m) for m in small],
            out_specs=[
                pl.BlockSpec((4 * T, px.shape[1]), lambda s, k, order: (s, 0)),
                pl.BlockSpec((8, width), fixed),
                pl.BlockSpec((8, 2 * N), fixed),
                pl.BlockSpec((2 * HP, T), fixed),
            ],
            scratch_shapes=[
                pltpu.VMEM((N, width), f32),
                pltpu.VMEM((8, width), f32),
                pltpu.VMEM((8, 2 * N), f32),
                pltpu.VMEM((T, T), f32),
                pltpu.VMEM((4 * T, LANES), f32),
                pltpu.VMEM((56, width), f32),
                pltpu.VMEM((40, 2 * N), f32),
            ],
        ),
        out_shape=[
            pltpu.HBM((rows, px.shape[1]), bf16),
            jax.ShapeDtypeStruct((8, width), f32),
            jax.ShapeDtypeStruct((8, 2 * N), f32),
            jax.ShapeDtypeStruct((2 * HP, T), f32),
        ],
        compiler_params=pltpu.CompilerParams(vmem_limit_bytes=40 * 2**20),
        cost_estimate=pl.CostEstimate(flops=24 * 10**9, bytes_accessed=24 * 2**20, transcendentals=10**7),
        name="scan_backward",
    )(order, *hbm(px, px, conv_x, y, states, d_out), stats, *hbm(*small[:2]), *small[2:7], *hbm(*small[7:]))


def dots_kernel(do, w_out, og, d_ref, dots_ref):
    d_ref[...] = dot_nn(do[...], w_out[...])
    for c in range(do.shape[0] // T):
        at = slice(c * T, (c + 1) * T)
        total = jnp.zeros((T, LANES), f32)
        for p in range(0, og.shape[1], LANES):
            total = total + d_ref[at, p : p + LANES] * og[at, p : p + LANES].astype(f32)
        dots_ref[c] = jnp.broadcast_to(jnp.sum(jnp.transpose(total), axis=0, keepdims=True), (8, T))


def rows_and_dots(do, w_out, og):
    rows, width = og.shape
    size = rows // 2
    return pl.pallas_call(
        dots_kernel,
        grid=(2,),
        in_specs=[
            pl.BlockSpec((size, do.shape[1]), lambda i: (i, 0)),
            pl.BlockSpec(w_out.shape, lambda i: (0, 0), pipeline_mode=pl.Buffered(1)),
            pl.BlockSpec((size, width), lambda i: (i, 0)),
        ],
        out_specs=[
            pl.BlockSpec((size, width), lambda i: (i, 0)),
            pl.BlockSpec((size // T, 8, T), lambda i: (i, 0, 0)),
        ],
        out_shape=[pltpu.HBM((rows, width), f32), jax.ShapeDtypeStruct((rows // T, 8, T), f32)],
        compiler_params=pltpu.CompilerParams(vmem_limit_bytes=40 * 2**20),
        cost_estimate=pl.CostEstimate(flops=4 * 10**9, bytes_accessed=10 * 2**20, transcendentals=0),
        name="rows_and_dots",
    )(*hbm(do, w_out, og))


def rows_kernel(rows, w, *outs):
    product = dot_nt(rows[...], w[...]).astype(bf16)
    size = product.shape[0] // len(outs)
    for i, out in enumerate(outs):
        out[...] = product[i * size : (i + 1) * size]


def rows_product(rows, w):
    count, size = rows.shape[0], rows.shape[0] // 4
    wide = w.shape[0] // 3
    return pl.pallas_call(
        rows_kernel,
        grid=(3,),
        in_specs=[
            pl.BlockSpec(rows.shape, lambda i: (0, 0), pipeline_mode=pl.Buffered(1)),
            pl.BlockSpec((wide, w.shape[1]), lambda i: (i, 0)),
        ],
        out_specs=[pl.BlockSpec((size, wide), lambda i: (0, i))] * 4,
        out_shape=[jax.ShapeDtypeStruct((size, w.shape[0]), bf16)] * 4,
        compiler_params=pltpu.CompilerParams(vmem_limit_bytes=40 * 2**20),
        cost_estimate=pl.CostEstimate(
            flops=4 * count * w.shape[0] * w.shape[1], bytes_accessed=2 * (rows.size + w.size), transcendentals=0
        ),
        name="rows_product",
    )(*hbm(rows, w))


def fixed_tables(width):
    heads = width // P_SIZE
    column, lane = np.indices((LANES, heads * LANES))
    spread_run = (column < 3 * HP) & (column % HP == lane // LANES)
    column, lane = np.indices((LANES, width))
    spread_steps = (column >= 3 * HP) & (column < 6 * HP) & (column % HP == lane // P_SIZE)
    feature, target = np.indices((4 * width, LANES))
    part, head = (feature // LANES) % 4, 2 * (feature // (4 * LANES)) + (feature % LANES) // P_SIZE
    sums = target == np.array([0, 0, 1, 2])[part] * HP + head
    return tuple(jnp.asarray(m, bf16) for m in (spread_run, spread_steps, sums))


tied = lax.optimization_barrier


def swap(value, axis):
    return lax.ppermute(value, axis, [(0, 1), (1, 0)])


AXES = (("section", "tensor"), ("tensor", "section"))


def spread_first(value):
    return [swap(value[s], axes[0]) for s, axes in enumerate(AXES)]


def join_first(value, received):
    return [jnp.concatenate([value[s], received[s]], axis=0) for s in range(len(AXES))]


def spread_second(twos):
    return [swap(two, axes[1]) for two, axes in zip(twos, AXES)]


def join_second(twos, received):
    return jnp.concatenate([part for pair in zip(twos, received) for part in pair], axis=0)


def spread_all(*values):
    received = tied([spread_first(value) for value in values])
    twos = [join_first(value, r) for value, r in zip(values, received)]
    received = tied([spread_second(pair) for pair in twos])
    return [join_second(pair, r) for pair, r in zip(twos, received)]


def local(
    block_input,
    plan,
    lengths,
    norm_gain,
    gate_proj,
    value_proj,
    shared_proj,
    step_proj,
    conv_value,
    conv_shared,
    head_params,
    gate_gain,
    out_proj,
    cotangent,
):
    x = lax.axis_index("section")
    yy = lax.axis_index("tensor")
    streams = block_input.shape[1]
    model_width = block_input.shape[3]
    width = gate_proj.shape[2] // 2
    head_count = step_proj.shape[2] // 2
    rows_here = gate_proj.shape[1]

    def both(value):
        other = swap(value, "section")
        return jnp.where(x == 0, value, other), jnp.where(x == 0, other, value)

    def quarters(value):
        size = value.shape[-1] // 2
        axis = value.ndim - 1
        kept = lax.dynamic_slice_in_dim(value, x * size, size, axis)
        other = swap(lax.dynamic_slice_in_dim(value, (1 - x) * size, size, axis), "section")
        return jnp.where(x == 0, kept, other), jnp.where(x == 0, other, kept)

    shared_other = swap(shared_proj[0], "tensor")
    shared_full = jnp.where(
        yy == 0,
        jnp.concatenate([shared_proj[0], shared_other], axis=1),
        jnp.concatenate([shared_other, shared_proj[0]], axis=1),
    )

    def quarter_of(value, which):
        return lax.dynamic_slice_in_dim(value, which * (value.shape[1] // 2), value.shape[1] // 2, 1)

    def packed_in(which):
        steps = jnp.pad(quarter_of(step_proj[0], which), ((0, 0), (0, LANES - head_count)))
        return jnp.concatenate([steps, quarter_of(value_proj[0], which), quarter_of(gate_proj[0], which)], axis=1)

    in_kept, in_other = packed_in(x), swap(packed_in(1 - x), "section")
    shared_section = swap(shared_full, "section")
    out_kept, out_other = quarter_of(out_proj[0], x), swap(quarter_of(out_proj[0], 1 - x), "section")
    weights = []
    for l in range(2):
        shared_l = jnp.where(x == l, shared_full, shared_section)
        rest = jnp.where(x == l, in_kept, in_other)
        packed = jnp.concatenate(
            [rest[:, LANES : LANES + width], shared_l, rest[:, :LANES], rest[:, LANES + width :]], axis=1
        )
        weights.append(
            (
                lax.all_gather(packed, "dp", axis=0, tiled=True),
                lax.all_gather(jnp.where(x == l, out_kept, out_other), "dp", axis=0, tiled=True),
            )
        )

    taps_x_two = quarters(jnp.pad(conv_value[0], ((0, 3), (0, 0))))
    shared_taps_other = swap(conv_shared[0], "tensor")
    taps_bc_full = jnp.where(
        yy == 0,
        jnp.concatenate([conv_shared[0], shared_taps_other], axis=1),
        jnp.concatenate([shared_taps_other, conv_shared[0]], axis=1),
    )
    taps_bc_two = both(jnp.pad(taps_bc_full, ((0, 3), (0, 0))))
    heads_two = quarters(head_params[0])
    gain_two = quarters(gate_gain)
    norm_two = both(norm_gain)
    layers = []
    for l in range(2):
        head_rows = heads_two[l]
        columns_of = jnp.stack([head_rows[0], -jnp.exp(head_rows[1])], axis=1)
        layers.append(
            dict(
                taps_x=taps_x_two[l],
                taps_bc=taps_bc_two[l],
                heads=jnp.pad(columns_of, ((0, HP - head_count), (0, LANES - 2))),
                skip=jnp.repeat(head_rows[2], P_SIZE)[None],
                gain=gain_two[l],
                norm=norm_two[l],
                decay=columns_of[:, 1],
            )
        )
    tables = fixed_tables(width)

    chunk = jnp.arange(4, dtype=jnp.int32)
    x_bit, y_bit = (chunk & 1) ^ x, (chunk >> 1) ^ yy
    order = jnp.concatenate([2 * y_bit + x_bit, 4 + 2 * x_bit + y_bit]).astype(jnp.int32)

    def own_rows(value):
        half = value.shape[1] // 2
        return lax.dynamic_slice_in_dim(value, x * half, half, 1)

    first_rows = (2 * yy + x) * T
    positions = first_rows + lax.broadcasted_iota(jnp.int32, (T, 1), 0)
    valid = jnp.sum(jnp.where(plan[0][:, None] == jnp.arange(streams)[None, :], lengths[0][:, None], 0), axis=0)
    keep = (positions[None] < valid[:, None, None]).astype(f32)
    u = own_rows(block_input[0]).astype(f32)
    top = own_rows(cotangent[0]).astype(f32) * keep

    size = 4 * T

    def send_half(parts):
        return [swap(parts[2 * s + 1], AXES[s][1]) for s in range(streams)]

    def add_half(parts, received):
        return [parts[2 * s].astype(f32) + received[s].astype(f32) for s in range(streams)]

    def send_quarter(twos, kind):
        return [swap(two[size // 4 :].astype(kind), AXES[s][0]) for s, two in enumerate(twos)]

    def add_quarter(twos, received):
        return jnp.stack([two[: size // 4] + other.astype(f32) for two, other in zip(twos, received)])

    saved = []
    for l in range(2):
        w_in, w_out = weights[l]
        layer = layers[l]
        rho = lax.rsqrt(jnp.mean(u * u, axis=2, keepdims=True) + eps)
        a_own = (u * rho * layer["norm"][None]).astype(bf16)
        (a,) = spread_all(a_own)
        if l == 0:
            top_rounded, a = tied((top.astype(bf16), a))
            top_received = spread_first(top_rounded)
        pre = dot_nn(a, w_in)
        if l == 0:
            pre, top_received = tied((pre, top_received))
            top_twos = join_first(top_rounded, top_received)
            top_received = spread_second(top_twos)
        og, y, conv_x, states, squares, row_steps, col_steps = scan_forward(order, pre, layer, tables)
        if l == 1:
            og, do_top = tied((og, do_top))
        sq = squares[:, 0, :]
        saved.append((u, rho, a, pre, og, y, conv_x, states, sq, row_steps, col_steps))
        if l == 0:
            o_part, sq_part = rows_product(og, w_out), list(sq.reshape(4, size // 2))
            o_part, top_received = tied((o_part, top_received))
            do_top = join_second(top_twos, top_received)
            received, sq_received = tied((send_half(o_part), send_half(sq_part)))
            twos, sq_twos = add_half(o_part, received), add_half(sq_part, sq_received)
            o = add_quarter(twos, send_quarter(twos, bf16))
            total = add_quarter(sq_twos, send_quarter(sq_twos, f32))[:, :, None]
            r_first = lax.rsqrt(total / DI + eps)
            o_first = o * r_first
            u = u + o_first

    def summed_rows(rows_sums):
        count = rows_sums.shape[0]
        total = rows_sums.reshape(count, streams, 2, 2, T)
        for flips, pairs in (((1, 0), (2, 3, 0, 1)), ((0, 1), (1, 0, 3, 2)), ((1, 1), (3, 2, 1, 0))):
            other = lax.ppermute(rows_sums, ("section", "tensor"), list(enumerate(pairs)))
            other = other.reshape(count, streams, 2, 2, T)
            turned = []
            for s in range(streams):
                piece = other[:, s]
                for axis in (0, 1):
                    if flips[0 if AXES[s][axis] == "section" else 1]:
                        piece = jnp.flip(piece, axis=2 - axis)
                turned.append(piece)
            total = total + jnp.stack(turned, axis=1)
        return total.reshape(count, -1)

    def rows_of_stats(scale, stat):
        pair = jnp.stack([scale.reshape(-1, T), stat.reshape(-1, T)], axis=1)
        return jnp.pad(pair, ((0, 0), (0, 6), (0, 0)))

    u, rho, a, pre, og, y, conv_x, states, sq, row_steps, col_steps = saved[1]
    d_out, dots = rows_and_dots(do_top, weights[1][1], og)
    square_sums, dots = tied((summed_rows(sq.reshape(1, -1)), dots[:, 0, :].reshape(-1)))
    r_last = lax.rsqrt(square_sums[0] / DI + eps)
    scaled_og = (og.astype(f32) * r_last[:, None]).astype(bf16)
    grad_out_last = dot_tn(do_top, scaled_og).astype(bf16)
    dot_sums, grad_out_last = tied((summed_rows(dots[None]), grad_out_last))
    stats_last = rows_of_stats(r_last, r_last**3 * dot_sums[0] / DI)

    shards = [None, None]

    def pack(acc_x, acc_bc, acc_dt, da_part, a, layer):
        norm = sum(
            jnp.sum(part.astype(f32) * a[i * part.shape[0] : (i + 1) * part.shape[0]].astype(f32), axis=0)
            for i, part in enumerate(da_part)
        ) / layer["norm"][0]
        return jnp.concatenate([acc_x[:7].reshape(-1), acc_bc[:5].reshape(-1), jnp.sum(acc_dt, axis=1), norm])

    def sum_steps():
        devices = lax.axis_size("dp")
        if devices & (devices - 1):
            return [lambda value: jnp.sum(lax.all_gather(value, "dp", axis=0), axis=0), lambda value: value]

        def add_others(value, masks):
            return value + sum(
                lax.ppermute(value, "dp", [(i, i ^ mask) for i in range(devices)]) for mask in masks
            )

        steps, bit = [], 1
        while bit < devices:
            four = bit > 1 and 2 * bit < devices
            steps.append(functools.partial(add_others, masks=(bit, 2 * bit, 3 * bit) if four else (bit,)))
            bit *= 4 if four else 2
        return steps + [lambda value: value] * max(0, 2 - len(steps))

    def input_gradient(l, dv, da):
        u, rho = saved[l][0], saved[l][1]
        scaled = da * layers[l]["norm"][None]
        return dv + rho * scaled - u * rho**3 * jnp.mean(scaled * u, axis=2, keepdims=True)

    shard_out = lax.psum_scatter(grad_out_last, "dp", scatter_dimension=0, tiled=True)
    d_pre, acc_x, acc_bc, acc_dt = scan_backward(
        order, pre, conv_x, y, states, d_out, stats_last, row_steps, col_steps, layers[1], tables
    )
    da_part = rows_product(d_pre, weights[1][0])
    d_pre, da_part = tied((d_pre, da_part))
    grad_in = dot_tn(a, d_pre).astype(bf16)
    small_last = pack(acc_x, acc_bc, acc_dt, da_part, a, layers[1])
    received, grad_after, small_last, shard_out, og = tied(
        (send_half(da_part), grad_in, small_last, shard_out, og)
    )
    o_part = rows_product(og, weights[1][1])
    small_last = small_last + 0.0 * grad_after[0, 0].astype(f32)
    twos = add_half(da_part, received)
    da = add_quarter(twos, send_quarter(twos, bf16))
    shards[1] = (shard_out, lax.psum_scatter(grad_in, "dp", scatter_dimension=0, tiled=True))
    dv = input_gradient(1, top, da)

    do_own = (dv * r_first).astype(bf16)
    kappa = r_first[:, :, 0] ** 2 * jnp.sum(dv * o_first, axis=2) / DI
    stat_parts = [kappa] + [
        lax.ppermute(kappa, ("section", "tensor"), list(enumerate(pairs)))
        for pairs in ((2, 3, 0, 1), (1, 0, 3, 2), (3, 2, 1, 0))
    ]
    (do,) = spread_all(do_own)
    do, stat_parts = tied((do, stat_parts))
    places = ((0, 1, 2, 3), (0, 2, 1, 3))
    stat = jnp.concatenate([stat_parts[i][s] for s in range(streams) for i in places[s]])
    do, o_part = tied((do, o_part))
    u, rho, a, pre, og, y, conv_x, states, sq, row_steps, col_steps = saved[0]
    w_in, w_out = weights[0]
    stats = rows_of_stats(jnp.ones_like(stat), stat)
    d_out = dot_nn(do, w_out)
    do, d_out = tied((do, d_out))
    grad_out = dot_tn(do, og).astype(bf16)
    grad_out, shards[1] = tied((grad_out, shards[1]))
    d_out, grad_out = tied((d_out, grad_out))
    shard_out = lax.psum_scatter(grad_out, "dp", scatter_dimension=0, tiled=True)
    d_pre, acc_x, acc_bc, acc_dt = scan_backward(
        order, pre, conv_x, y, states, d_out, stats, row_steps, col_steps, layers[0], tables
    )
    d_pre, o_received = tied((d_pre, send_half(o_part)))
    grad_in = dot_tn(a, d_pre).astype(bf16)
    d_pre, grad_after, o_received = tied((d_pre, grad_in, o_received))
    o_twos = add_half(o_part, o_received)
    da_part = rows_product(d_pre, w_in)
    da_part, o_received, shard_out = tied((da_part, send_quarter(o_twos, bf16), shard_out))
    r_own = jnp.stack([r_last[s * size : s * size + T] for s in range(streams)])
    final = saved[1][0] + add_quarter(o_twos, o_received) * r_own[:, :, None]
    small = jnp.stack([pack(acc_x, acc_bc, acc_dt, da_part, a, layers[0]), small_last])
    received, small = tied((send_half(da_part), small))
    twos = add_half(da_part, received)
    steps = sum_steps()
    received, small = tied((send_quarter(twos, bf16), steps[0](small)))
    for step in steps[1:]:
        small = step(small)
    da = add_quarter(twos, received)
    dv = input_gradient(0, dv, da)
    shard_in = lax.psum_scatter(grad_in, "dp", scatter_dimension=0, tiled=True)
    ends_other = swap(jnp.where(x == 0, final, dv).astype(bf16), "section")

    partners = ((2, 3, 0, 1), (1, 0, 3, 2), (3, 2, 1, 0))

    def mine_and_partners(first, last):
        return jnp.where(x == 0, first, last), jnp.where(x == 0, last, first)

    kept, sent = mine_and_partners(small[0], small[1])
    from_section = swap(sent, "section")
    from_tensor = swap(kept, "tensor")
    from_diagonal = lax.ppermute(sent, ("section", "tensor"), list(enumerate(partners[2])))

    out_kept, out_sent = mine_and_partners(shard_out, shards[1][0])
    out_other = swap(out_sent, "section")
    ends_other, from_section, from_tensor, from_diagonal = tied(
        (ends_other, from_section, from_tensor, from_diagonal)
    )
    own_row = jnp.stack(mine_and_partners(kept, from_section))
    other_row = jnp.stack(mine_and_partners(from_tensor, from_diagonal))
    mine = jnp.stack([jnp.where(yy == 0, own_row, other_row), jnp.where(yy == 0, other_row, own_row)], axis=1)
    mine = mine.reshape(4, -1)
    end_x, end_bc = 7 * width, 7 * width + 5 * 2 * N
    end_dt = end_bc + 2 * HP
    over_all = jnp.sum(mine, axis=0)
    halves = lax.dynamic_index_in_dim(mine.reshape(2, 2, -1), yy, 1, keepdims=False)
    by_x = halves[:, :end_x].reshape(2, 7, width).transpose(1, 0, 2).reshape(7, 2 * width)
    by_dt = halves[:, end_bc:end_dt].reshape(2, 2, HP)[:, :, :head_count].transpose(1, 0, 2).reshape(2, 2 * head_count)
    grad_conv_value = by_x[:5]
    grad_gate_gain = by_x[5]
    grad_skip = jnp.sum(by_x[6].reshape(2 * head_count, P_SIZE), axis=1)
    grad_heads = jnp.stack([by_dt[1], by_dt[0] * -jnp.exp(head_params[0, 1]), grad_skip])
    bc_all = over_all[end_x:end_bc].reshape(5, 2 * N)
    grad_conv_shared = lax.dynamic_slice_in_dim(bc_all, yy * N, N, 1)
    grad_norm = over_all[end_dt:]

    mine = jnp.where(x == 0, dv, final)
    other = ends_other.astype(f32)
    relay = jnp.concatenate([jnp.where(x == 0, mine, other), jnp.where(x == 0, other, mine)], axis=1)
    grad_out = jnp.concatenate(mine_and_partners(out_kept, out_other), axis=1).astype(f32)

    shard_in, relay, grad_out = tied((shard_in, relay, grad_out))
    in_kept, in_sent = mine_and_partners(shard_in, shards[1][1])
    bc_at, dt_at, z_at = width, width + 2 * N, width + 2 * N + LANES

    def half_of(value, which):
        return lax.dynamic_slice_in_dim(value, bc_at + which * N, N, 1)

    in_other = swap(in_sent, "section")
    bc_tensor = swap(half_of(in_kept, 1 - yy), "tensor")
    bc_diagonal = lax.ppermute(half_of(in_sent, 1 - yy), ("section", "tensor"), list(enumerate(partners[2])))
    in_other, bc_tensor, bc_diagonal = tied((in_other, bc_tensor, bc_diagonal))

    def both_halves(first, last):
        return jnp.concatenate(mine_and_partners(in_kept[:, first:last], in_other[:, first:last]), axis=1).astype(f32)

    grad_value = both_halves(0, width)
    grad_gate = both_halves(z_at, z_at + width)
    grad_step = both_halves(dt_at, dt_at + head_count)
    grad_shared = sum(
        part.astype(f32) for part in (half_of(in_kept, yy), half_of(in_other, yy), bc_tensor, bc_diagonal)
    )

    return (
        relay[None, None],
        grad_norm[None],
        grad_gate[None],
        grad_value[None],
        grad_shared[None],
        grad_step[None],
        grad_conv_value[None],
        grad_conv_shared[None],
        grad_heads[None],
        grad_gate_gain[None],
        grad_out[None],
    )


def solution(mesh):
    placed = (
        P("dp", None, "tensor", None),
        P("dp", None),
        P("dp", None),
        P("section", None),
        P("section", "dp", "tensor"),
        P("section", "dp", "tensor"),
        P("section", "dp", "tensor"),
        P("section", "dp", "tensor"),
        P("section", None, "tensor"),
        P("section", None, "tensor"),
        P("section", None, "tensor"),
        P("section", "tensor"),
        P("section", "dp", "tensor"),
        P("dp", None, "tensor", None),
    )
    return jax.shard_map(
        local,
        mesh=mesh,
        in_specs=placed,
        out_specs=(
            P("section", "dp", None, "tensor", None),
            P("section", None),
            P("section", "dp", "tensor"),
            P("section", "dp", "tensor"),
            P("section", "dp", "tensor"),
            P("section", "dp", "tensor"),
            P("section", None, "tensor"),
            P("section", None, "tensor"),
            P("section", None, "tensor"),
            P("section", "tensor"),
            P("section", "dp", "tensor"),
        ),
        check_vma=False,
    )
```
